128 devices in a mesh: seq: 32 (over z, x, core), tp: 4 (over y).
Axes of the slice: x: 4, y: 4, z: 4, core: 2. Of those that a mesh axis runs over, the one named last changes fastest.
Arguments:
- tokens: bfloat16 [131072, 1024], P('seq'), may hold values from -16 to 16
- w_qkv: bfloat16 [3, 1024, 1024], P(None, None, 'tp'), as said below
- w_out: bfloat16 [1024, 1024], P('tp'), may hold values from -0.1875 to 0.1875
Outputs:
- mixed: bfloat16 [131072, 1024], P('seq', 'tp')
The draws below stay inside these ranges and needn't reach their ends.
Inputs may be any that keep to these rules, and one draw needn't show every extreme that they name: `w_qkv`: entries lie within six times 1024 ** -0.5 of zero.
All inputs are finite; a program needn't handle non-finite values.
Results may differ from the reference program's by a relative error of at most 0.03.
Values may be sent and summed in bfloat16 or wider, within the bound.
A program may use at most 128 MiB of HBM per device.

```python
import jax
import jax.numpy as jnp
from jax import lax

D = 1024
HEADS = 16
HEAD_DIM = 64
LANDMARKS = 256
NEWTON = 6
TOK_DEV = 4096
TOKENS = 131072
N_SEQ = 32


def draw_tokens(key, part):
    first = jax.random.fold_in(key, 0)
    fifth = jax.random.fold_in(key, 4)
    base = jax.random.normal(first, (TOKENS, D), jnp.float32)
    offsets = jax.random.normal(fifth, (LANDMARKS, D), jnp.float32)
    seg_offsets = jnp.repeat(offsets, TOKENS // LANDMARKS, axis=0, total_repeat_length=TOKENS)
    base = base + seg_offsets
    return jnp.clip(base, -16.0, 16.0).astype(jnp.bfloat16)


def draw_w_qkv(key, part):
    limit = 6.0 * D ** (-0.5)
    weights = jax.random.normal(key, (3, D, D), jnp.float32) * D ** (-0.5)
    return jnp.clip(weights, -limit, limit).astype(jnp.bfloat16)


def block_levels(rng, extent, cuts, low, top_value):
    level = 1.0
    for dim, blocks in cuts:
        heights = jax.random.uniform(jax.random.fold_in(jax.random.fold_in(rng, 6), dim), (blocks,), jnp.float32, low / len(cuts), top_value / len(cuts))
        level = level * jnp.repeat(jnp.exp(heights), extent[dim] // blocks).reshape((-1,) + (1,) * (len(extent) - 1 - dim))
    return level


def normal_values(key, dims, width, most, cuts=(), kind=jnp.bfloat16):
    factor_of = block_levels(key, dims, cuts, -0.22, 0.18) if cuts else 1.0
    result = jax.random.normal(key, dims, jnp.float32) * width * factor_of
    return jnp.minimum(jnp.maximum(result, -most), most).astype(kind)


def setup_inputs(seed: int = 0) -> dict:
    keys = jax.random.split(jax.random.key(seed), 4)
    tokens = draw_tokens(jax.random.fold_in(keys[3], 71), 0)
    w_qkv = draw_w_qkv(jax.random.fold_in(keys[3], 71), 0)
    w_out = normal_values(keys[2], (D, D), D ** -0.5, 0.1875, ((0, 4),))
    return {"tokens": tokens, "w_qkv": w_qkv, "w_out": w_out}


def softmax_rows(logit_scores):
    top = jnp.max(logit_scores, axis=-1, keepdims=True)
    exponent_terms = jnp.exp(logit_scores - top)
    return exponent_terms / jnp.sum(exponent_terms, axis=-1, keepdims=True)


def newton_inverse(kernel_a):
    eye = jnp.eye(LANDMARKS, dtype=jnp.float32)
    hi = lax.Precision.HIGHEST
    colmax = jnp.max(jnp.sum(kernel_a, axis=0))
    rowmax = jnp.max(jnp.sum(kernel_a, axis=1))
    approx = kernel_a.T / (colmax * rowmax)
    for turn in range(NEWTON):
        prod_az = jnp.dot(kernel_a, approx, precision=hi)
        inner = jnp.dot(prod_az, 7.0 * eye - prod_az, precision=hi)
        outer = jnp.dot(prod_az, 15.0 * eye - inner, precision=hi)
        approx = 0.25 * jnp.dot(approx, 13.0 * eye - outer, precision=hi)
    return approx


def one_head(items):
    q_head, k_head, v_head, query_landmark_rows, key_landmark_rows = items
    score_scale = HEAD_DIM ** -0.5
    kernel_a = softmax_rows(jnp.dot(query_landmark_rows, key_landmark_rows.T, preferred_element_type=jnp.float32) * score_scale)
    pseudoinverse_kernel = newton_inverse(kernel_a)
    query_kernel_matrix = softmax_rows(jnp.dot(q_head, key_landmark_rows.T, preferred_element_type=jnp.float32) * score_scale).astype(jnp.bfloat16)
    logit_scores = (jnp.dot(query_landmark_rows, k_head.T, preferred_element_type=jnp.float32) * score_scale).reshape(LANDMARKS, N_SEQ, TOK_DEV)
    block_max = jnp.max(logit_scores, axis=2)
    exponent_terms = jnp.exp(logit_scores - block_max[:, :, None])
    block_total = jnp.sum(exponent_terms, axis=2)
    weights = exponent_terms.astype(jnp.bfloat16)
    block_acc = jnp.einsum("mnt,ntd->nmd", weights.astype(jnp.float32), v_head.reshape(N_SEQ, TOK_DEV, HEAD_DIM).astype(jnp.float32))
    row_max = jnp.max(block_max, axis=1)
    factor = jnp.exp(block_max - row_max[:, None])
    total = jnp.sum(block_total * factor, axis=1)
    landmark_value_rows = jnp.sum(block_acc * factor.T[:, :, None], axis=0) / total[:, None]
    center_kernel = jnp.dot(pseudoinverse_kernel, landmark_value_rows, precision=lax.Precision.HIGHEST).astype(jnp.bfloat16)
    return jnp.dot(query_kernel_matrix, center_kernel, preferred_element_type=jnp.float32).astype(jnp.bfloat16)


def reference(tokens, w_qkv, w_out):
    proj = lax.map(lambda weight: jnp.dot(tokens, weight, preferred_element_type=jnp.float32).astype(jnp.bfloat16), w_qkv)
    segment = TOKENS // LANDMARKS

    def marks(array):
        return jnp.mean(array.astype(jnp.float32).reshape(LANDMARKS, segment, D), axis=1).astype(jnp.bfloat16)

    q_marks = marks(proj[0])
    k_marks = marks(proj[1])

    def by_head(array, rows):
        return jnp.transpose(array.reshape(rows, HEADS, HEAD_DIM), (1, 0, 2))

    heads_out = lax.map(one_head, (by_head(proj[0], TOKENS), by_head(proj[1], TOKENS), by_head(proj[2], TOKENS), by_head(q_marks, LANDMARKS), by_head(k_marks, LANDMARKS)))
    attended = jnp.transpose(heads_out, (1, 0, 2)).reshape(TOKENS, D)
    return jnp.dot(attended, w_out, preferred_element_type=jnp.float32).astype(jnp.bfloat16)
```

```python
import functools
import math

import jax
import jax.numpy as jnp
from jax import lax
from jax.experimental import pallas as pl
from jax.experimental.pallas import tpu as pltpu
from jax.sharding import PartitionSpec as P

HEAD_DIM = 64
MARKS = 256
NEWTON = 6
D = 1024
W = 256
T = 4096
SEG = 512
C = 1024
LOG_SCALE = HEAD_DIM**-0.5 * math.log2(math.e)
bf16, f32 = jnp.bfloat16, jnp.float32
NT = (((1,), (1,)), ((), ()))
MESH = pl.DeviceIdType.MESH


def dot(a, b):
    return jnp.dot(a, b, preferred_element_type=f32)


def dot_nt(a, b):
    return lax.dot_general(a, b, NT, preferred_element_type=f32)


def halves(a):
    hi = a.astype(bf16)
    return hi, (a - hi.astype(f32)).astype(bf16)


def dot3(a, b):
    ah, al = halves(a)
    bh, bl = halves(b)
    return dot(jnp.concatenate([ah, al, ah], 1), jnp.concatenate([bh, bh, bl], 0))


def low_lanes(rows):
    return lax.broadcasted_iota(jnp.int32, (rows, 128), 1) < 64


def one_head(block, head):
    low = low_lanes(block.shape[0])
    return jnp.where(low if head % 2 == 0 else ~low, block, 0.0)


def pair_columns(array, pair):
    return array[:, pair * 128 : (pair + 1) * 128]


def softmax_terms(logits):
    return jnp.exp2(logits - jnp.max(logits, axis=1, keepdims=True))


def kernel(
    n_seq, n_tp,
    x_hbm, w_hbm, wo_hbm, out_hbm,
    x, wk, wv, wq, wo, q, k, v, means, mk_s, mk_r, qm, km, kmt,
    acc, mx, lv_s, lv_r, a_ref, z_ref, mid_s, mid_r, midt, midb, e_own, att, outv,
    load_sem, x_sem, out_sem,
    mk_ss, mk_rs, lv_ss, lv_rs, mid_ss, mid_rs,
    wq_ss, wq_rs, wo_ss, wo_rs, km_ss, km_rs, mt_ss, mt_rs,
):
    seq, tp = lax.axis_index("seq"), lax.axis_index("tp")
    n_chunks = T // C

    def rows_of(i):
        return pl.ds(pl.multiple_of(i * C, C), C)

    loads = [
        pltpu.make_async_copy(w_hbm.at[1], wk, load_sem.at[0]),
        pltpu.make_async_copy(w_hbm.at[0], wq.at[tp], load_sem.at[1]),
        pltpu.make_async_copy(w_hbm.at[2], wv, load_sem.at[2]),
        pltpu.make_async_copy(
            wo_hbm.at[:, pl.ds(pl.multiple_of(tp * W, W), W)], wo.at[tp], load_sem.at[3]
        ),
    ]

    def x_load(i):
        return pltpu.make_async_copy(x_hbm.at[rows_of(i)], x.at[rows_of(i)], x_sem.at[i])

    loads[0].start()
    loads[1].start()
    for i in range(n_chunks):
        x_load(i).start()
    loads[2].start()
    loads[3].start()

    barrier = pltpu.get_barrier_semaphore()

    @pl.loop(1, n_seq)
    def _(j):
        pl.semaphore_signal(
            barrier, inc=1, device_id={"seq": lax.rem(seq + j, n_seq)}, device_id_type=MESH
        )

    for j in range(1, n_tp):
        pl.semaphore_signal(
            barrier, inc=1, device_id={"tp": lax.rem(tp + j, n_tp)}, device_id_type=MESH
        )
    pl.semaphore_wait(barrier, n_seq - 1 + n_tp - 1)

    def to_tp(j):
        return lax.rem(tp + j, n_tp)

    def from_tp(j):
        return lax.rem(tp + n_tp - j, n_tp)

    def remote_tp(src, dst_of, ss, rs, j):
        return pltpu.make_async_remote_copy(
            src_ref=src, dst_ref=dst_of, send_sem=ss.at[j], recv_sem=rs.at[j],
            device_id={"tp": to_tp(j)}, device_id_type=MESH,
        )

    def wq_copy(j, slot):
        return remote_tp(w_hbm.at[0], wq.at[slot], wq_ss, wq_rs, j)

    def wo_copy(j, slot):
        columns = pl.ds(pl.multiple_of(to_tp(j) * W, W), W)
        return remote_tp(wo_hbm.at[:, columns], wo.at[slot], wo_ss, wo_rs, j)

    def km_copy(j, slot):
        return remote_tp(kmt.at[tp], kmt.at[slot], km_ss, km_rs, j)

    def mt_copy(j, slot):
        return remote_tp(midt.at[tp], midt.at[slot], mt_ss, mt_rs, j)

    for j in range(1, n_tp):
        wq_copy(j, tp).start()
    for j in range(1, n_tp):
        wo_copy(j, tp).start()

    loads[0].wait()
    loads[1].wait()

    @pl.loop(0, n_chunks)
    def _(i):
        x_load(i).wait()
        rows = rows_of(i)
        xc = x[rows, :]
        kp = dot(xc, wk[...])
        qp = dot(xc, wq[tp]) * LOG_SCALE
        k[rows, :] = kp.astype(bf16)
        q[tp, rows, :] = qp.astype(bf16)
        for s in range(C // SEG):
            at = i * (C // SEG) + s
            part = slice(s * SEG, (s + 1) * SEG)
            means[pl.ds(at, 1), :] = jnp.sum(qp[part], axis=0, keepdims=True) * (1.0 / SEG)
            means[pl.ds(8 + at, 1), :] = jnp.sum(kp[part], axis=0, keepdims=True) * (1.0 / SEG)

    def exchange(copy_of, slots):
        @pl.loop(1, n_seq)
        def _(j):
            copy_of(j, seq).start()

    def finish(copy_of):
        @pl.loop(1, n_seq)
        def _(j):
            copy_of(j, lax.rem(seq + n_seq - j, n_seq)).wait_recv()

    def finish_sends(copy_of):
        @pl.loop(1, n_seq)
        def _(j):
            copy_of(j, seq).wait_send()

    def remote_seq(src, dst, ss, rs, j):
        return pltpu.make_async_remote_copy(
            src_ref=src, dst_ref=dst, send_sem=ss.at[j], recv_sem=rs.at[j],
            device_id={"seq": lax.rem(seq + j, n_seq)}, device_id_type=MESH,
        )

    def mk_copy(j, slot):
        return remote_seq(mk_s, mk_r.at[slot], mk_ss, mk_rs, j)

    def lv_copy(j, slot):
        return remote_seq(lv_s.at[lax.rem(seq + j, n_seq)], lv_r.at[slot], lv_ss, lv_rs, j)

    def mid_copy(j, slot):
        return remote_seq(mid_s, mid_r.at[slot], mid_ss, mid_rs, j)

    mk_s[...] = means[...].astype(bf16)
    exchange(mk_copy, mk_r)
    mk_r[seq] = means[...].astype(bf16)

    loads[2].wait()
    ones = jnp.ones((C, 128), bf16)

    @pl.loop(0, n_chunks)
    def _(i):
        rows = rows_of(i)
        vp = dot(x[rows, :], wv[...]).astype(bf16)
        for p in range(2):
            v[p, rows, 0:128] = pair_columns(vp, p)
            v[p, rows, 128:256] = ones

    finish(mk_copy)
    marks = mk_r[...].astype(f32)
    q_marks = marks[:, 0:8, :].reshape(MARKS, W)
    k_marks = marks[:, 8:16, :].reshape(MARKS, W)
    kmt[tp] = k_marks.astype(bf16)
    for j in range(1, n_tp):
        km_copy(j, tp).start()
    for h in range(4):
        qm[h] = one_head(pair_columns(q_marks, h // 2), h).astype(bf16)
        km[tp * 4 + h] = one_head(pair_columns(k_marks, h // 2), h).astype(bf16)

    acc[...] = jnp.zeros_like(acc)
    mx[...] = jnp.full_like(mx, -jnp.inf)

    @pl.loop(0, n_chunks)
    def _(i):
        rows = rows_of(i)
        for h in range(4):
            p = h // 2
            s = dot_nt(qm[h], k[rows, p * 128 : (p + 1) * 128])
            before = mx[h]
            now = jnp.maximum(before, jnp.max(s, axis=1, keepdims=True))
            e = jnp.exp2(s - now[:, :1]).astype(bf16)
            mx[h] = now
            fade = jnp.exp2(before - now)
            acc[h] = acc[h] * jnp.concatenate([fade, fade], 1) + dot(e, v[p, rows, :])

    sub = lax.broadcasted_iota(jnp.int32, (8, W), 0)
    for p in range(2):
        even, odd = acc[2 * p], acc[2 * p + 1]
        mean_values = jnp.where(
            low_lanes(MARKS), even[:, :128] / even[:, 128:], odd[:, :128] / odd[:, 128:]
        ).T
        for i, r in enumerate((even, odd)):
            h = 2 * p + i
            level = (mx[h] + jnp.log2(r[:, 128:])).T[0:8, :]
            first = level.astype(bf16).astype(f32)
            second = (level - first).astype(bf16).astype(f32)
            third = level - first - second
            lines = jnp.where(
                sub == 0, first, jnp.where(sub == 1, second, jnp.where(sub == 2, third, 0.0))
            )
            for b in range(8):
                part = mean_values[i * 64 + b * 8 : i * 64 + b * 8 + 8, :]
                lv_s[h * 8 + b] = jnp.concatenate([part, lines], 0).astype(bf16)
    exchange(lv_copy, lv_r)
    lv_r[seq] = lv_s[seq]

    head = lax.div(seq, 8)
    terms = softmax_terms(dot_nt(qm[head], km[tp * 4 + head]))
    kernel_a = terms / jnp.sum(terms, axis=1, keepdims=True)
    col = jnp.max(jnp.sum(kernel_a, axis=0, keepdims=True), axis=1, keepdims=True)
    row = jnp.max(jnp.sum(kernel_a, axis=1, keepdims=True), axis=0, keepdims=True)
    a_ref[...] = kernel_a
    z_ref[...] = kernel_a.T / (col * row)
    for j in range(1, n_tp):
        wq_copy(j, from_tp(j)).wait_recv()

    units = 3 * (T // 512) // NEWTON

    @pl.loop(0, NEWTON)
    def _(turn):
        def other_queries(i):
            unit = turn * units + i
            t = to_tp(1 + lax.div(unit, 8))
            rows = pl.ds(pl.multiple_of(lax.rem(unit, 8) * 512, 512), 512)
            q[t, rows, :] = (dot(x[rows, :], wq[t]) * LOG_SCALE).astype(bf16)

        eye = jnp.where(
            lax.broadcasted_iota(jnp.int32, (MARKS, MARKS), 0)
            == lax.broadcasted_iota(jnp.int32, (MARKS, MARKS), 1),
            1.0,
            0.0,
        )
        z = z_ref[...]
        az = dot3(a_ref[...], z)
        other_queries(0)
        inner = dot3(az, 7.0 * eye - az)
        other_queries(1)
        outer = dot3(az, 15.0 * eye - inner)
        other_queries(2)
        z_ref[...] = 0.25 * dot3(z, 13.0 * eye - outer)
        other_queries(3)

    finish(lv_copy)
    lv = lv_r[...].astype(f32)
    level = lv[:, 8:9, :] + lv[:, 9:10, :] + lv[:, 10:11, :]
    share = jnp.exp2(level - jnp.max(level, axis=0, keepdims=True))
    columns = jnp.sum(lv[:, 0:8, :] * share, axis=0) / jnp.sum(share, axis=0)
    ch, cl = halves(columns)
    zh, zl = halves(z_ref[...])
    middle = dot_nt(jnp.concatenate([ch, cl, ch], 1), jnp.concatenate([zh, zh, zl], 1))
    mid_s[...] = middle
    exchange(mid_copy, mid_r)
    mid_r[seq] = middle

    @pl.loop(0, n_chunks)
    def _(i):
        rows = rows_of(i)
        for h in range(4):
            p = h // 2
            logits = dot_nt(q[tp, rows, p * 128 : (p + 1) * 128], km[tp * 4 + h])
            e_own[rows, h * MARKS : (h + 1) * MARKS] = softmax_terms(logits).astype(bf16)

    def place_middle(t):
        m = midt[t].astype(f32)
        low = low_lanes(MARKS)
        for p in range(2):
            both = pair_columns(m, p)
            for i in range(2):
                mask = low if i == 0 else ~low
                midb[t * 2 + p, i * MARKS : (i + 1) * MARKS, :] = jnp.concatenate(
                    [jnp.where(mask, both, 0.0), jnp.where(mask, 1.0, 0.0)], 1
                ).astype(bf16)

    finish(mid_copy)
    midt[tp] = mid_r[...].reshape(W, MARKS).T.astype(bf16)
    for j in range(1, n_tp):
        mt_copy(j, tp).start()
    place_middle(tp)

    def normalised(r):
        return (r[:, :128] * (1.0 / r[:, 128:])).astype(bf16)

    @pl.loop(0, n_chunks)
    def _(i):
        rows = rows_of(i)
        for p in range(2):
            r = dot(e_own[rows, p * 512 : (p + 1) * 512], midb[tp * 2 + p])
            att[rows, p * 128 : (p + 1) * 128] = normalised(r)

    loads[3].wait()
    for j in range(1, n_tp):
        t = from_tp(j)
        km_copy(j, t).wait_recv()
        others = kmt[t].astype(f32)
        for h in range(4):
            km[t * 4 + h] = one_head(pair_columns(others, h // 2), h).astype(bf16)
        wo_copy(j, t).wait_recv()
    for j in range(1, n_tp):
        t = from_tp(j)
        mt_copy(j, t).wait_recv()
        place_middle(t)

    def out_copy(i):
        return pltpu.make_async_copy(outv.at[rows_of(i)], out_hbm.at[rows_of(i)], out_sem.at[i])

    @pl.loop(0, n_chunks)
    def _(i):
        rows = rows_of(i)
        total = dot(att[rows, :], wo[tp])
        for j in range(1, n_tp):
            t = to_tp(j)
            parts = []
            for p in range(2):
                qc = q[t, rows, p * 128 : (p + 1) * 128]
                e = [
                    softmax_terms(dot_nt(qc, km[t * 4 + 2 * p + b])).astype(bf16) for b in range(2)
                ]
                parts.append(normalised(dot(jnp.concatenate(e, 1), midb[t * 2 + p])))
            total = total + dot(jnp.concatenate(parts, 1), wo[t])
        outv[rows, :] = total.astype(bf16)
        out_copy(i).start()

    for copy_of in (mk_copy, lv_copy, mid_copy):
        finish_sends(copy_of)
    for copy_of in (wq_copy, wo_copy, km_copy, mt_copy):
        for j in range(1, n_tp):
            copy_of(j, tp).wait_send()
    for i in range(n_chunks):
        out_copy(i).wait()


def on_device(n_seq, n_tp, tokens, w_qkv, w_out):
    vmem = pltpu.VMEM
    sems = pltpu.SemaphoreType.DMA
    scratch = [
        vmem((T, D), bf16),
        vmem((D, W), bf16),
        vmem((D, W), bf16),
        vmem((n_tp, D, W), bf16),
        vmem((n_tp, W, W), bf16),
        vmem((n_tp, T, W), bf16),
        vmem((T, W), bf16),
        vmem((2, T, 256), bf16),
        vmem((16, W), f32),
        vmem((16, W), bf16),
        vmem((n_seq, 16, W), bf16),
        vmem((4, MARKS, 128), bf16),
        vmem((4 * n_tp, MARKS, 128), bf16),
        vmem((n_tp, MARKS, W), bf16),
        vmem((4, MARKS, 256), f32),
        vmem((4, MARKS, 128), f32),
        vmem((n_seq, 16, MARKS), bf16),
        vmem((n_seq, 16, MARKS), bf16),
        vmem((MARKS, MARKS), f32),
        vmem((MARKS, MARKS), f32),
        vmem((8, MARKS), f32),
        vmem((n_seq, 8, MARKS), f32),
        vmem((n_tp, MARKS, W), bf16),
        vmem((2 * n_tp, 2 * MARKS, 256), bf16),
        vmem((T, 4 * MARKS), bf16),
        vmem((T, W), bf16),
        vmem((T, W), bf16),
        sems((4,)), sems((T // C,)), sems((T // C,)),
        *[sems((n_seq,))] * 6,
        *[sems((n_tp,))] * 8,
    ]
    hbm = pl.BlockSpec(memory_space=pl.ANY)
    return pl.pallas_call(
        functools.partial(kernel, n_seq, n_tp),
        out_shape=jax.ShapeDtypeStruct((T, W), bf16),
        in_specs=[hbm] * 3,
        out_specs=hbm,
        scratch_shapes=scratch,
        compiler_params=pltpu.CompilerParams(
            collective_id=0, has_side_effects=True, vmem_limit_bytes=60 * 2**20
        ),
    )(tokens, w_qkv, w_out)


def solution(mesh):
    return jax.shard_map(
        functools.partial(on_device, mesh.shape["seq"], mesh.shape["tp"]),
        mesh=mesh,
        in_specs=(P("seq", None), P(None, None, "tp"), P("tp", None)),
        out_specs=P("seq", "tp"),
        check_vma=False,
    )
```

```python
import functools
import math

import jax
import jax.numpy as jnp
from jax import lax
from jax.experimental import pallas as pl
from jax.experimental.pallas import tpu as pltpu
from jax.sharding import PartitionSpec as P

HEAD_DIM = 64
MARKS = 256
NEWTON = 6
D = 1024
W = 256
T = 4096
SEG = 512
C = 1024
LOG_SCALE = HEAD_DIM**-0.5 * math.log2(math.e)
bf16, f32 = jnp.bfloat16, jnp.float32
NT = (((1,), (1,)), ((), ()))
MESH = pl.DeviceIdType.MESH
ORDER = (3, 1, 2)


def dot(a, b):
    return jnp.dot(a, b, preferred_element_type=f32)


def dot_nt(a, b):
    return lax.dot_general(a, b, NT, preferred_element_type=f32)


def halves(a):
    hi = a.astype(bf16)
    return hi, (a - hi.astype(f32)).astype(bf16)


def dot3(a, b):
    ah, al = halves(a)
    bh, bl = halves(b)
    return dot(jnp.concatenate([ah, al, ah], 1), jnp.concatenate([bh, bh, bl], 0))


def low_lanes(rows):
    return lax.broadcasted_iota(jnp.int32, (rows, 128), 1) < 64


def one_head(block, head):
    low = low_lanes(block.shape[0])
    return jnp.where(low if head % 2 == 0 else ~low, block, 0.0)


def pair_columns(array, pair):
    return array[:, pair * 128 : (pair + 1) * 128]


def softmax_terms(logits):
    return jnp.exp2(logits - jnp.max(logits, axis=1, keepdims=True))


def kernel(
    n_seq, n_tp,
    x_hbm, w_hbm, wo_hbm, out_hbm,
    x, wk, wv, wq, wo, q, k, v, means, mk_s, mk_r, qm, km, kmt,
    acc, mx, lv_s, lv_r, a_ref, z_ref, mid_s, mid_r, midt, midb, e_a, e_b, outv,
    load_sem, x_sem, out_sem,
    mk_ss, mk_rs, lv_ss, lv_rs, mid_ss, mid_rs,
    wq_sems, wo_sems, km_sems, mt_sems,
):
    seq, tp = lax.axis_index("seq"), lax.axis_index("tp")
    core = lax.rem(seq, 2)
    n_chunks = T // C

    def rows_of(i):
        return pl.ds(pl.multiple_of(i * C, C), C)

    def to_tp(j):
        return lax.rem(tp + j, n_tp)

    def from_tp(j):
        return lax.rem(tp + n_tp - j, n_tp)

    barrier = pltpu.get_barrier_semaphore()

    loads = [
        pltpu.make_async_copy(w_hbm.at[1], wk, load_sem.at[0]),
        pltpu.make_async_copy(w_hbm.at[0], wq.at[tp], load_sem.at[1]),
        pltpu.make_async_copy(w_hbm.at[2], wv, load_sem.at[2]),
        pltpu.make_async_copy(
            wo_hbm.at[:, pl.ds(pl.multiple_of(tp * W, W), W)], wo.at[tp], load_sem.at[3]
        ),
    ]

    def x_load(i):
        return pltpu.make_async_copy(x_hbm.at[rows_of(i)], x.at[rows_of(i)], x_sem.at[i])

    loads[0].start()
    loads[1].start()
    for i in range(n_chunks):
        x_load(i).start()
    loads[2].start()
    loads[3].start()

    @pl.loop(1, n_seq)
    def _(j):
        pl.semaphore_signal(
            barrier, inc=1, device_id={"seq": lax.rem(seq + j, n_seq)}, device_id_type=MESH
        )

    for j in range(1, n_tp):
        pl.semaphore_signal(
            barrier, inc=1, device_id={"tp": to_tp(j)}, device_id_type=MESH
        )

    class Gather:
        def __init__(self, source, ref, sems):
            half = ref.shape[1] // 2
            self.source, self.ref, self.sems = source, ref, sems
            self.mine = pl.ds(pl.multiple_of(core * half, half), half)
            self.other = pl.ds(pl.multiple_of((1 - core) * half, half), half)

        def over(self, j, slot):
            return pltpu.make_async_remote_copy(
                src_ref=self.source(j, self.mine), dst_ref=self.ref.at[slot, self.mine],
                send_sem=self.sems.at[0, j], recv_sem=self.sems.at[1, j],
                device_id={"tp": to_tp(j)}, device_id_type=MESH,
            )

        def across(self, j, part):
            t = from_tp(j)
            return pltpu.make_async_remote_copy(
                src_ref=self.ref.at[t, part], dst_ref=self.ref.at[t, part],
                send_sem=self.sems.at[2, j], recv_sem=self.sems.at[3, j],
                device_id={"seq": seq + 1 - 2 * core}, device_id_type=MESH,
            )

        def send(self):
            for j in ORDER:
                self.over(j, tp).start()

        def swap(self, j):
            self.over(j, from_tp(j)).wait_recv()
            self.across(j, self.mine).start()

        def ready(self, j):
            self.across(j, self.other).wait_recv()

        def drain(self):
            for j in ORDER:
                self.over(j, tp).wait_send()
                self.across(j, self.mine).wait_send()

    def columns_of(j):
        return pl.ds(pl.multiple_of(to_tp(j) * W, W), W)

    wq_all = Gather(lambda j, part: w_hbm.at[0, part], wq, wq_sems)
    wo_all = Gather(lambda j, part: wo_hbm.at[part, columns_of(j)], wo, wo_sems)
    km_all = Gather(lambda j, part: kmt.at[tp, part], kmt, km_sems)
    mt_all = Gather(lambda j, part: midt.at[tp, part], midt, mt_sems)

    def own_rows(i):
        x_load(i).wait()
        rows = rows_of(i)
        xc = x[rows, :]
        kp = dot(xc, wk[...])
        qp = dot(xc, wq[tp]) * LOG_SCALE
        k[rows, :] = kp.astype(bf16)
        q[tp, rows, :] = qp.astype(bf16)
        for s in range(C // SEG):
            at = i * (C // SEG) + s
            part = slice(s * SEG, (s + 1) * SEG)
            means[pl.ds(at, 1), :] = jnp.sum(qp[part], axis=0, keepdims=True) * (1.0 / SEG)
            means[pl.ds(8 + at, 1), :] = jnp.sum(kp[part], axis=0, keepdims=True) * (1.0 / SEG)

    loads[0].wait()
    loads[1].wait()
    own_rows(0)
    pl.semaphore_wait(barrier, n_seq - 1 + n_tp - 1)
    wq_all.send()
    wo_all.send()

    @pl.loop(1, n_chunks)
    def _(i):
        own_rows(i)

    def exchange(copy_of):
        @pl.loop(1, n_seq)
        def _(j):
            copy_of(j, seq).start()

    def finish(copy_of):
        @pl.loop(1, n_seq)
        def _(j):
            copy_of(j, lax.rem(seq + n_seq - j, n_seq)).wait_recv()

    def finish_sends(copy_of):
        @pl.loop(1, n_seq)
        def _(j):
            copy_of(j, seq).wait_send()

    def remote_seq(src, dst, ss, rs, j):
        return pltpu.make_async_remote_copy(
            src_ref=src, dst_ref=dst, send_sem=ss.at[j], recv_sem=rs.at[j],
            device_id={"seq": lax.rem(seq + j, n_seq)}, device_id_type=MESH,
        )

    def mk_copy(j, slot):
        return remote_seq(mk_s, mk_r.at[slot], mk_ss, mk_rs, j)

    def lv_copy(j, slot):
        return remote_seq(lv_s.at[lax.rem(seq + j, n_seq)], lv_r.at[slot], lv_ss, lv_rs, j)

    def mid_copy(j, slot):
        return remote_seq(mid_s, mid_r.at[slot], mid_ss, mid_rs, j)

    mk_s[...] = means[...].astype(bf16)
    exchange(mk_copy)
    mk_r[seq] = means[...].astype(bf16)

    loads[2].wait()
    ones = jnp.ones((C, 128), bf16)

    def own_values(i):
        rows = rows_of(i)
        vp = dot(x[rows, :], wv[...]).astype(bf16)
        for p in range(2):
            v[p, rows, 0:128] = pair_columns(vp, p)
            v[p, rows, 128:256] = ones

    def other_queries(t, rows):
        q[t, rows, :] = (dot(x[rows, :], wq[t]) * LOG_SCALE).astype(bf16)

    pl.loop(0, n_chunks - 1)(own_values)
    wq_all.swap(ORDER[0])
    own_values(n_chunks - 1)
    wq_all.ready(ORDER[0])

    @pl.loop(0, n_chunks)
    def _(i):
        other_queries(from_tp(ORDER[0]), rows_of(i))

    finish(mk_copy)
    marks = mk_r[...].astype(f32)
    q_marks = marks[:, 0:8, :].reshape(MARKS, W)
    k_marks = marks[:, 8:16, :].reshape(MARKS, W)
    kmt[tp] = k_marks.astype(bf16)
    km_all.send()
    for h in range(4):
        qm[h] = one_head(pair_columns(q_marks, h // 2), h).astype(bf16)
        km[tp * 4 + h] = one_head(pair_columns(k_marks, h // 2), h).astype(bf16)

    acc[...] = jnp.zeros_like(acc)
    mx[...] = jnp.full_like(mx, -jnp.inf)

    @pl.loop(0, n_chunks)
    def _(i):
        rows = rows_of(i)
        for h in range(4):
            p = h // 2
            s = dot_nt(qm[h], k[rows, p * 128 : (p + 1) * 128])
            before = mx[h]
            now = jnp.maximum(before, jnp.max(s, axis=1, keepdims=True))
            e = jnp.exp2(s - now[:, :1]).astype(bf16)
            mx[h] = now
            fade = jnp.exp2(before - now)
            acc[h] = acc[h] * jnp.concatenate([fade, fade], 1) + dot(e, v[p, rows, :])

    for j in ORDER[1:]:
        wq_all.swap(j)
    sub = lax.broadcasted_iota(jnp.int32, (8, W), 0)
    for p in range(2):
        even, odd = acc[2 * p], acc[2 * p + 1]
        mean_values = jnp.where(
            low_lanes(MARKS), even[:, :128] / even[:, 128:], odd[:, :128] / odd[:, 128:]
        ).T
        for i, r in enumerate((even, odd)):
            h = 2 * p + i
            level = (mx[h] + jnp.log2(r[:, 128:])).T[0:8, :]
            first = level.astype(bf16).astype(f32)
            second = (level - first).astype(bf16).astype(f32)
            third = level - first - second
            lines = jnp.where(
                sub == 0, first, jnp.where(sub == 1, second, jnp.where(sub == 2, third, 0.0))
            )
            for b in range(8):
                part = mean_values[i * 64 + b * 8 : i * 64 + b * 8 + 8, :]
                lv_s[h * 8 + b] = jnp.concatenate([part, lines], 0).astype(bf16)
    exchange(lv_copy)
    lv_r[seq] = lv_s[seq]
    for j in ORDER:
        km_all.swap(j)
    for j in ORDER:
        wo_all.swap(j)

    head = lax.div(seq, 8)
    terms = softmax_terms(dot_nt(qm[head], km[tp * 4 + head]))
    kernel_a = terms / jnp.sum(terms, axis=1, keepdims=True)
    col = jnp.max(jnp.sum(kernel_a, axis=0, keepdims=True), axis=1, keepdims=True)
    row = jnp.max(jnp.sum(kernel_a, axis=1, keepdims=True), axis=0, keepdims=True)
    a_ref[...] = kernel_a
    z_ref[...] = kernel_a.T / (col * row)
    for j in ORDER[1:]:
        wq_all.ready(j)

    def unit(u):
        t = lax.rem(tp + 3 + 3 * lax.div(u, 16), n_tp)
        other_queries(t, pl.ds(pl.multiple_of(lax.rem(u, 16) * 256, 256), 256))

    @pl.loop(0, NEWTON)
    def _(turn):
        eye = jnp.where(
            lax.broadcasted_iota(jnp.int32, (MARKS, MARKS), 0)
            == lax.broadcasted_iota(jnp.int32, (MARKS, MARKS), 1),
            1.0,
            0.0,
        )
        z = z_ref[...]
        az = dot3(a_ref[...], z)
        unit(turn * 4)
        inner = dot3(az, 7.0 * eye - az)
        unit(turn * 4 + 1)
        outer = dot3(az, 15.0 * eye - inner)
        unit(turn * 4 + 2)
        z_ref[...] = 0.25 * dot3(z, 13.0 * eye - outer)
        unit(turn * 4 + 3)

    finish(lv_copy)
    lv = lv_r[...].astype(f32)
    level = lv[:, 8:9, :] + lv[:, 9:10, :] + lv[:, 10:11, :]
    share = jnp.exp2(level - jnp.max(level, axis=0, keepdims=True))
    columns = jnp.sum(lv[:, 0:8, :] * share, axis=0) / jnp.sum(share, axis=0)
    ch, cl = halves(columns)
    zh, zl = halves(z_ref[...])
    middle = dot_nt(jnp.concatenate([ch, cl, ch], 1), jnp.concatenate([zh, zh, zl], 1))
    mid_s[...] = middle
    exchange(mid_copy)
    mid_r[seq] = middle

    def terms_of(t, e, rows):
        for h in range(4):
            p = h // 2
            logits = dot_nt(q[t, rows, p * 128 : (p + 1) * 128], km[t * 4 + h])
            e[rows, h * MARKS : (h + 1) * MARKS] = softmax_terms(logits).astype(bf16)

    def attended_of(t, e, rows):
        for p in range(2):
            r = dot(e[rows, p * 512 : (p + 1) * 512], midb[t * 2 + p])
            q[t, rows, p * 128 : (p + 1) * 128] = (r[:, :128] * (1.0 / r[:, 128:])).astype(bf16)

    pl.loop(24, 32)(unit)

    @pl.loop(0, n_chunks)
    def _(i):
        terms_of(tp, e_a, rows_of(i))

    def place_middle(t):
        m = midt[t].astype(f32)
        low = low_lanes(MARKS)
        for p in range(2):
            both = pair_columns(m, p)
            for i in range(2):
                mask = low if i == 0 else ~low
                midb[t * 2 + p, i * MARKS : (i + 1) * MARKS, :] = jnp.concatenate(
                    [jnp.where(mask, both, 0.0), jnp.where(mask, 1.0, 0.0)], 1
                ).astype(bf16)

    finish(mid_copy)
    midt[tp] = mid_r[...].reshape(W, MARKS).T.astype(bf16)
    mt_all.send()
    place_middle(tp)
    for j in ORDER:
        t = from_tp(j)
        km_all.ready(j)
        others = kmt[t].astype(f32)
        for h in range(4):
            km[t * 4 + h] = one_head(pair_columns(others, h // 2), h).astype(bf16)
        wo_all.ready(j)
    loads[3].wait()

    groups = [tp] + [from_tp(j) for j in ORDER]
    buffers = (e_a, e_b)

    def step(g, i):
        rows = rows_of(i)
        attended_of(groups[g], buffers[g % 2], rows)
        terms_of(groups[g + 1], buffers[(g + 1) % 2], rows)

    pl.loop(0, n_chunks - 1)(functools.partial(step, 0))
    for j in ORDER:
        mt_all.swap(j)
    step(0, n_chunks - 1)
    for j in ORDER:
        mt_all.ready(j)
        place_middle(from_tp(j))
    pl.loop(0, n_chunks)(functools.partial(step, 1))
    pl.loop(0, n_chunks)(functools.partial(step, 2))

    def out_copy(i):
        return pltpu.make_async_copy(outv.at[rows_of(i)], out_hbm.at[rows_of(i)], out_sem.at[i])

    @pl.loop(0, n_chunks)
    def _(i):
        rows = rows_of(i)
        attended_of(groups[3], buffers[1], rows)
        total = dot(q[groups[0], rows, :], wo[groups[0]])
        for t in groups[1:]:
            total = total + dot(q[t, rows, :], wo[t])
        outv[rows, :] = total.astype(bf16)
        out_copy(i).start()

    for copy_of in (mk_copy, lv_copy, mid_copy):
        finish_sends(copy_of)
    for gather in (wq_all, wo_all, km_all, mt_all):
        gather.drain()
    for i in range(n_chunks):
        out_copy(i).wait()


def on_device(n_seq, n_tp, tokens, w_qkv, w_out):
    vmem = pltpu.VMEM
    sems = pltpu.SemaphoreType.DMA
    scratch = [
        vmem((T, D), bf16),
        vmem((D, W), bf16),
        vmem((D, W), bf16),
        vmem((n_tp, D, W), bf16),
        vmem((n_tp, W, W), bf16),
        vmem((n_tp, T, W), bf16),
        vmem((T, W), bf16),
        vmem((2, T, 256), bf16),
        vmem((16, W), f32),
        vmem((16, W), bf16),
        vmem((n_seq, 16, W), bf16),
        vmem((4, MARKS, 128), bf16),
        vmem((4 * n_tp, MARKS, 128), bf16),
        vmem((n_tp, MARKS, W), bf16),
        vmem((4, MARKS, 256), f32),
        vmem((4, MARKS, 128), f32),
        vmem((n_seq, 16, MARKS), bf16),
        vmem((n_seq, 16, MARKS), bf16),
        vmem((MARKS, MARKS), f32),
        vmem((MARKS, MARKS), f32),
        vmem((8, MARKS), f32),
        vmem((n_seq, 8, MARKS), f32),
        vmem((n_tp, MARKS, W), bf16),
        vmem((2 * n_tp, 2 * MARKS, 256), bf16),
        vmem((T, 4 * MARKS), bf16),
        vmem((T, 4 * MARKS), bf16),
        vmem((T, W), bf16),
        sems((4,)), sems((T // C,)), sems((T // C,)),
        *[sems((n_seq,))] * 6,
        *[sems((4, n_tp))] * 4,
    ]
    hbm = pl.BlockSpec(memory_space=pl.ANY)
    return pl.pallas_call(
        functools.partial(kernel, n_seq, n_tp),
        out_shape=jax.ShapeDtypeStruct((T, W), bf16),
        in_specs=[hbm] * 3,
        out_specs=hbm,
        scratch_shapes=scratch,
        compiler_params=pltpu.CompilerParams(
            collective_id=0, has_side_effects=True, vmem_limit_bytes=60 * 2**20
        ),
    )(tokens, w_qkv, w_out)


def solution(mesh):
    return jax.shard_map(
        functools.partial(on_device, mesh.shape["seq"], mesh.shape["tp"]),
        mesh=mesh,
        in_specs=(P("seq", None), P(None, None, "tp"), P("tp", None)),
        out_specs=P("seq", "tp"),
        check_vma=False,
    )
```

```python
import functools
import math

import jax
import jax.numpy as jnp
from jax import lax
from jax.experimental import pallas as pl
from jax.experimental.pallas import tpu as pltpu
from jax.sharding import PartitionSpec as P

HEAD_DIM = 64
MARKS = 256
NEWTON = 6
UNITS = 7
D = 1024
W = 256
T = 4096
SEG = 512
C = 1024
LOG_SCALE = HEAD_DIM**-0.5 * math.log2(math.e)
bf16, f32 = jnp.bfloat16, jnp.float32
NT = (((1,), (1,)), ((), ()))
MESH = pl.DeviceIdType.MESH
ORDER = (3, 1, 2)


def dot(a, b):
    return jnp.dot(a, b, preferred_element_type=f32)


def dot_nt(a, b):
    return lax.dot_general(a, b, NT, preferred_element_type=f32)


def halves(a):
    hi = a.astype(bf16)
    return hi, (a - hi.astype(f32)).astype(bf16)


def dot3(a, b):
    ah, al = halves(a)
    bh, bl = halves(b)
    return dot(jnp.concatenate([ah, al, ah], 1), jnp.concatenate([bh, bh, bl], 0))


def low_lanes(rows):
    return lax.broadcasted_iota(jnp.int32, (rows, 128), 1) < 64


def one_head(block, head):
    low = low_lanes(block.shape[0])
    return jnp.where(low if head % 2 == 0 else ~low, block, 0.0)


def pair_columns(array, pair):
    return array[:, pair * 128 : (pair + 1) * 128]


def softmax_terms(logits):
    return jnp.exp2(logits - jnp.max(logits, axis=1, keepdims=True))


def three_lines(level, sub):
    first = level.astype(bf16).astype(f32)
    second = (level - first).astype(bf16).astype(f32)
    third = level - first - second
    return jnp.where(
        sub == 0, first, jnp.where(sub == 1, second, jnp.where(sub == 2, third, 0.0))
    )


def kernel(
    n_seq, n_tp,
    x_hbm, w_hbm, wo_hbm, out_hbm,
    x, wk, wv, wq, wo, q, k, v, means, mk_r, qm, km, kmt,
    lv_s, lv_t, lv_m, lv_r, a_ref, z_ref, mid_r, midt, midb, e_own, outv,
    load_sem, x_sem, out_sem,
    mk_sems, lv_sems, mid_sems, mate_sems,
    wq_sems, wo_sems, km_sems, mt_sems,
):
    seq, tp = lax.axis_index("seq"), lax.axis_index("tp")
    core, chip, n_chips = lax.rem(seq, 2), lax.div(seq, 2), n_seq // 2
    n_chunks = T // C

    def rows_of(i):
        return pl.ds(pl.multiple_of(i * C, C), C)

    def to_tp(j):
        return lax.rem(tp + j, n_tp)

    def from_tp(j):
        return lax.rem(tp + n_tp - j, n_tp)

    barrier = pltpu.get_barrier_semaphore()

    loads = [
        pltpu.make_async_copy(w_hbm.at[1], wk, load_sem.at[0]),
        pltpu.make_async_copy(w_hbm.at[0], wq.at[tp], load_sem.at[1]),
        pltpu.make_async_copy(w_hbm.at[2], wv, load_sem.at[2]),
        pltpu.make_async_copy(
            wo_hbm.at[:, pl.ds(pl.multiple_of(tp * W, W), W)], wo.at[tp], load_sem.at[3]
        ),
    ]

    def x_load(i):
        return pltpu.make_async_copy(x_hbm.at[rows_of(i)], x.at[rows_of(i)], x_sem.at[i])

    loads[0].start()
    loads[1].start()
    for i in range(n_chunks):
        x_load(i).start()
    loads[2].start()
    loads[3].start()

    def peer(j):
        return {"seq": 2 * lax.rem(chip + j, n_chips) + core}

    mate = {"seq": seq + 1 - 2 * core}

    @pl.loop(1, n_chips)
    def _(j):
        pl.semaphore_signal(barrier, inc=1, device_id=peer(j), device_id_type=MESH)

    pl.semaphore_signal(barrier, inc=1, device_id=mate, device_id_type=MESH)
    for j in range(1, n_tp):
        pl.semaphore_signal(
            barrier, inc=1, device_id={"tp": to_tp(j)}, device_id_type=MESH
        )

    class Gather:
        def __init__(self, source, ref, sems):
            half = ref.shape[1] // 2
            self.source, self.ref, self.sems = source, ref, sems
            self.mine = pl.ds(pl.multiple_of(core * half, half), half)
            self.other = pl.ds(pl.multiple_of((1 - core) * half, half), half)

        def over(self, j, slot):
            return pltpu.make_async_remote_copy(
                src_ref=self.source(j, self.mine), dst_ref=self.ref.at[slot, self.mine],
                send_sem=self.sems.at[0, j], recv_sem=self.sems.at[1, j],
                device_id={"tp": to_tp(j)}, device_id_type=MESH,
            )

        def across(self, j, part):
            t = from_tp(j)
            return pltpu.make_async_remote_copy(
                src_ref=self.ref.at[t, part], dst_ref=self.ref.at[t, part],
                send_sem=self.sems.at[2, j], recv_sem=self.sems.at[3, j],
                device_id=mate, device_id_type=MESH,
            )

        def send(self):
            for j in ORDER:
                self.over(j, tp).start()

        def swap(self, j):
            self.over(j, from_tp(j)).wait_recv()
            self.across(j, self.mine).start()

        def ready(self, j):
            self.across(j, self.other).wait_recv()

        def drain(self):
            for j in ORDER:
                self.over(j, tp).wait_send()
                self.across(j, self.mine).wait_send()

    def columns_of(j):
        return pl.ds(pl.multiple_of(to_tp(j) * W, W), W)

    wq_all = Gather(lambda j, part: w_hbm.at[0, part], wq, wq_sems)
    wo_all = Gather(lambda j, part: wo_hbm.at[part, columns_of(j)], wo, wo_sems)
    km_all = Gather(lambda j, part: kmt.at[tp, part], kmt, km_sems)
    mt_all = Gather(lambda j, part: midt.at[tp, part], midt, mt_sems)

    def own_rows(i):
        x_load(i).wait()
        rows = rows_of(i)
        xc = x[rows, :]
        kp = dot(xc, wk[...])
        qp = dot(xc, wq[tp]) * LOG_SCALE
        k[rows, :] = kp.astype(bf16)
        q[tp, rows, :] = qp.astype(bf16)
        for s in range(C // SEG):
            at = i * (C // SEG) + s
            part = slice(s * SEG, (s + 1) * SEG)
            means[pl.ds(at, 1), :] = jnp.sum(qp[part], axis=0, keepdims=True) * (1.0 / SEG)
            means[pl.ds(8 + at, 1), :] = jnp.sum(kp[part], axis=0, keepdims=True) * (1.0 / SEG)

    def to_chips(src, dst, sems, j):
        return pltpu.make_async_remote_copy(
            src_ref=src, dst_ref=dst, send_sem=sems.at[0, j], recv_sem=sems.at[1, j],
            device_id=peer(j), device_id_type=MESH,
        )

    def to_mate(src, dst, n):
        return pltpu.make_async_remote_copy(
            src_ref=src, dst_ref=dst, send_sem=mate_sems.at[0, n], recv_sem=mate_sems.at[1, n],
            device_id=mate, device_id_type=MESH,
        )

    def chip_before(j):
        return lax.rem(chip + n_chips - j, n_chips)

    class Spread:
        def __init__(self, ref, sems, n):
            self.ref, self.sems, self.n = ref, sems, n

        def copy(self, j, place):
            return to_chips(self.ref.at[core, chip], self.ref.at[core, place], self.sems, j)

        def swap_copy(self, side):
            return to_mate(self.ref.at[side], self.ref.at[side], self.n)

        def send(self):
            @pl.loop(1, n_chips)
            def _(j):
                self.copy(j, chip).start()

        def swap(self):
            @pl.loop(1, n_chips)
            def _(j):
                self.copy(j, chip_before(j)).wait_recv()

            self.swap_copy(core).start()

        def ready(self):
            self.swap_copy(1 - core).wait_recv()

        def drain(self):
            @pl.loop(1, n_chips)
            def _(j):
                self.copy(j, chip).wait_send()

            self.swap_copy(core).wait_send()

    mk_all = Spread(mk_r, mk_sems, 0)
    mid_all = Spread(mid_r, mid_sems, 1)

    loads[0].wait()
    loads[1].wait()
    pl.loop(0, n_chunks)(own_rows)
    mk_r[core, chip] = means[...].astype(bf16)
    pl.semaphore_wait(barrier, n_chips + n_tp - 1)
    mk_all.send()
    wq_all.send()
    wo_all.send()

    loads[2].wait()
    ones = jnp.ones((C, 128), bf16)

    def own_values(i):
        rows = rows_of(i)
        vp = dot(x[rows, :], wv[...]).astype(bf16)
        for p in range(2):
            v[p, rows, 0:128] = pair_columns(vp, p)
            v[p, rows, 128:256] = ones

    pl.loop(0, n_chunks - 1)(own_values)
    mk_all.swap()
    own_values(n_chunks - 1)
    mk_all.ready()

    marks = mk_r[...].astype(f32).reshape(n_seq, 16, W)
    q_marks = marks[:, 0:8, :].reshape(MARKS, W)
    k_marks = marks[:, 8:16, :].reshape(MARKS, W)
    kmt[tp] = k_marks.astype(bf16)
    km_all.send()
    for h in range(4):
        qm[h] = one_head(pair_columns(q_marks, h // 2), h).astype(bf16)
        km[tp * 4 + h] = one_head(pair_columns(k_marks, h // 2), h).astype(bf16)

    sub = lax.broadcasted_iota(jnp.int32, (8, W), 0)
    for p in range(2):
        parts, levels = [], []
        for i in range(2):
            s = dot_nt(qm[2 * p + i], k[:, p * 128 : (p + 1) * 128])
            top = jnp.max(s, axis=1, keepdims=True)
            r = dot(jnp.exp2(s - top).astype(bf16), v[p])
            parts.append(r[:, :128] / r[:, 128:])
            levels.append((top + jnp.log2(r[:, 128:])).T[0:8, :])
        mean_values = jnp.where(low_lanes(MARKS), parts[0], parts[1]).T
        for i, level in enumerate(levels):
            lines = three_lines(level, sub)
            for b in range(8):
                part = mean_values[i * 64 + b * 8 : i * 64 + b * 8 + 8, :]
                at = (2 * p + i) * 8 + b
                lv_s[at // n_chips, at % n_chips] = jnp.concatenate([part, lines], 0).astype(bf16)

    lv_mate = to_mate(lv_s.at[1 - core], lv_t, 2)
    lv_mate.start()
    wq_all.swap(ORDER[0])
    for j in ORDER:
        km_all.swap(j)

    def lv_copy(j, place):
        return to_chips(lv_m.at[lax.rem(chip + j, n_chips)], lv_r.at[place], lv_sems, j)

    def merged(blocks):
        level = blocks[:, 8:9, :] + blocks[:, 9:10, :] + blocks[:, 10:11, :]
        top = jnp.max(level, axis=0, keepdims=True)
        share = jnp.exp2(level - top)
        total = jnp.sum(share, axis=0)
        return jnp.sum(blocks[:, 0:8, :] * share, axis=0) / total, top[0] + jnp.log2(total)

    head = 2 * core + lax.div(chip, 8)
    terms = softmax_terms(dot_nt(qm[head], km[tp * 4 + head]))
    kernel_a = terms / jnp.sum(terms, axis=1, keepdims=True)
    col = jnp.max(jnp.sum(kernel_a, axis=0, keepdims=True), axis=1, keepdims=True)
    row = jnp.max(jnp.sum(kernel_a, axis=1, keepdims=True), axis=0, keepdims=True)
    a_ref[...] = kernel_a
    z_ref[...] = kernel_a.T / (col * row)
    wq_all.ready(ORDER[0])

    def unit(u):
        g = lax.div(u, 16)
        t = lax.rem(tp + 1 + 2 * g + lax.div(g, 2), n_tp)
        rows = pl.ds(pl.multiple_of(lax.rem(u, 16) * 256, 256), 256)
        q[t, rows, :] = (dot(x[rows, :], wq[t]) * LOG_SCALE).astype(bf16)

    def newton_turn(turn):
        eye = jnp.where(
            lax.broadcasted_iota(jnp.int32, (MARKS, MARKS), 0)
            == lax.broadcasted_iota(jnp.int32, (MARKS, MARKS), 1),
            1.0,
            0.0,
        )
        first = turn * UNITS
        z = z_ref[...]
        az = dot3(a_ref[...], z)
        unit(first)
        unit(first + 1)
        inner = dot3(az, 7.0 * eye - az)
        unit(first + 2)
        unit(first + 3)
        outer = dot3(az, 15.0 * eye - inner)
        unit(first + 4)
        unit(first + 5)
        z_ref[...] = 0.25 * dot3(z, 13.0 * eye - outer)
        unit(first + 6)

    newton_turn(0)
    lv_mate.wait_recv()
    for c in range(n_chips):
        values, level = merged(jnp.stack([lv_s[core, c].astype(f32), lv_t[c].astype(f32)]))
        lines = three_lines(jnp.broadcast_to(level, (8, MARKS)), sub)
        lv_m[c] = jnp.concatenate([values, lines], 0).astype(bf16)
    @pl.loop(1, n_chips)
    def _(j):
        lv_copy(j, chip).start()

    lv_r[chip] = lv_m[chip]
    newton_turn(1)
    for j in ORDER[1:]:
        wq_all.swap(j)
    for j in ORDER:
        wo_all.swap(j)
    for j in ORDER[1:]:
        wq_all.ready(j)
    pl.loop(2, NEWTON)(newton_turn)

    @pl.loop(1, n_chips)
    def _(j):
        lv_copy(j, chip_before(j)).wait_recv()

    columns, _ = merged(lv_r[...].astype(f32))
    ch, cl = halves(columns)
    zh, zl = halves(z_ref[...])
    mid_r[core, chip] = dot_nt(
        jnp.concatenate([ch, cl, ch], 1), jnp.concatenate([zh, zh, zl], 1)
    )
    mid_all.send()

    @pl.loop(0, n_chunks)
    def _(i):
        rows = rows_of(i)
        for h in range(4):
            p = h // 2
            logits = dot_nt(q[tp, rows, p * 128 : (p + 1) * 128], km[tp * 4 + h])
            e_own[rows, h * MARKS : (h + 1) * MARKS] = softmax_terms(logits).astype(bf16)

    mid_all.swap()
    pl.loop(UNITS * NEWTON, 48)(unit)
    for j in ORDER:
        t = from_tp(j)
        km_all.ready(j)
        others = kmt[t].astype(f32)
        for h in range(4):
            km[t * 4 + h] = one_head(pair_columns(others, h // 2), h).astype(bf16)
    mid_all.ready()

    def place_middle(t):
        m = midt[t].astype(f32)
        low = low_lanes(MARKS)
        for p in range(2):
            both = pair_columns(m, p)
            for i in range(2):
                mask = low if i == 0 else ~low
                midb[t * 2 + p, i * MARKS : (i + 1) * MARKS, :] = jnp.concatenate(
                    [jnp.where(mask, both, 0.0), jnp.where(mask, 1.0, 0.0)], 1
                ).astype(bf16)

    midt[tp] = mid_r[...].reshape(W, MARKS).T.astype(bf16)
    mt_all.send()
    place_middle(tp)

    def normalised(r):
        return (r[:, :128] * (1.0 / r[:, 128:])).astype(bf16)

    def own_attended(i):
        rows = rows_of(i)
        for p in range(2):
            r = dot(e_own[rows, p * 512 : (p + 1) * 512], midb[tp * 2 + p])
            q[tp, rows, p * 128 : (p + 1) * 128] = normalised(r)

    pl.loop(0, n_chunks - 1)(own_attended)
    for j in ORDER:
        mt_all.swap(j)
    own_attended(n_chunks - 1)
    loads[3].wait()
    for j in ORDER:
        wo_all.ready(j)
        mt_all.ready(j)
        place_middle(from_tp(j))
    groups = [from_tp(j) for j in ORDER]

    def out_copy(i):
        return pltpu.make_async_copy(outv.at[rows_of(i)], out_hbm.at[rows_of(i)], out_sem.at[i])

    @pl.loop(0, n_chunks)
    def _(i):
        rows = rows_of(i)
        parts = [q[tp, rows, :]]
        for t in groups:
            for p in range(2):
                qc = q[t, rows, p * 128 : (p + 1) * 128]
                e = [
                    softmax_terms(dot_nt(qc, km[t * 4 + 2 * p + b])).astype(bf16) for b in range(2)
                ]
                parts.append(normalised(dot(jnp.concatenate(e, 1), midb[t * 2 + p])))
        weights = jnp.concatenate([wo[t] for t in [tp] + groups], 0)
        outv[rows, :] = dot(jnp.concatenate(parts, 1), weights).astype(bf16)
        out_copy(i).start()

    @pl.loop(1, n_chips)
    def _(j):
        lv_copy(j, chip).wait_send()

    lv_mate.wait_send()
    for part in (mk_all, mid_all, wq_all, wo_all, km_all, mt_all):
        part.drain()
    for i in range(n_chunks):
        out_copy(i).wait()


def on_device(n_seq, n_tp, tokens, w_qkv, w_out):
    vmem = pltpu.VMEM
    sems = pltpu.SemaphoreType.DMA
    n_chips = n_seq // 2
    scratch = [
        vmem((T, D), bf16),
        vmem((D, W), bf16),
        vmem((D, W), bf16),
        vmem((n_tp, D, W), bf16),
        vmem((n_tp, W, W), bf16),
        vmem((n_tp, T, W), bf16),
        vmem((T, W), bf16),
        vmem((2, T, 256), bf16),
        vmem((16, W), f32),
        vmem((2, n_chips, 16, W), bf16),
        vmem((4, MARKS, 128), bf16),
        vmem((4 * n_tp, MARKS, 128), bf16),
        vmem((n_tp, MARKS, W), bf16),
        vmem((2, n_chips, 16, MARKS), bf16),
        vmem((n_chips, 16, MARKS), bf16),
        vmem((n_chips, 16, MARKS), bf16),
        vmem((n_chips, 16, MARKS), bf16),
        vmem((MARKS, MARKS), f32),
        vmem((MARKS, MARKS), f32),
        vmem((2, n_chips, 8, MARKS), f32),
        vmem((n_tp, MARKS, W), bf16),
        vmem((2 * n_tp, 2 * MARKS, 256), bf16),
        vmem((T, 4 * MARKS), bf16),
        vmem((T, W), bf16),
        sems((4,)), sems((T // C,)), sems((T // C,)),
        *[sems((2, n_chips))] * 3,
        sems((2, 3)),
        *[sems((4, n_tp))] * 4,
    ]
    hbm = pl.BlockSpec(memory_space=pl.ANY)
    return pl.pallas_call(
        functools.partial(kernel, n_seq, n_tp),
        out_shape=jax.ShapeDtypeStruct((T, W), bf16),
        in_specs=[hbm] * 3,
        out_specs=hbm,
        scratch_shapes=scratch,
        compiler_params=pltpu.CompilerParams(
            collective_id=0, has_side_effects=True, vmem_limit_bytes=60 * 2**20
        ),
    )(tokens, w_qkv, w_out)


def solution(mesh):
    return jax.shard_map(
        functools.partial(on_device, mesh.shape["seq"], mesh.shape["tp"]),
        mesh=mesh,
        in_specs=(P("seq", None), P(None, None, "tp"), P("tp", None)),
        out_specs=P("seq", "tp"),
        check_vma=False,
    )
```

```python
import functools
import math

import jax
import jax.numpy as jnp
from jax import lax
from jax.experimental import pallas as pl
from jax.experimental.pallas import tpu as pltpu
from jax.sharding import PartitionSpec as P

HEAD_DIM = 64
MARKS = 256
NEWTON = 6
UNITS = 4
D = 1024
W = 256
T = 4096
SEG = 512
C = 1024
LOG_SCALE = HEAD_DIM**-0.5 * math.log2(math.e)
bf16, f32 = jnp.bfloat16, jnp.float32
NT = (((1,), (1,)), ((), ()))
MESH = pl.DeviceIdType.MESH
ORDER = (3, 1, 2)


def dot(a, b):
    return jnp.dot(a, b, preferred_element_type=f32)


def dot_nt(a, b):
    return lax.dot_general(a, b, NT, preferred_element_type=f32)


def halves(a):
    hi = a.astype(bf16)
    return hi, (a - hi.astype(f32)).astype(bf16)


def dot3(a, b):
    ah, al = halves(a)
    bh, bl = halves(b)
    return dot(jnp.concatenate([ah, al, ah], 1), jnp.concatenate([bh, bh, bl], 0))


def low_lanes(rows):
    return lax.broadcasted_iota(jnp.int32, (rows, 128), 1) < 64


def one_head(block, head):
    low = low_lanes(block.shape[0])
    return jnp.where(low if head % 2 == 0 else ~low, block, 0.0)


def pair_columns(array, pair):
    return array[:, pair * 128 : (pair + 1) * 128]


def softmax_terms(logits):
    return jnp.exp2(logits - jnp.max(logits, axis=1, keepdims=True))


def three_lines(level, sub):
    first = level.astype(bf16).astype(f32)
    second = (level - first).astype(bf16).astype(f32)
    third = level - first - second
    return jnp.where(
        sub == 0, first, jnp.where(sub == 1, second, jnp.where(sub == 2, third, 0.0))
    )


def kernel(
    n_seq, n_tp,
    x_hbm, w_hbm, wo_hbm, out_hbm,
    x, wk, wv, wq, wo, q, k, v, means, mk_r, qm, km, kmt,
    lv_s, lv_t, lv_m, lv_r, a_ref, z_ref, mid_r, midt, midb, e_own, outv,
    load_sem, x_sem, out_sem,
    mk_sems, lv_sems, mid_sems, mate_sems,
    wq_sems, wo_sems, km_sems, mt_sems,
):
    seq, tp = lax.axis_index("seq"), lax.axis_index("tp")
    core, chip, n_chips = lax.rem(seq, 2), lax.div(seq, 2), n_seq // 2
    n_chunks = T // C

    def rows_of(i):
        return pl.ds(pl.multiple_of(i * C, C), C)

    def to_tp(j):
        return lax.rem(tp + j, n_tp)

    def from_tp(j):
        return lax.rem(tp + n_tp - j, n_tp)

    barrier = pltpu.get_barrier_semaphore()

    loads = [
        pltpu.make_async_copy(w_hbm.at[1], wk, load_sem.at[0]),
        pltpu.make_async_copy(w_hbm.at[0], wq.at[tp], load_sem.at[1]),
        pltpu.make_async_copy(w_hbm.at[2], wv, load_sem.at[2]),
        pltpu.make_async_copy(
            wo_hbm.at[:, pl.ds(pl.multiple_of(tp * W, W), W)], wo.at[tp], load_sem.at[3]
        ),
    ]

    def x_load(i):
        return pltpu.make_async_copy(x_hbm.at[rows_of(i)], x.at[rows_of(i)], x_sem.at[i])

    loads[0].start()
    loads[1].start()
    for i in range(n_chunks):
        x_load(i).start()
    loads[2].start()
    loads[3].start()

    def peer(j):
        return {"seq": 2 * lax.rem(chip + j, n_chips) + core}

    mate = {"seq": seq + 1 - 2 * core}

    @pl.loop(1, n_chips)
    def _(j):
        pl.semaphore_signal(barrier, inc=1, device_id=peer(j), device_id_type=MESH)

    pl.semaphore_signal(barrier, inc=1, device_id=mate, device_id_type=MESH)
    for j in range(1, n_tp):
        pl.semaphore_signal(
            barrier, inc=1, device_id={"tp": to_tp(j)}, device_id_type=MESH
        )

    class Gather:
        def __init__(self, source, ref, sems):
            half = ref.shape[1] // 2
            self.source, self.ref, self.sems = source, ref, sems
            self.mine = pl.ds(pl.multiple_of(core * half, half), half)
            self.other = pl.ds(pl.multiple_of((1 - core) * half, half), half)

        def over(self, j, slot):
            return pltpu.make_async_remote_copy(
                src_ref=self.source(j, self.mine), dst_ref=self.ref.at[slot, self.mine],
                send_sem=self.sems.at[0, j], recv_sem=self.sems.at[1, j],
                device_id={"tp": to_tp(j)}, device_id_type=MESH,
            )

        def across(self, j, part):
            t = from_tp(j)
            return pltpu.make_async_remote_copy(
                src_ref=self.ref.at[t, part], dst_ref=self.ref.at[t, part],
                send_sem=self.sems.at[2, j], recv_sem=self.sems.at[3, j],
                device_id=mate, device_id_type=MESH,
            )

        def send(self):
            for j in ORDER:
                self.over(j, tp).start()

        def swap(self, j):
            self.over(j, from_tp(j)).wait_recv()
            self.across(j, self.mine).start()

        def ready(self, j):
            self.across(j, self.other).wait_recv()

        def drain(self):
            for j in ORDER:
                self.over(j, tp).wait_send()
                self.across(j, self.mine).wait_send()

    def columns_of(j):
        return pl.ds(pl.multiple_of(to_tp(j) * W, W), W)

    wq_all = Gather(lambda j, part: w_hbm.at[0, part], wq, wq_sems)
    wo_all = Gather(lambda j, part: wo_hbm.at[part, columns_of(j)], wo, wo_sems)
    km_all = Gather(lambda j, part: kmt.at[tp, part], kmt, km_sems)
    mt_all = Gather(lambda j, part: midt.at[tp, part], midt, mt_sems)

    def own_rows(i):
        x_load(i).wait()
        rows = rows_of(i)
        xc = x[rows, :]
        kp = dot(xc, wk[...])
        qp = dot(xc, wq[tp]) * LOG_SCALE
        k[rows, :] = kp.astype(bf16)
        q[tp, rows, :] = qp.astype(bf16)
        for s in range(C // SEG):
            at = i * (C // SEG) + s
            part = slice(s * SEG, (s + 1) * SEG)
            means[pl.ds(at, 1), :] = jnp.sum(qp[part], axis=0, keepdims=True) * (1.0 / SEG)
            means[pl.ds(8 + at, 1), :] = jnp.sum(kp[part], axis=0, keepdims=True) * (1.0 / SEG)

    def to_chips(src, dst, sems, j):
        return pltpu.make_async_remote_copy(
            src_ref=src, dst_ref=dst, send_sem=sems.at[0, j], recv_sem=sems.at[1, j],
            device_id=peer(j), device_id_type=MESH,
        )

    def to_mate(src, dst, n):
        return pltpu.make_async_remote_copy(
            src_ref=src, dst_ref=dst, send_sem=mate_sems.at[0, n], recv_sem=mate_sems.at[1, n],
            device_id=mate, device_id_type=MESH,
        )

    def chip_before(j):
        return lax.rem(chip + n_chips - j, n_chips)

    class Spread:
        def __init__(self, ref, sems, n):
            self.ref, self.sems, self.n = ref, sems, n

        def copy(self, j, place):
            return to_chips(self.ref.at[core, chip], self.ref.at[core, place], self.sems, j)

        def swap_copy(self, side):
            return to_mate(self.ref.at[side], self.ref.at[side], self.n)

        def send(self):
            @pl.loop(1, n_chips)
            def _(j):
                self.copy(j, chip).start()

        def swap(self):
            @pl.loop(1, n_chips)
            def _(j):
                self.copy(j, chip_before(j)).wait_recv()

            self.swap_copy(core).start()

        def ready(self):
            self.swap_copy(1 - core).wait_recv()

        def drain(self):
            @pl.loop(1, n_chips)
            def _(j):
                self.copy(j, chip).wait_send()

            self.swap_copy(core).wait_send()

    mk_all = Spread(mk_r, mk_sems, 0)
    mid_all = Spread(mid_r, mid_sems, 1)

    loads[0].wait()
    loads[1].wait()
    pl.loop(0, n_chunks)(own_rows)
    mk_r[core, chip] = means[...].astype(bf16)
    pl.semaphore_wait(barrier, n_chips + n_tp - 1)
    mk_all.send()
    wq_all.send()
    wo_all.send()

    loads[2].wait()
    ones = jnp.ones((C, 128), bf16)

    def own_values(i):
        rows = rows_of(i)
        vp = dot(x[rows, :], wv[...]).astype(bf16)
        for p in range(2):
            v[p, rows, 0:128] = pair_columns(vp, p)
            v[p, rows, 128:256] = ones

    pl.loop(0, n_chunks - 1)(own_values)
    mk_all.swap()
    own_values(n_chunks - 1)
    mk_all.ready()

    marks = mk_r[...].astype(f32).reshape(n_seq, 16, W)
    q_marks = marks[:, 0:8, :].reshape(MARKS, W)
    k_marks = marks[:, 8:16, :].reshape(MARKS, W)
    kmt[tp] = k_marks.astype(bf16)
    km_all.send()
    for h in range(4):
        qm[h] = one_head(pair_columns(q_marks, h // 2), h).astype(bf16)
        km[tp * 4 + h] = one_head(pair_columns(k_marks, h // 2), h).astype(bf16)

    sub = lax.broadcasted_iota(jnp.int32, (8, W), 0)
    for p in range(2):
        parts, levels = [], []
        for i in range(2):
            s = dot_nt(qm[2 * p + i], k[:, p * 128 : (p + 1) * 128])
            top = jnp.max(s, axis=1, keepdims=True)
            r = dot(jnp.exp2(s - top).astype(bf16), v[p])
            parts.append(r[:, :128] / r[:, 128:])
            levels.append((top + jnp.log2(r[:, 128:])).T[0:8, :])
        mean_values = jnp.where(low_lanes(MARKS), parts[0], parts[1]).T
        for i, level in enumerate(levels):
            lines = three_lines(level, sub)
            for b in range(8):
                part = mean_values[i * 64 + b * 8 : i * 64 + b * 8 + 8, :]
                at = (2 * p + i) * 8 + b
                lv_s[at // n_chips, at % n_chips] = jnp.concatenate([part, lines], 0).astype(bf16)

    lv_mate = to_mate(lv_s.at[1 - core], lv_t, 2)
    lv_mate.start()
    wq_all.swap(ORDER[0])
    for j in ORDER:
        km_all.swap(j)

    def lv_copy(j, place):
        return to_chips(lv_m.at[lax.rem(chip + j, n_chips)], lv_r.at[place], lv_sems, j)

    def values_and_level(blocks):
        blocks = blocks.astype(f32)
        return blocks[:, 0:8, :], blocks[:, 8:9, :] + blocks[:, 9:10, :] + blocks[:, 10:11, :]

    head = 2 * core + lax.div(chip, 8)
    terms = softmax_terms(dot_nt(qm[head], km[tp * 4 + head]))
    kernel_a = terms / jnp.sum(terms, axis=1, keepdims=True)
    col = jnp.max(jnp.sum(kernel_a, axis=0, keepdims=True), axis=1, keepdims=True)
    row = jnp.max(jnp.sum(kernel_a, axis=1, keepdims=True), axis=0, keepdims=True)
    a_ref[...] = kernel_a
    z_ref[...] = kernel_a.T / (col * row)
    wq_all.ready(ORDER[0])

    def unit(u):
        g = lax.div(u, 16)
        t = lax.rem(tp + 1 + 2 * g + lax.div(g, 2), n_tp)
        rows = pl.ds(pl.multiple_of(lax.rem(u, 16) * 256, 256), 256)
        q[t, rows, :] = (dot(x[rows, :], wq[t]) * LOG_SCALE).astype(bf16)

    def newton_turn(turn):
        eye = jnp.where(
            lax.broadcasted_iota(jnp.int32, (MARKS, MARKS), 0)
            == lax.broadcasted_iota(jnp.int32, (MARKS, MARKS), 1),
            1.0,
            0.0,
        )
        first = turn * UNITS
        z = z_ref[...]
        az = dot3(a_ref[...], z)
        unit(first)
        inner = dot3(az, 7.0 * eye - az)
        unit(first + 1)
        outer = dot3(az, 15.0 * eye - inner)
        unit(first + 2)
        z_ref[...] = 0.25 * dot3(z, 13.0 * eye - outer)
        unit(first + 3)

    newton_turn(0)
    lv_mate.wait_recv()
    (va, la), (vb, lb) = values_and_level(lv_s[core]), values_and_level(lv_t[...])
    top = jnp.maximum(la, lb)
    wa, wb = jnp.exp2(la - top), jnp.exp2(lb - top)
    level = jnp.broadcast_to(top + jnp.log2(wa + wb), va.shape)
    lines = three_lines(level, lax.broadcasted_iota(jnp.int32, va.shape, 1))
    lv_m[...] = jnp.concatenate([(va * wa + vb * wb) / (wa + wb), lines], 1).astype(bf16)

    @pl.loop(1, n_chips)
    def _(j):
        lv_copy(j, chip).start()

    lv_r[chip] = lv_m[chip]
    pl.loop(1, 3)(newton_turn)
    wq_all.swap(ORDER[1])
    newton_turn(3)
    wq_all.ready(ORDER[1])
    pl.loop(4, NEWTON)(newton_turn)
    wq_all.swap(ORDER[2])

    @pl.loop(1, n_chips)
    def _(j):
        lv_copy(j, chip_before(j)).wait_recv()

    values, level = values_and_level(lv_r[...])
    share = jnp.exp2(level - jnp.max(level, axis=0, keepdims=True))
    columns = jnp.sum(values * share, axis=0) / jnp.sum(share, axis=0)
    ch, cl = halves(columns)
    zh, zl = halves(z_ref[...])
    mid_r[core, chip] = dot_nt(
        jnp.concatenate([ch, cl, ch], 1), jnp.concatenate([zh, zh, zl], 1)
    )
    mid_all.send()

    @pl.loop(0, n_chunks)
    def _(i):
        rows = rows_of(i)
        for h in range(4):
            p = h // 2
            logits = dot_nt(q[tp, rows, p * 128 : (p + 1) * 128], km[tp * 4 + h])
            e_own[rows, h * MARKS : (h + 1) * MARKS] = softmax_terms(logits).astype(bf16)

    pl.loop(24, 32)(unit)
    wq_all.ready(ORDER[2])
    mid_all.swap()
    pl.loop(32, 40)(unit)
    for j in ORDER:
        wo_all.swap(j)
    for j in ORDER:
        t = from_tp(j)
        km_all.ready(j)
        others = kmt[t].astype(f32)
        for h in range(4):
            km[t * 4 + h] = one_head(pair_columns(others, h // 2), h).astype(bf16)
    mid_all.ready()

    def place_middle(t):
        m = midt[t].astype(f32)
        low = low_lanes(MARKS)
        for p in range(2):
            both = pair_columns(m, p)
            for i in range(2):
                mask = low if i == 0 else ~low
                midb[t * 2 + p, i * MARKS : (i + 1) * MARKS, :] = jnp.concatenate(
                    [jnp.where(mask, both, 0.0), jnp.where(mask, 1.0, 0.0)], 1
                ).astype(bf16)

    midt[tp] = mid_r[...].reshape(W, MARKS).T.astype(bf16)
    mt_all.send()
    place_middle(tp)

    def normalised(r):
        return (r[:, :128] * (1.0 / r[:, 128:])).astype(bf16)

    def own_attended(i):
        rows = rows_of(i)
        for p in range(2):
            r = dot(e_own[rows, p * 512 : (p + 1) * 512], midb[tp * 2 + p])
            q[tp, rows, p * 128 : (p + 1) * 128] = normalised(r)

    pl.loop(0, n_chunks - 1)(own_attended)
    pl.loop(40, 43)(unit)
    for j in ORDER:
        mt_all.swap(j)
    own_attended(n_chunks - 1)
    pl.loop(43, 48)(unit)
    loads[3].wait()
    for j in ORDER:
        wo_all.ready(j)
        mt_all.ready(j)
        place_middle(from_tp(j))
    groups = [from_tp(j) for j in ORDER]

    def out_copy(i):
        return pltpu.make_async_copy(outv.at[rows_of(i)], out_hbm.at[rows_of(i)], out_sem.at[i])

    @pl.loop(0, n_chunks)
    def _(i):
        rows = rows_of(i)
        parts = [q[tp, rows, :]]
        for t in groups:
            for p in range(2):
                qc = q[t, rows, p * 128 : (p + 1) * 128]
                e = [
                    softmax_terms(dot_nt(qc, km[t * 4 + 2 * p + b])).astype(bf16) for b in range(2)
                ]
                parts.append(normalised(dot(jnp.concatenate(e, 1), midb[t * 2 + p])))
        weights = jnp.concatenate([wo[t] for t in [tp] + groups], 0)
        outv[rows, :] = dot(jnp.concatenate(parts, 1), weights).astype(bf16)
        out_copy(i).start()

    @pl.loop(1, n_chips)
    def _(j):
        lv_copy(j, chip).wait_send()

    lv_mate.wait_send()
    for part in (mk_all, mid_all, wq_all, wo_all, km_all, mt_all):
        part.drain()
    for i in range(n_chunks):
        out_copy(i).wait()


def on_device(n_seq, n_tp, tokens, w_qkv, w_out):
    vmem = pltpu.VMEM
    sems = pltpu.SemaphoreType.DMA
    n_chips = n_seq // 2
    scratch = [
        vmem((T, D), bf16),
        vmem((D, W), bf16),
        vmem((D, W), bf16),
        vmem((n_tp, D, W), bf16),
        vmem((n_tp, W, W), bf16),
        vmem((n_tp, T, W), bf16),
        vmem((T, W), bf16),
        vmem((2, T, 256), bf16),
        vmem((16, W), f32),
        vmem((2, n_chips, 16, W), bf16),
        vmem((4, MARKS, 128), bf16),
        vmem((4 * n_tp, MARKS, 128), bf16),
        vmem((n_tp, MARKS, W), bf16),
        vmem((2, n_chips, 16, MARKS), bf16),
        vmem((n_chips, 16, MARKS), bf16),
        vmem((n_chips, 16, MARKS), bf16),
        vmem((n_chips, 16, MARKS), bf16),
        vmem((MARKS, MARKS), f32),
        vmem((MARKS, MARKS), f32),
        vmem((2, n_chips, 8, MARKS), f32),
        vmem((n_tp, MARKS, W), bf16),
        vmem((2 * n_tp, 2 * MARKS, 256), bf16),
        vmem((T, 4 * MARKS), bf16),
        vmem((T, W), bf16),
        sems((4,)), sems((T // C,)), sems((T // C,)),
        *[sems((2, n_chips))] * 3,
        sems((2, 3)),
        *[sems((4, n_tp))] * 4,
    ]
    hbm = pl.BlockSpec(memory_space=pl.ANY)
    return pl.pallas_call(
        functools.partial(kernel, n_seq, n_tp),
        out_shape=jax.ShapeDtypeStruct((T, W), bf16),
        in_specs=[hbm] * 3,
        out_specs=hbm,
        scratch_shapes=scratch,
        compiler_params=pltpu.CompilerParams(
            collective_id=0, has_side_effects=True, vmem_limit_bytes=60 * 2**20
        ),
    )(tokens, w_qkv, w_out)


def solution(mesh):
    return jax.shard_map(
        functools.partial(on_device, mesh.shape["seq"], mesh.shape["tp"]),
        mesh=mesh,
        in_specs=(P("seq", None), P(None, None, "tp"), P("tp", None)),
        out_specs=P("seq", "tp"),
        check_vma=False,
    )
```

```python
import functools
import math

import jax
import jax.numpy as jnp
from jax import lax
from jax.experimental import pallas as pl
from jax.experimental.pallas import tpu as pltpu
from jax.sharding import PartitionSpec as P

HEAD_DIM = 64
MARKS = 256
NEWTON = 6
UNITS = 4
D = 1024
W = 256
T = 4096
SEG = 512
C = 1024
LOG_SCALE = HEAD_DIM**-0.5 * math.log2(math.e)
bf16, f32 = jnp.bfloat16, jnp.float32
NT = (((1,), (1,)), ((), ()))
MESH = pl.DeviceIdType.MESH
ORDER = (3, 1, 2)


def dot(a, b):
    return jnp.dot(a, b, preferred_element_type=f32)


def dot_nt(a, b):
    return lax.dot_general(a, b, NT, preferred_element_type=f32)


def halves(a):
    hi = a.astype(bf16)
    return hi, (a - hi.astype(f32)).astype(bf16)


def dot3(a, b):
    ah, al = halves(a)
    bh, bl = halves(b)
    return dot(jnp.concatenate([ah, al, ah], 1), jnp.concatenate([bh, bh, bl], 0))


def low_lanes(rows):
    return lax.broadcasted_iota(jnp.int32, (rows, 128), 1) < 64


def one_head(block, head):
    low = low_lanes(block.shape[0])
    return jnp.where(low if head % 2 == 0 else ~low, block, 0.0)


def pair_columns(array, pair):
    return array[:, pair * 128 : (pair + 1) * 128]


def softmax_terms(logits):
    return jnp.exp2(logits - jnp.max(logits, axis=1, keepdims=True))


def three_lines(level, sub):
    first = level.astype(bf16).astype(f32)
    second = (level - first).astype(bf16).astype(f32)
    third = level - first - second
    return jnp.where(
        sub == 0, first, jnp.where(sub == 1, second, jnp.where(sub == 2, third, 0.0))
    )


def kernel(
    n_seq, n_tp,
    x_hbm, w_hbm, wo_hbm, out_hbm,
    x, wk, wv, wq, wo, q, k, v, means, mk_r, qm, km, kmt,
    lv_s, lv_t, lv_m, lv_r, a_ref, z_ref, mid_r, midt, midb, e_own, outv,
    load_sem, x_sem, out_sem,
    mk_sems, lv_sems, mid_sems, mate_sems,
    wq_sems, wo_sems, km_sems, mt_sems,
):
    seq, tp = lax.axis_index("seq"), lax.axis_index("tp")
    core, chip, n_chips = lax.rem(seq, 2), lax.div(seq, 2), n_seq // 2
    n_chunks = T // C

    def rows_of(i):
        return pl.ds(pl.multiple_of(i * C, C), C)

    def to_tp(j):
        return lax.rem(tp + j, n_tp)

    def from_tp(j):
        return lax.rem(tp + n_tp - j, n_tp)

    barrier = pltpu.get_barrier_semaphore()

    loads = [
        pltpu.make_async_copy(w_hbm.at[1], wk, load_sem.at[0]),
        pltpu.make_async_copy(w_hbm.at[0], wq.at[tp], load_sem.at[1]),
        pltpu.make_async_copy(w_hbm.at[2], wv, load_sem.at[2]),
        pltpu.make_async_copy(
            wo_hbm.at[:, pl.ds(pl.multiple_of(tp * W, W), W)], wo.at[tp], load_sem.at[3]
        ),
    ]

    def x_load(i):
        return pltpu.make_async_copy(x_hbm.at[rows_of(i)], x.at[rows_of(i)], x_sem.at[i])

    loads[0].start()
    loads[1].start()
    for i in range(n_chunks):
        x_load(i).start()
    loads[2].start()
    loads[3].start()

    def peer(j):
        return {"seq": 2 * lax.rem(chip + j, n_chips) + core}

    mate = {"seq": seq + 1 - 2 * core}

    def any_peer(j):
        return {"seq": lax.rem(seq + j, n_seq)}

    @pl.loop(1, n_seq)
    def _(j):
        pl.semaphore_signal(barrier, inc=1, device_id=any_peer(j), device_id_type=MESH)

    for j in range(1, n_tp):
        pl.semaphore_signal(
            barrier, inc=1, device_id={"tp": to_tp(j)}, device_id_type=MESH
        )

    class Gather:
        def __init__(self, source, ref, sems):
            half = ref.shape[1] // 2
            self.source, self.ref, self.sems = source, ref, sems
            self.mine = pl.ds(pl.multiple_of(core * half, half), half)
            self.other = pl.ds(pl.multiple_of((1 - core) * half, half), half)

        def over(self, j, slot):
            return pltpu.make_async_remote_copy(
                src_ref=self.source(j, self.mine), dst_ref=self.ref.at[slot, self.mine],
                send_sem=self.sems.at[0, j], recv_sem=self.sems.at[1, j],
                device_id={"tp": to_tp(j)}, device_id_type=MESH,
            )

        def across(self, j, part):
            t = from_tp(j)
            return pltpu.make_async_remote_copy(
                src_ref=self.ref.at[t, part], dst_ref=self.ref.at[t, part],
                send_sem=self.sems.at[2, j], recv_sem=self.sems.at[3, j],
                device_id=mate, device_id_type=MESH,
            )

        def send(self):
            for j in ORDER:
                self.over(j, tp).start()

        def swap(self, j):
            self.over(j, from_tp(j)).wait_recv()
            self.across(j, self.mine).start()

        def ready(self, j):
            self.across(j, self.other).wait_recv()

        def drain(self):
            for j in ORDER:
                self.over(j, tp).wait_send()
                self.across(j, self.mine).wait_send()

    def columns_of(j):
        return pl.ds(pl.multiple_of(to_tp(j) * W, W), W)

    wq_all = Gather(lambda j, part: w_hbm.at[0, part], wq, wq_sems)
    wo_all = Gather(lambda j, part: wo_hbm.at[part, columns_of(j)], wo, wo_sems)
    km_all = Gather(lambda j, part: kmt.at[tp, part], kmt, km_sems)
    mt_all = Gather(lambda j, part: midt.at[tp, part], midt, mt_sems)

    def own_rows(i):
        x_load(i).wait()
        rows = rows_of(i)
        xc = x[rows, :]
        kp = dot(xc, wk[...])
        qp = dot(xc, wq[tp]) * LOG_SCALE
        k[rows, :] = kp.astype(bf16)
        q[tp, rows, :] = qp.astype(bf16)
        for s in range(C // SEG):
            at = i * (C // SEG) + s
            part = slice(s * SEG, (s + 1) * SEG)
            means[pl.ds(at, 1), :] = jnp.sum(qp[part], axis=0, keepdims=True) * (1.0 / SEG)
            means[pl.ds(8 + at, 1), :] = jnp.sum(kp[part], axis=0, keepdims=True) * (1.0 / SEG)

    def to_chips(src, dst, sems, j):
        return pltpu.make_async_remote_copy(
            src_ref=src, dst_ref=dst, send_sem=sems.at[0, j], recv_sem=sems.at[1, j],
            device_id=peer(j), device_id_type=MESH,
        )

    def to_mate(src, dst):
        return pltpu.make_async_remote_copy(
            src_ref=src, dst_ref=dst, send_sem=mate_sems.at[0], recv_sem=mate_sems.at[1],
            device_id=mate, device_id_type=MESH,
        )

    def chip_before(j):
        return lax.rem(chip + n_chips - j, n_chips)

    class Spread:
        def __init__(self, ref, sems):
            self.ref, self.sems = ref, sems

        def copy(self, j, place):
            return pltpu.make_async_remote_copy(
                src_ref=self.ref.at[seq], dst_ref=self.ref.at[place],
                send_sem=self.sems.at[0, j], recv_sem=self.sems.at[1, j],
                device_id=any_peer(j), device_id_type=MESH,
            )

        def send(self):
            @pl.loop(1, n_seq)
            def _(j):
                self.copy(j, seq).start()

        def ready(self):
            @pl.loop(1, n_seq)
            def _(j):
                self.copy(j, lax.rem(seq + n_seq - j, n_seq)).wait_recv()

        def drain(self):
            @pl.loop(1, n_seq)
            def _(j):
                self.copy(j, seq).wait_send()

    mk_all = Spread(mk_r, mk_sems)
    mid_all = Spread(mid_r, mid_sems)

    loads[0].wait()
    loads[1].wait()
    pl.loop(0, n_chunks)(own_rows)
    mk_r[seq] = means[...].astype(bf16)
    pl.semaphore_wait(barrier, n_seq - 1 + n_tp - 1)
    mk_all.send()
    wq_all.send()

    loads[2].wait()
    ones = jnp.ones((C, 128), bf16)

    def own_values(i):
        rows = rows_of(i)
        vp = dot(x[rows, :], wv[...]).astype(bf16)
        for p in range(2):
            v[p, rows, 0:128] = pair_columns(vp, p)
            v[p, rows, 128:256] = ones

    pl.loop(0, n_chunks)(own_values)
    mk_all.ready()
    marks = mk_r[...].astype(f32)
    q_marks = marks[:, 0:8, :].reshape(MARKS, W)
    k_marks = marks[:, 8:16, :].reshape(MARKS, W)
    kmt[tp] = k_marks.astype(bf16)
    km_all.send()
    wo_all.send()
    for h in range(4):
        qm[h] = one_head(pair_columns(q_marks, h // 2), h).astype(bf16)
        km[tp * 4 + h] = one_head(pair_columns(k_marks, h // 2), h).astype(bf16)

    sub = lax.broadcasted_iota(jnp.int32, (8, W), 0)
    for p in range(2):
        parts, levels = [], []
        for i in range(2):
            s = dot_nt(qm[2 * p + i], k[:, p * 128 : (p + 1) * 128])
            top = jnp.max(s, axis=1, keepdims=True)
            r = dot(jnp.exp2(s - top).astype(bf16), v[p])
            parts.append(r[:, :128] / r[:, 128:])
            levels.append((top + jnp.log2(r[:, 128:])).T[0:8, :])
        mean_values = jnp.where(low_lanes(MARKS), parts[0], parts[1]).T
        for i, level in enumerate(levels):
            lines = three_lines(level, sub)
            for b in range(8):
                part = mean_values[i * 64 + b * 8 : i * 64 + b * 8 + 8, :]
                at = (2 * p + i) * 8 + b
                lv_s[at // n_chips, at % n_chips] = jnp.concatenate([part, lines], 0).astype(bf16)

    lv_mate = to_mate(lv_s.at[1 - core], lv_t)
    lv_mate.start()
    wq_all.swap(ORDER[0])

    def lv_copy(j, place):
        return to_chips(lv_m.at[lax.rem(chip + j, n_chips)], lv_r.at[place], lv_sems, j)

    def values_and_level(blocks):
        blocks = blocks.astype(f32)
        return blocks[:, 0:8, :], blocks[:, 8:9, :] + blocks[:, 9:10, :] + blocks[:, 10:11, :]

    head = 2 * core + lax.div(chip, 8)
    terms = softmax_terms(dot_nt(qm[head], km[tp * 4 + head]))
    kernel_a = terms / jnp.sum(terms, axis=1, keepdims=True)
    col = jnp.max(jnp.sum(kernel_a, axis=0, keepdims=True), axis=1, keepdims=True)
    row = jnp.max(jnp.sum(kernel_a, axis=1, keepdims=True), axis=0, keepdims=True)
    a_ref[...] = kernel_a
    z_ref[...] = kernel_a.T / (col * row)
    wq_all.ready(ORDER[0])

    def unit(u):
        g = lax.div(u, 16)
        t = lax.rem(tp + 1 + 2 * g + lax.div(g, 2), n_tp)
        rows = pl.ds(pl.multiple_of(lax.rem(u, 16) * 256, 256), 256)
        q[t, rows, :] = (dot(x[rows, :], wq[t]) * LOG_SCALE).astype(bf16)

    def newton_turn(turn):
        eye = jnp.where(
            lax.broadcasted_iota(jnp.int32, (MARKS, MARKS), 0)
            == lax.broadcasted_iota(jnp.int32, (MARKS, MARKS), 1),
            1.0,
            0.0,
        )
        first = turn * UNITS
        z = z_ref[...]
        az = dot3(a_ref[...], z)
        unit(first)
        inner = dot3(az, 7.0 * eye - az)
        unit(first + 1)
        outer = dot3(az, 15.0 * eye - inner)
        unit(first + 2)
        z_ref[...] = 0.25 * dot3(z, 13.0 * eye - outer)
        unit(first + 3)

    newton_turn(0)
    lv_mate.wait_recv()
    (va, la), (vb, lb) = values_and_level(lv_s[core]), values_and_level(lv_t[...])
    top = jnp.maximum(la, lb)
    wa, wb = jnp.exp2(la - top), jnp.exp2(lb - top)
    level = jnp.broadcast_to(top + jnp.log2(wa + wb), va.shape)
    lines = three_lines(level, lax.broadcasted_iota(jnp.int32, va.shape, 1))
    lv_m[...] = jnp.concatenate([(va * wa + vb * wb) / (wa + wb), lines], 1).astype(bf16)

    @pl.loop(1, n_chips)
    def _(j):
        lv_copy(j, chip).start()

    lv_r[chip] = lv_m[chip]
    pl.loop(1, 3)(newton_turn)
    wq_all.swap(ORDER[1])
    newton_turn(3)
    wq_all.ready(ORDER[1])
    pl.loop(4, NEWTON)(newton_turn)
    wq_all.swap(ORDER[2])

    @pl.loop(1, n_chips)
    def _(j):
        lv_copy(j, chip_before(j)).wait_recv()

    values, level = values_and_level(lv_r[...])
    share = jnp.exp2(level - jnp.max(level, axis=0, keepdims=True))
    columns = jnp.sum(values * share, axis=0) / jnp.sum(share, axis=0)
    ch, cl = halves(columns)
    zh, zl = halves(z_ref[...])
    mid_r[seq] = dot_nt(jnp.concatenate([ch, cl, ch], 1), jnp.concatenate([zh, zh, zl], 1))
    mid_all.send()

    @pl.loop(0, n_chunks)
    def _(i):
        rows = rows_of(i)
        for h in range(4):
            p = h // 2
            logits = dot_nt(q[tp, rows, p * 128 : (p + 1) * 128], km[tp * 4 + h])
            e_own[rows, h * MARKS : (h + 1) * MARKS] = softmax_terms(logits).astype(bf16)

    wq_all.ready(ORDER[2])
    pl.loop(24, 40)(unit)
    for j in ORDER:
        km_all.swap(j)
    for j in ORDER:
        wo_all.swap(j)
    mid_all.ready()

    def place_middle(t):
        m = midt[t].astype(f32)
        low = low_lanes(MARKS)
        for p in range(2):
            both = pair_columns(m, p)
            for i in range(2):
                mask = low if i == 0 else ~low
                midb[t * 2 + p, i * MARKS : (i + 1) * MARKS, :] = jnp.concatenate(
                    [jnp.where(mask, both, 0.0), jnp.where(mask, 1.0, 0.0)], 1
                ).astype(bf16)

    pieces = [mid_r[2 * (n % n_chips) + n // n_chips] for n in range(n_seq)]
    midt[tp] = jnp.concatenate(pieces, 0).T.astype(bf16)
    mt_all.send()
    place_middle(tp)

    def normalised(r):
        return (r[:, :128] * (1.0 / r[:, 128:])).astype(bf16)

    def own_attended(i):
        rows = rows_of(i)
        for p in range(2):
            r = dot(e_own[rows, p * 512 : (p + 1) * 512], midb[tp * 2 + p])
            q[tp, rows, p * 128 : (p + 1) * 128] = normalised(r)

    pl.loop(0, n_chunks - 1)(own_attended)
    pl.loop(40, 43)(unit)
    for j in ORDER:
        mt_all.swap(j)
    own_attended(n_chunks - 1)
    pl.loop(43, 48)(unit)
    for j in ORDER:
        t = from_tp(j)
        km_all.ready(j)
        others = kmt[t].astype(f32)
        for h in range(4):
            km[t * 4 + h] = one_head(pair_columns(others, h // 2), h).astype(bf16)
    loads[3].wait()
    for j in ORDER:
        wo_all.ready(j)
        mt_all.ready(j)
        place_middle(from_tp(j))
    groups = [from_tp(j) for j in ORDER]

    def out_copy(i):
        return pltpu.make_async_copy(outv.at[rows_of(i)], out_hbm.at[rows_of(i)], out_sem.at[i])

    @pl.loop(0, n_chunks)
    def _(i):
        rows = rows_of(i)
        parts = [q[tp, rows, :]]
        for t in groups:
            for p in range(2):
                qc = q[t, rows, p * 128 : (p + 1) * 128]
                e = [
                    softmax_terms(dot_nt(qc, km[t * 4 + 2 * p + b])).astype(bf16) for b in range(2)
                ]
                parts.append(normalised(dot(jnp.concatenate(e, 1), midb[t * 2 + p])))
        weights = jnp.concatenate([wo[t] for t in [tp] + groups], 0)
        outv[rows, :] = dot(jnp.concatenate(parts, 1), weights).astype(bf16)
        out_copy(i).start()

    @pl.loop(1, n_chips)
    def _(j):
        lv_copy(j, chip).wait_send()

    lv_mate.wait_send()
    for part in (mk_all, mid_all, wq_all, wo_all, km_all, mt_all):
        part.drain()
    for i in range(n_chunks):
        out_copy(i).wait()


def on_device(n_seq, n_tp, tokens, w_qkv, w_out):
    vmem = pltpu.VMEM
    sems = pltpu.SemaphoreType.DMA
    n_chips = n_seq // 2
    scratch = [
        vmem((T, D), bf16),
        vmem((D, W), bf16),
        vmem((D, W), bf16),
        vmem((n_tp, D, W), bf16),
        vmem((n_tp, W, W), bf16),
        vmem((n_tp, T, W), bf16),
        vmem((T, W), bf16),
        vmem((2, T, 256), bf16),
        vmem((16, W), f32),
        vmem((n_seq, 16, W), bf16),
        vmem((4, MARKS, 128), bf16),
        vmem((4 * n_tp, MARKS, 128), bf16),
        vmem((n_tp, MARKS, W), bf16),
        vmem((2, n_chips, 16, MARKS), bf16),
        vmem((n_chips, 16, MARKS), bf16),
        vmem((n_chips, 16, MARKS), bf16),
        vmem((n_chips, 16, MARKS), bf16),
        vmem((MARKS, MARKS), f32),
        vmem((MARKS, MARKS), f32),
        vmem((n_seq, 8, MARKS), f32),
        vmem((n_tp, MARKS, W), bf16),
        vmem((2 * n_tp, 2 * MARKS, 256), bf16),
        vmem((T, 4 * MARKS), bf16),
        vmem((T, W), bf16),
        sems((4,)), sems((T // C,)), sems((T // C,)),
        sems((2, n_seq)), sems((2, n_chips)), sems((2, n_seq)),
        sems((2,)),
        *[sems((4, n_tp))] * 4,
    ]
    hbm = pl.BlockSpec(memory_space=pl.ANY)
    return pl.pallas_call(
        functools.partial(kernel, n_seq, n_tp),
        out_shape=jax.ShapeDtypeStruct((T, W), bf16),
        in_specs=[hbm] * 3,
        out_specs=hbm,
        scratch_shapes=scratch,
        compiler_params=pltpu.CompilerParams(
            collective_id=0, has_side_effects=True, vmem_limit_bytes=60 * 2**20
        ),
    )(tokens, w_qkv, w_out)


def solution(mesh):
    return jax.shard_map(
        functools.partial(on_device, mesh.shape["seq"], mesh.shape["tp"]),
        mesh=mesh,
        in_specs=(P("seq", None), P(None, None, "tp"), P("tp", None)),
        out_specs=P("seq", "tp"),
        check_vma=False,
    )
```

```python
import functools
import math

import jax
import jax.numpy as jnp
from jax import lax
from jax.experimental import pallas as pl
from jax.experimental.pallas import tpu as pltpu
from jax.sharding import PartitionSpec as P

HEAD_DIM = 64
MARKS = 256
NEWTON = 6
UNITS = 4
D = 1024
W = 256
T = 4096
SEG = 512
C = 1024
LOG_SCALE = HEAD_DIM**-0.5 * math.log2(math.e)
bf16, f32 = jnp.bfloat16, jnp.float32
NT = (((1,), (1,)), ((), ()))
MESH = pl.DeviceIdType.MESH
ORDER = (3, 1, 2)


def dot(a, b):
    return jnp.dot(a, b, preferred_element_type=f32)


def dot_nt(a, b):
    return lax.dot_general(a, b, NT, preferred_element_type=f32)


def halves(a):
    hi = a.astype(bf16)
    return hi, (a - hi.astype(f32)).astype(bf16)


def dot3(a, b):
    ah, al = halves(a)
    bh, bl = halves(b)
    return dot(jnp.concatenate([ah, al, ah], 1), jnp.concatenate([bh, bh, bl], 0))


def low_lanes(rows):
    return lax.broadcasted_iota(jnp.int32, (rows, 128), 1) < 64


def one_head(block, head):
    low = low_lanes(block.shape[0])
    return jnp.where(low if head % 2 == 0 else ~low, block, 0.0)


def pair_columns(array, pair):
    return array[:, pair * 128 : (pair + 1) * 128]


def softmax_terms(logits):
    return jnp.exp2(logits - jnp.max(logits, axis=1, keepdims=True))


def three_lines(level, sub):
    first = level.astype(bf16).astype(f32)
    second = (level - first).astype(bf16).astype(f32)
    third = level - first - second
    return jnp.where(
        sub == 0, first, jnp.where(sub == 1, second, jnp.where(sub == 2, third, 0.0))
    )


def kernel(
    n_seq, n_tp,
    x_hbm, w_hbm, wo_hbm, out_hbm,
    x, wk, wv, wq, wo, q, k, v, means, mk_r, qm, km, kmt,
    lv_s, lv_t, lv_m, lv_r, a_ref, z_ref, mid_r, midt, midb, e_own, outv,
    load_sem, x_sem, out_sem,
    mk_sems, lv_sems, mid_sems, mate_sems,
    wq_sems, wo_sems, km_sems, mt_sems,
):
    seq, tp = lax.axis_index("seq"), lax.axis_index("tp")
    core, chip, n_chips = lax.rem(seq, 2), lax.div(seq, 2), n_seq // 2
    n_chunks = T // C

    def rows_of(i):
        return pl.ds(pl.multiple_of(i * C, C), C)

    def to_tp(j):
        return lax.rem(tp + j, n_tp)

    def from_tp(j):
        return lax.rem(tp + n_tp - j, n_tp)

    barrier = pltpu.get_barrier_semaphore()

    loads = [
        pltpu.make_async_copy(w_hbm.at[1], wk, load_sem.at[0]),
        pltpu.make_async_copy(w_hbm.at[0], wq.at[tp], load_sem.at[1]),
        pltpu.make_async_copy(w_hbm.at[2], wv, load_sem.at[2]),
        pltpu.make_async_copy(
            wo_hbm.at[:, pl.ds(pl.multiple_of(tp * W, W), W)], wo.at[tp], load_sem.at[3]
        ),
    ]

    def x_load(i):
        return pltpu.make_async_copy(x_hbm.at[rows_of(i)], x.at[rows_of(i)], x_sem.at[i])

    loads[0].start()
    loads[1].start()
    for i in range(n_chunks):
        x_load(i).start()
    loads[2].start()
    loads[3].start()

    def peer(j):
        return {"seq": 2 * lax.rem(chip + j, n_chips) + core}

    mate = {"seq": seq + 1 - 2 * core}

    def any_peer(j):
        return {"seq": lax.rem(seq + j, n_seq)}

    @pl.loop(1, n_seq)
    def _(j):
        pl.semaphore_signal(barrier, inc=1, device_id=any_peer(j), device_id_type=MESH)

    for j in range(1, n_tp):
        pl.semaphore_signal(
            barrier, inc=1, device_id={"tp": to_tp(j)}, device_id_type=MESH
        )

    class Gather:
        def __init__(self, source, ref, sems):
            half = ref.shape[1] // 2
            self.source, self.ref, self.sems = source, ref, sems
            self.mine = pl.ds(pl.multiple_of(core * half, half), half)
            self.other = pl.ds(pl.multiple_of((1 - core) * half, half), half)

        def over(self, j, slot):
            return pltpu.make_async_remote_copy(
                src_ref=self.source(j, self.mine), dst_ref=self.ref.at[slot, self.mine],
                send_sem=self.sems.at[0, j], recv_sem=self.sems.at[1, j],
                device_id={"tp": to_tp(j)}, device_id_type=MESH,
            )

        def across(self, j, part):
            t = from_tp(j)
            return pltpu.make_async_remote_copy(
                src_ref=self.ref.at[t, part], dst_ref=self.ref.at[t, part],
                send_sem=self.sems.at[2, j], recv_sem=self.sems.at[3, j],
                device_id=mate, device_id_type=MESH,
            )

        def send(self):
            for j in ORDER:
                self.over(j, tp).start()

        def swap(self, j):
            self.over(j, from_tp(j)).wait_recv()
            self.across(j, self.mine).start()

        def ready(self, j):
            self.across(j, self.other).wait_recv()

        def drain(self):
            for j in ORDER:
                self.over(j, tp).wait_send()
                self.across(j, self.mine).wait_send()

    def columns_of(j):
        return pl.ds(pl.multiple_of(to_tp(j) * W, W), W)

    wq_all = Gather(lambda j, part: w_hbm.at[0, part], wq, wq_sems)
    wo_all = Gather(lambda j, part: wo_hbm.at[part, columns_of(j)], wo, wo_sems)
    km_all = Gather(lambda j, part: kmt.at[tp, part], kmt, km_sems)
    mt_all = Gather(lambda j, part: midt.at[tp, part], midt, mt_sems)

    def own_rows(i):
        x_load(i).wait()
        rows = rows_of(i)
        xc = x[rows, :]
        kp = dot(xc, wk[...])
        qp = dot(xc, wq[tp]) * LOG_SCALE
        k[rows, :] = kp.astype(bf16)
        q[tp, rows, :] = qp.astype(bf16)
        for s in range(C // SEG):
            at = i * (C // SEG) + s
            part = slice(s * SEG, (s + 1) * SEG)
            means[pl.ds(at, 1), :] = jnp.sum(qp[part], axis=0, keepdims=True) * (1.0 / SEG)
            means[pl.ds(8 + at, 1), :] = jnp.sum(kp[part], axis=0, keepdims=True) * (1.0 / SEG)

    def to_chips(src, dst, sems, j):
        return pltpu.make_async_remote_copy(
            src_ref=src, dst_ref=dst, send_sem=sems.at[0, j], recv_sem=sems.at[1, j],
            device_id=peer(j), device_id_type=MESH,
        )

    def to_mate(src, dst):
        return pltpu.make_async_remote_copy(
            src_ref=src, dst_ref=dst, send_sem=mate_sems.at[0], recv_sem=mate_sems.at[1],
            device_id=mate, device_id_type=MESH,
        )

    def chip_before(j):
        return lax.rem(chip + n_chips - j, n_chips)

    class Spread:
        def __init__(self, ref, sems):
            self.ref, self.sems = ref, sems

        def copy(self, j, place):
            return pltpu.make_async_remote_copy(
                src_ref=self.ref.at[seq], dst_ref=self.ref.at[place],
                send_sem=self.sems.at[0, j], recv_sem=self.sems.at[1, j],
                device_id=any_peer(j), device_id_type=MESH,
            )

        def send(self):
            @pl.loop(1, n_seq)
            def _(j):
                self.copy(j, seq).start()

        def ready(self):
            @pl.loop(1, n_seq)
            def _(j):
                self.copy(j, lax.rem(seq + n_seq - j, n_seq)).wait_recv()

        def drain(self):
            @pl.loop(1, n_seq)
            def _(j):
                self.copy(j, seq).wait_send()

    mk_all = Spread(mk_r, mk_sems)
    mid_all = Spread(mid_r, mid_sems)

    loads[0].wait()
    loads[1].wait()
    pl.loop(0, n_chunks)(own_rows)
    mk_r[seq] = means[...].astype(bf16)
    pl.semaphore_wait(barrier, n_seq - 1 + n_tp - 1)
    mk_all.send()
    wq_all.send()

    loads[2].wait()
    ones = jnp.ones((C, 128), bf16)

    def own_values(i):
        rows = rows_of(i)
        vp = dot(x[rows, :], wv[...]).astype(bf16)
        for p in range(2):
            v[p, rows, 0:128] = pair_columns(vp, p)
            v[p, rows, 128:256] = ones

    pl.loop(0, n_chunks)(own_values)
    mk_all.ready()
    marks = mk_r[...].astype(f32)
    q_marks = marks[:, 0:8, :].reshape(MARKS, W)
    k_marks = marks[:, 8:16, :].reshape(MARKS, W)
    kmt[tp] = k_marks.astype(bf16)
    km_all.send()
    wo_all.send()
    for h in range(4):
        qm[h] = one_head(pair_columns(q_marks, h // 2), h).astype(bf16)
        km[tp * 4 + h] = one_head(pair_columns(k_marks, h // 2), h).astype(bf16)

    sub = lax.broadcasted_iota(jnp.int32, (8, W), 0)
    for p in range(2):
        parts, levels = [], []
        for i in range(2):
            s = dot_nt(qm[2 * p + i], k[:, p * 128 : (p + 1) * 128])
            top = jnp.max(s, axis=1, keepdims=True)
            r = dot(jnp.exp2(s - top).astype(bf16), v[p])
            parts.append(r[:, :128] / r[:, 128:])
            levels.append((top + jnp.log2(r[:, 128:])).T[0:8, :])
        mean_values = jnp.where(low_lanes(MARKS), parts[0], parts[1]).T
        for i, level in enumerate(levels):
            lines = three_lines(level, sub)
            for b in range(8):
                part = mean_values[i * 64 + b * 8 : i * 64 + b * 8 + 8, :]
                at = (2 * p + i) * 8 + b
                lv_s[at // n_chips, at % n_chips] = jnp.concatenate([part, lines], 0).astype(bf16)

    lv_mate = to_mate(lv_s.at[1 - core], lv_t)
    lv_mate.start()
    wq_all.swap(ORDER[0])

    def lv_copy(j, place):
        return to_chips(lv_m.at[lax.rem(chip + j, n_chips)], lv_r.at[place], lv_sems, j)

    def values_and_level(blocks):
        blocks = blocks.astype(f32)
        return blocks[:, 0:8, :], blocks[:, 8:9, :] + blocks[:, 9:10, :] + blocks[:, 10:11, :]

    head = 2 * core + lax.div(chip, 8)
    terms = softmax_terms(dot_nt(qm[head], km[tp * 4 + head]))
    kernel_a = terms / jnp.sum(terms, axis=1, keepdims=True)
    col = jnp.max(jnp.sum(kernel_a, axis=0, keepdims=True), axis=1, keepdims=True)
    row = jnp.max(jnp.sum(kernel_a, axis=1, keepdims=True), axis=0, keepdims=True)
    a_ref[...] = kernel_a
    z_ref[...] = kernel_a.T / (col * row)
    wq_all.ready(ORDER[0])

    def unit(u):
        g = lax.div(u, 16)
        t = lax.rem(tp + 1 + 2 * g + lax.div(g, 2), n_tp)
        rows = pl.ds(pl.multiple_of(lax.rem(u, 16) * 256, 256), 256)
        q[t, rows, :] = (dot(x[rows, :], wq[t]) * LOG_SCALE).astype(bf16)

    def newton_turn(turn):
        eye = jnp.where(
            lax.broadcasted_iota(jnp.int32, (MARKS, MARKS), 0)
            == lax.broadcasted_iota(jnp.int32, (MARKS, MARKS), 1),
            1.0,
            0.0,
        )
        first = turn * UNITS
        z = z_ref[...]
        az = dot3(a_ref[...], z)
        unit(first)
        inner = dot3(az, 7.0 * eye - az)
        unit(first + 1)
        outer = dot3(az, 15.0 * eye - inner)
        unit(first + 2)
        z_ref[...] = 0.25 * dot3(z, 13.0 * eye - outer)
        unit(first + 3)

    newton_turn(0)
    lv_mate.wait_recv()
    (va, la), (vb, lb) = values_and_level(lv_s[core]), values_and_level(lv_t[...])
    top = jnp.maximum(la, lb)
    wa, wb = jnp.exp2(la - top), jnp.exp2(lb - top)
    level = jnp.broadcast_to(top + jnp.log2(wa + wb), va.shape)
    lines = three_lines(level, lax.broadcasted_iota(jnp.int32, va.shape, 1))
    lv_m[...] = jnp.concatenate([(va * wa + vb * wb) / (wa + wb), lines], 1).astype(bf16)

    @pl.loop(1, n_chips)
    def _(j):
        lv_copy(j, chip).start()

    lv_r[chip] = lv_m[chip]
    pl.loop(1, 3)(newton_turn)
    wq_all.swap(ORDER[1])
    newton_turn(3)
    wq_all.ready(ORDER[1])
    pl.loop(4, NEWTON)(newton_turn)
    wq_all.swap(ORDER[2])

    @pl.loop(1, n_chips)
    def _(j):
        lv_copy(j, chip_before(j)).wait_recv()

    values, level = values_and_level(lv_r[...])
    share = jnp.exp2(level - jnp.max(level, axis=0, keepdims=True))
    columns = jnp.sum(values * share, axis=0) / jnp.sum(share, axis=0)
    ch, cl = halves(columns)
    zh, zl = halves(z_ref[...])
    mid_r[seq] = dot_nt(jnp.concatenate([ch, cl, ch], 1), jnp.concatenate([zh, zh, zl], 1))
    mid_all.send()

    @pl.loop(0, n_chunks)
    def _(i):
        rows = rows_of(i)
        for h in range(4):
            p = h // 2
            logits = dot_nt(q[tp, rows, p * 128 : (p + 1) * 128], km[tp * 4 + h])
            e_own[rows, h * MARKS : (h + 1) * MARKS] = softmax_terms(logits).astype(bf16)

    wq_all.ready(ORDER[2])
    pl.loop(24, 40)(unit)
    for j in ORDER:
        km_all.swap(j)
    for j in ORDER:
        wo_all.swap(j)
    mid_all.ready()

    def place_middle(t):
        m = midt[t].astype(f32)
        low = low_lanes(MARKS)
        for p in range(2):
            both = pair_columns(m, p)
            for i in range(2):
                mask = low if i == 0 else ~low
                midb[t * 2 + p, i * MARKS : (i + 1) * MARKS, :] = jnp.concatenate(
                    [jnp.where(mask, both, 0.0), jnp.where(mask, 1.0, 0.0)], 1
                ).astype(bf16)

    pieces = [mid_r[2 * (n % n_chips) + n // n_chips] for n in range(n_seq)]
    midt[tp] = jnp.concatenate(pieces, 0).T.astype(bf16)
    mt_all.send()
    place_middle(tp)

    def normalised(r):
        return (r[:, :128] * (1.0 / r[:, 128:])).astype(bf16)

    def own_attended(i):
        rows = rows_of(i)
        for p in range(2):
            r = dot(e_own[rows, p * 512 : (p + 1) * 512], midb[tp * 2 + p])
            q[tp, rows, p * 128 : (p + 1) * 128] = normalised(r)

    def attended_of(t, rows):
        parts = []
        for p in range(2):
            qc = q[t, rows, p * 128 : (p + 1) * 128]
            e = [softmax_terms(dot_nt(qc, km[t * 4 + 2 * p + b])).astype(bf16) for b in range(2)]
            parts.append(normalised(dot(jnp.concatenate(e, 1), midb[t * 2 + p])))
        return parts

    def place_group(j):
        t = from_tp(j)
        km_all.ready(j)
        others = kmt[t].astype(f32)
        for h in range(4):
            km[t * 4 + h] = one_head(pair_columns(others, h // 2), h).astype(bf16)
        mt_all.ready(j)
        place_middle(t)

    groups = [from_tp(j) for j in ORDER]

    def first_group(i):
        rows = rows_of(i)
        q[groups[0], rows, :] = jnp.concatenate(attended_of(groups[0], rows), 1)

    pl.loop(0, n_chunks - 1)(own_attended)
    pl.loop(40, 43)(unit)
    mt_all.swap(ORDER[0])
    own_attended(n_chunks - 1)
    pl.loop(43, 48)(unit)
    place_group(ORDER[0])
    pl.loop(0, n_chunks // 2)(first_group)
    for j in ORDER[1:]:
        mt_all.swap(j)
    pl.loop(n_chunks // 2, n_chunks)(first_group)
    for j in ORDER[1:]:
        place_group(j)
    loads[3].wait()
    for j in ORDER:
        wo_all.ready(j)

    def out_copy(i):
        return pltpu.make_async_copy(outv.at[rows_of(i)], out_hbm.at[rows_of(i)], out_sem.at[i])

    @pl.loop(0, n_chunks)
    def _(i):
        rows = rows_of(i)
        parts = [q[tp, rows, :], q[groups[0], rows, :]]
        for t in groups[1:]:
            parts += attended_of(t, rows)
        weights = jnp.concatenate([wo[t] for t in [tp] + groups], 0)
        outv[rows, :] = dot(jnp.concatenate(parts, 1), weights).astype(bf16)
        out_copy(i).start()

    @pl.loop(1, n_chips)
    def _(j):
        lv_copy(j, chip).wait_send()

    lv_mate.wait_send()
    for part in (mk_all, mid_all, wq_all, wo_all, km_all, mt_all):
        part.drain()
    for i in range(n_chunks):
        out_copy(i).wait()


def on_device(n_seq, n_tp, tokens, w_qkv, w_out):
    vmem = pltpu.VMEM
    sems = pltpu.SemaphoreType.DMA
    n_chips = n_seq // 2
    scratch = [
        vmem((T, D), bf16),
        vmem((D, W), bf16),
        vmem((D, W), bf16),
        vmem((n_tp, D, W), bf16),
        vmem((n_tp, W, W), bf16),
        vmem((n_tp, T, W), bf16),
        vmem((T, W), bf16),
        vmem((2, T, 256), bf16),
        vmem((16, W), f32),
        vmem((n_seq, 16, W), bf16),
        vmem((4, MARKS, 128), bf16),
        vmem((4 * n_tp, MARKS, 128), bf16),
        vmem((n_tp, MARKS, W), bf16),
        vmem((2, n_chips, 16, MARKS), bf16),
        vmem((n_chips, 16, MARKS), bf16),
        vmem((n_chips, 16, MARKS), bf16),
        vmem((n_chips, 16, MARKS), bf16),
        vmem((MARKS, MARKS), f32),
        vmem((MARKS, MARKS), f32),
        vmem((n_seq, 8, MARKS), f32),
        vmem((n_tp, MARKS, W), bf16),
        vmem((2 * n_tp, 2 * MARKS, 256), bf16),
        vmem((T, 4 * MARKS), bf16),
        vmem((T, W), bf16),
        sems((4,)), sems((T // C,)), sems((T // C,)),
        sems((2, n_seq)), sems((2, n_chips)), sems((2, n_seq)),
        sems((2,)),
        *[sems((4, n_tp))] * 4,
    ]
    hbm = pl.BlockSpec(memory_space=pl.ANY)
    return pl.pallas_call(
        functools.partial(kernel, n_seq, n_tp),
        out_shape=jax.ShapeDtypeStruct((T, W), bf16),
        in_specs=[hbm] * 3,
        out_specs=hbm,
        scratch_shapes=scratch,
        compiler_params=pltpu.CompilerParams(
            collective_id=0, has_side_effects=True, vmem_limit_bytes=60 * 2**20
        ),
    )(tokens, w_qkv, w_out)


def solution(mesh):
    return jax.shard_map(
        functools.partial(on_device, mesh.shape["seq"], mesh.shape["tp"]),
        mesh=mesh,
        in_specs=(P("seq", None), P(None, None, "tp"), P("tp", None)),
        out_specs=P("seq", "tp"),
        check_vma=False,
    )
```

```python
import functools
import math

import jax
import jax.numpy as jnp
from jax import lax
from jax.experimental import pallas as pl
from jax.experimental.pallas import tpu as pltpu
from jax.sharding import PartitionSpec as P

HEAD_DIM = 64
MARKS = 256
NEWTON = 6
UNITS = 4
D = 1024
W = 256
T = 4096
SEG = 512
C = 1024
SHARE = 256
PER_GROUP = 1 + (T - C) // 256
LOG_SCALE = HEAD_DIM**-0.5 * math.log2(math.e)
bf16, f32 = jnp.bfloat16, jnp.float32
NT = (((1,), (1,)), ((), ()))
MESH = pl.DeviceIdType.MESH
ORDER = (3, 1, 2)


def dot(a, b):
    return jnp.dot(a, b, preferred_element_type=f32)


def dot_nt(a, b):
    return lax.dot_general(a, b, NT, preferred_element_type=f32)


def halves(a):
    hi = a.astype(bf16)
    return hi, (a - hi.astype(f32)).astype(bf16)


def dot3(a, b):
    ah, al = halves(a)
    bh, bl = halves(b)
    return dot(jnp.concatenate([ah, al, ah], 1), jnp.concatenate([bh, bh, bl], 0))


def low_lanes(rows):
    return lax.broadcasted_iota(jnp.int32, (rows, 128), 1) < 64


def one_head(block, head):
    low = low_lanes(block.shape[0])
    return jnp.where(low if head % 2 == 0 else ~low, block, 0.0)


def pair_columns(array, pair):
    return array[:, pair * 128 : (pair + 1) * 128]


def softmax_terms(logits):
    return jnp.exp2(logits - jnp.max(logits, axis=1, keepdims=True))


def three_lines(level, sub):
    first = level.astype(bf16).astype(f32)
    second = (level - first).astype(bf16).astype(f32)
    third = level - first - second
    return jnp.where(
        sub == 0, first, jnp.where(sub == 1, second, jnp.where(sub == 2, third, 0.0))
    )


def kernel(
    n_seq, n_tp,
    x_hbm, w_hbm, wo_hbm, out_hbm,
    x, wk, wv, wq, wo, q, k, v, means, mk_r, qm, km, kmt,
    lv_s, lv_t, lv_m, lv_r, a_ref, z_ref, mid_r, midt, midb, e_own, outv, sent,
    load_sem, x_sem, out_sem,
    mk_sems, lv_sems, mid_sems, mate_sems,
    wq_sems, wo_sems, km_sems, mt_sems, share_sems,
):
    seq, tp = lax.axis_index("seq"), lax.axis_index("tp")
    core, chip, n_chips = lax.rem(seq, 2), lax.div(seq, 2), n_seq // 2
    n_chunks = T // C

    def rows_of(i):
        return pl.ds(pl.multiple_of(i * C, C), C)

    def to_tp(j):
        return lax.rem(tp + j, n_tp)

    def from_tp(j):
        return lax.rem(tp + n_tp - j, n_tp)

    barrier = pltpu.get_barrier_semaphore()

    loads = [
        pltpu.make_async_copy(w_hbm.at[1], wk, load_sem.at[0]),
        pltpu.make_async_copy(w_hbm.at[0], wq.at[tp], load_sem.at[1]),
        pltpu.make_async_copy(w_hbm.at[2], wv, load_sem.at[2]),
        pltpu.make_async_copy(wo_hbm, wo.at[tp], load_sem.at[3]),
    ]

    def x_load(i):
        return pltpu.make_async_copy(x_hbm.at[rows_of(i)], x.at[rows_of(i)], x_sem.at[i])

    loads[0].start()
    loads[1].start()
    for i in range(n_chunks):
        x_load(i).start()
    loads[2].start()
    loads[3].start()

    def peer(j):
        return {"seq": 2 * lax.rem(chip + j, n_chips) + core}

    mate = {"seq": seq + 1 - 2 * core}

    def any_peer(j):
        return {"seq": lax.rem(seq + j, n_seq)}

    @pl.loop(1, n_seq)
    def _(j):
        pl.semaphore_signal(barrier, inc=1, device_id=any_peer(j), device_id_type=MESH)

    for j in range(1, n_tp):
        pl.semaphore_signal(
            barrier, inc=1, device_id={"tp": to_tp(j)}, device_id_type=MESH
        )

    class Gather:
        def __init__(self, source, ref, sems):
            half = ref.shape[1] // 2
            self.source, self.ref, self.sems = source, ref, sems
            self.mine = pl.ds(pl.multiple_of(core * half, half), half)
            self.other = pl.ds(pl.multiple_of((1 - core) * half, half), half)

        def over(self, j, slot):
            return pltpu.make_async_remote_copy(
                src_ref=self.source(j, self.mine), dst_ref=self.ref.at[slot, self.mine],
                send_sem=self.sems.at[0, j], recv_sem=self.sems.at[1, j],
                device_id={"tp": to_tp(j)}, device_id_type=MESH,
            )

        def across(self, j, part):
            t = from_tp(j)
            return pltpu.make_async_remote_copy(
                src_ref=self.ref.at[t, part], dst_ref=self.ref.at[t, part],
                send_sem=self.sems.at[2, j], recv_sem=self.sems.at[3, j],
                device_id=mate, device_id_type=MESH,
            )

        def send(self):
            for j in ORDER:
                self.over(j, tp).start()

        def swap(self, j):
            self.over(j, from_tp(j)).wait_recv()
            self.across(j, self.mine).start()

        def ready(self, j):
            self.across(j, self.other).wait_recv()

        def drain(self):
            for j in ORDER:
                self.over(j, tp).wait_send()
                self.across(j, self.mine).wait_send()

    def columns_of(t):
        return pl.ds(pl.multiple_of(t * W, W), W)

    def share_of(t):
        return pl.ds(pl.multiple_of(t * SHARE, SHARE), SHARE)

    wq_all = Gather(lambda j, part: w_hbm.at[0, part], wq, wq_sems)
    wo_all = Gather(lambda j, part: wo_hbm.at[part], wo, wo_sems)
    km_all = Gather(lambda j, part: kmt.at[tp, part], kmt, km_sems)
    mt_all = Gather(lambda j, part: midt.at[tp, part], midt, mt_sems)

    def own_rows(i):
        x_load(i).wait()
        rows = rows_of(i)
        xc = x[rows, :]
        kp = dot(xc, wk[...])
        qp = dot(xc, wq[tp]) * LOG_SCALE
        k[rows, :] = kp.astype(bf16)
        q[tp, rows, :] = qp.astype(bf16)
        for s in range(C // SEG):
            at = i * (C // SEG) + s
            part = slice(s * SEG, (s + 1) * SEG)
            means[pl.ds(at, 1), :] = jnp.sum(qp[part], axis=0, keepdims=True) * (1.0 / SEG)
            means[pl.ds(8 + at, 1), :] = jnp.sum(kp[part], axis=0, keepdims=True) * (1.0 / SEG)

    def to_chips(src, dst, sems, j):
        return pltpu.make_async_remote_copy(
            src_ref=src, dst_ref=dst, send_sem=sems.at[0, j], recv_sem=sems.at[1, j],
            device_id=peer(j), device_id_type=MESH,
        )

    def to_mate(src, dst):
        return pltpu.make_async_remote_copy(
            src_ref=src, dst_ref=dst, send_sem=mate_sems.at[0], recv_sem=mate_sems.at[1],
            device_id=mate, device_id_type=MESH,
        )

    def chip_before(j):
        return lax.rem(chip + n_chips - j, n_chips)

    class Spread:
        def __init__(self, ref, sems):
            self.ref, self.sems = ref, sems

        def copy(self, j, place):
            return pltpu.make_async_remote_copy(
                src_ref=self.ref.at[seq], dst_ref=self.ref.at[place],
                send_sem=self.sems.at[0, j], recv_sem=self.sems.at[1, j],
                device_id=any_peer(j), device_id_type=MESH,
            )

        def send(self):
            @pl.loop(1, n_seq)
            def _(j):
                self.copy(j, seq).start()

        def ready(self):
            @pl.loop(1, n_seq)
            def _(j):
                self.copy(j, lax.rem(seq + n_seq - j, n_seq)).wait_recv()

        def drain(self):
            @pl.loop(1, n_seq)
            def _(j):
                self.copy(j, seq).wait_send()

    mk_all = Spread(mk_r, mk_sems)
    mid_all = Spread(mid_r, mid_sems)

    loads[0].wait()
    loads[1].wait()
    pl.loop(0, n_chunks)(own_rows)
    mk_r[seq] = means[...].astype(bf16)
    pl.semaphore_wait(barrier, n_seq - 1 + n_tp - 1)
    mk_all.send()
    wq_all.send()

    loads[2].wait()
    ones = jnp.ones((C, 128), bf16)

    def own_values(i):
        rows = rows_of(i)
        vp = dot(x[rows, :], wv[...]).astype(bf16)
        for p in range(2):
            v[p, rows, 0:128] = pair_columns(vp, p)
            v[p, rows, 128:256] = ones

    pl.loop(0, n_chunks)(own_values)
    mk_all.ready()
    marks = mk_r[...].astype(f32)
    q_marks = marks[:, 0:8, :].reshape(MARKS, W)
    k_marks = marks[:, 8:16, :].reshape(MARKS, W)
    kmt[tp] = k_marks.astype(bf16)
    km_all.send()
    wo_all.send()
    for h in range(4):
        qm[h] = one_head(pair_columns(q_marks, h // 2), h).astype(bf16)
        km[tp * 4 + h] = one_head(pair_columns(k_marks, h // 2), h).astype(bf16)

    sub = lax.broadcasted_iota(jnp.int32, (8, W), 0)
    for p in range(2):
        parts, levels = [], []
        for i in range(2):
            s = dot_nt(qm[2 * p + i], k[:, p * 128 : (p + 1) * 128])
            top = jnp.max(s, axis=1, keepdims=True)
            r = dot(jnp.exp2(s - top).astype(bf16), v[p])
            parts.append(r[:, :128] / r[:, 128:])
            levels.append((top + jnp.log2(r[:, 128:])).T[0:8, :])
        mean_values = jnp.where(low_lanes(MARKS), parts[0], parts[1]).T
        for i, level in enumerate(levels):
            lines = three_lines(level, sub)
            for b in range(8):
                part = mean_values[i * 64 + b * 8 : i * 64 + b * 8 + 8, :]
                at = (2 * p + i) * 8 + b
                lv_s[at // n_chips, at % n_chips] = jnp.concatenate([part, lines], 0).astype(bf16)

    lv_mate = to_mate(lv_s.at[1 - core], lv_t)
    lv_mate.start()
    wq_all.swap(ORDER[0])

    def lv_copy(j, place):
        return to_chips(lv_m.at[lax.rem(chip + j, n_chips)], lv_r.at[place], lv_sems, j)

    def values_and_level(blocks):
        blocks = blocks.astype(f32)
        return blocks[:, 0:8, :], blocks[:, 8:9, :] + blocks[:, 9:10, :] + blocks[:, 10:11, :]

    head = 2 * core + lax.div(chip, 8)
    terms = softmax_terms(dot_nt(qm[head], km[tp * 4 + head]))
    kernel_a = terms / jnp.sum(terms, axis=1, keepdims=True)
    col = jnp.max(jnp.sum(kernel_a, axis=0, keepdims=True), axis=1, keepdims=True)
    row = jnp.max(jnp.sum(kernel_a, axis=1, keepdims=True), axis=0, keepdims=True)
    a_ref[...] = kernel_a
    z_ref[...] = kernel_a.T / (col * row)
    wq_all.ready(ORDER[0])

    def unit(u):
        g, r = lax.div(u, PER_GROUP), lax.rem(u, PER_GROUP)
        t = lax.rem(tp + 1 + 2 * g + lax.div(g, 2), n_tp)
        later = lax.div(r + PER_GROUP - 1, PER_GROUP)
        start = (1 - later) * tp * SHARE + later * (C + (r - 1) * 256)
        rows = pl.ds(pl.multiple_of(start, 256), 256)
        q[t, rows, :] = (dot(x[rows, :], wq[t]) * LOG_SCALE).astype(bf16)

    def newton_turn(turn):
        eye = jnp.where(
            lax.broadcasted_iota(jnp.int32, (MARKS, MARKS), 0)
            == lax.broadcasted_iota(jnp.int32, (MARKS, MARKS), 1),
            1.0,
            0.0,
        )
        first = turn * UNITS
        z = z_ref[...]
        az = dot3(a_ref[...], z)
        unit(first)
        inner = dot3(az, 7.0 * eye - az)
        unit(first + 1)
        outer = dot3(az, 15.0 * eye - inner)
        unit(first + 2)
        z_ref[...] = 0.25 * dot3(z, 13.0 * eye - outer)
        unit(first + 3)

    newton_turn(0)
    lv_mate.wait_recv()
    (va, la), (vb, lb) = values_and_level(lv_s[core]), values_and_level(lv_t[...])
    top = jnp.maximum(la, lb)
    wa, wb = jnp.exp2(la - top), jnp.exp2(lb - top)
    level = jnp.broadcast_to(top + jnp.log2(wa + wb), va.shape)
    lines = three_lines(level, lax.broadcasted_iota(jnp.int32, va.shape, 1))
    lv_m[...] = jnp.concatenate([(va * wa + vb * wb) / (wa + wb), lines], 1).astype(bf16)

    @pl.loop(1, n_chips)
    def _(j):
        lv_copy(j, chip).start()

    lv_r[chip] = lv_m[chip]
    newton_turn(1)
    wq_all.swap(ORDER[1])
    newton_turn(2)
    wq_all.ready(ORDER[1])
    pl.loop(3, NEWTON)(newton_turn)
    wq_all.swap(ORDER[2])

    @pl.loop(1, n_chips)
    def _(j):
        lv_copy(j, chip_before(j)).wait_recv()

    values, level = values_and_level(lv_r[...])
    share = jnp.exp2(level - jnp.max(level, axis=0, keepdims=True))
    columns = jnp.sum(values * share, axis=0) / jnp.sum(share, axis=0)
    ch, cl = halves(columns)
    zh, zl = halves(z_ref[...])
    mid_r[seq] = dot_nt(jnp.concatenate([ch, cl, ch], 1), jnp.concatenate([zh, zh, zl], 1))
    mid_all.send()

    own_share = share_of(tp)

    def own_terms(rows):
        for h in range(4):
            p = h // 2
            logits = dot_nt(q[tp, rows, p * 128 : (p + 1) * 128], km[tp * 4 + h])
            e_own[rows, h * MARKS : (h + 1) * MARKS] = softmax_terms(logits).astype(bf16)

    def chunks(first, last, work):
        @pl.loop(first, last)
        def _(i):
            work(rows_of(i))

    chunks(1, n_chunks, own_terms)
    own_terms(own_share)
    wq_all.ready(ORDER[2])
    pl.loop(24, 36)(unit)
    for j in ORDER:
        km_all.swap(j)
    for j in ORDER:
        wo_all.swap(j)
    mid_all.ready()

    def place_middle(t):
        m = midt[t].astype(f32)
        low = low_lanes(MARKS)
        for p in range(2):
            both = pair_columns(m, p)
            for i in range(2):
                mask = low if i == 0 else ~low
                midb[t * 2 + p, i * MARKS : (i + 1) * MARKS, :] = jnp.concatenate(
                    [jnp.where(mask, both, 0.0), jnp.where(mask, 1.0, 0.0)], 1
                ).astype(bf16)

    pieces = [mid_r[2 * (n % n_chips) + n // n_chips] for n in range(n_seq)]
    midt[tp] = jnp.concatenate(pieces, 0).T.astype(bf16)
    mt_all.send()
    place_middle(tp)

    def normalised(r):
        return (r[:, :128] * (1.0 / r[:, 128:])).astype(bf16)

    def own_attended(rows):
        for p in range(2):
            r = dot(e_own[rows, p * 512 : (p + 1) * 512], midb[tp * 2 + p])
            q[tp, rows, p * 128 : (p + 1) * 128] = normalised(r)

    def attended_of(t, rows):
        parts = []
        for p in range(2):
            qc = q[t, rows, p * 128 : (p + 1) * 128]
            e = [softmax_terms(dot_nt(qc, km[t * 4 + 2 * p + b])).astype(bf16) for b in range(2)]
            parts.append(normalised(dot(jnp.concatenate(e, 1), midb[t * 2 + p])))
        return parts

    def place_group(j):
        t = from_tp(j)
        km_all.ready(j)
        others = kmt[t].astype(f32)
        for h in range(4):
            km[t * 4 + h] = one_head(pair_columns(others, h // 2), h).astype(bf16)
        mt_all.ready(j)
        place_middle(t)

    groups = [from_tp(j) for j in ORDER]

    def first_group(rows):
        q[groups[0], rows, :] = jnp.concatenate(attended_of(groups[0], rows), 1)

    chunks(1, n_chunks - 1, own_attended)
    pl.loop(36, 3 * PER_GROUP)(unit)
    mt_all.swap(ORDER[0])
    chunks(n_chunks - 1, n_chunks, own_attended)
    own_attended(own_share)
    place_group(ORDER[0])
    chunks(1, n_chunks - 1, first_group)
    for j in ORDER[1:]:
        mt_all.swap(j)
    chunks(n_chunks - 1, n_chunks, first_group)
    first_group(own_share)
    for j in ORDER[1:]:
        place_group(j)
    loads[3].wait()
    for j in ORDER:
        wo_all.ready(j)

    def out_copy(i):
        return pltpu.make_async_copy(outv.at[rows_of(i)], out_hbm.at[rows_of(i)], out_sem.at[i])

    def all_attended(rows):
        parts = [q[tp, rows, :], q[groups[0], rows, :]]
        for t in groups[1:]:
            parts += attended_of(t, rows)
        return jnp.concatenate(parts, 1)

    def out_columns(attended, t):
        columns = columns_of(t)
        weights = jnp.concatenate([wo[g, :, columns] for g in [tp] + groups], 0)
        return dot(attended, weights).astype(bf16)

    def share_copy(j, t):
        return pltpu.make_async_remote_copy(
            src_ref=sent.at[j], dst_ref=outv.at[share_of(t)],
            send_sem=share_sems.at[0, j], recv_sem=share_sems.at[1, j],
            device_id={"tp": to_tp(j)}, device_id_type=MESH,
        )

    attended = all_attended(own_share)
    for j in (2, 1, 3):
        sent[j] = out_columns(attended, to_tp(j))
        share_copy(j, tp).start()
    outv[own_share, :] = out_columns(attended, tp)

    @pl.loop(1, n_chunks)
    def _(i):
        rows = rows_of(i)
        outv[rows, :] = out_columns(all_attended(rows), tp)
        out_copy(i).start()

    for j in ORDER:
        share_copy(j, from_tp(j)).wait_recv()
    out_copy(0).start()
    for j in ORDER:
        share_copy(j, tp).wait_send()

    @pl.loop(1, n_chips)
    def _(j):
        lv_copy(j, chip).wait_send()

    lv_mate.wait_send()
    for part in (mk_all, mid_all, wq_all, wo_all, km_all, mt_all):
        part.drain()
    for i in range(n_chunks):
        out_copy(i).wait()


def on_device(n_seq, n_tp, tokens, w_qkv, w_out):
    vmem = pltpu.VMEM
    sems = pltpu.SemaphoreType.DMA
    n_chips = n_seq // 2
    scratch = [
        vmem((T, D), bf16),
        vmem((D, W), bf16),
        vmem((D, W), bf16),
        vmem((n_tp, D, W), bf16),
        vmem((n_tp, W, D), bf16),
        vmem((n_tp, T, W), bf16),
        vmem((T, W), bf16),
        vmem((2, T, 256), bf16),
        vmem((16, W), f32),
        vmem((n_seq, 16, W), bf16),
        vmem((4, MARKS, 128), bf16),
        vmem((4 * n_tp, MARKS, 128), bf16),
        vmem((n_tp, MARKS, W), bf16),
        vmem((2, n_chips, 16, MARKS), bf16),
        vmem((n_chips, 16, MARKS), bf16),
        vmem((n_chips, 16, MARKS), bf16),
        vmem((n_chips, 16, MARKS), bf16),
        vmem((MARKS, MARKS), f32),
        vmem((MARKS, MARKS), f32),
        vmem((n_seq, 8, MARKS), f32),
        vmem((n_tp, MARKS, W), bf16),
        vmem((2 * n_tp, 2 * MARKS, 256), bf16),
        vmem((T, 4 * MARKS), bf16),
        vmem((T, W), bf16),
        vmem((n_tp, SHARE, W), bf16),
        sems((4,)), sems((T // C,)), sems((T // C,)),
        sems((2, n_seq)), sems((2, n_chips)), sems((2, n_seq)),
        sems((2,)),
        *[sems((4, n_tp))] * 4,
        sems((2, n_tp)),
    ]
    hbm = pl.BlockSpec(memory_space=pl.ANY)
    return pl.pallas_call(
        functools.partial(kernel, n_seq, n_tp),
        out_shape=jax.ShapeDtypeStruct((T, W), bf16),
        in_specs=[hbm] * 3,
        out_specs=hbm,
        scratch_shapes=scratch,
        compiler_params=pltpu.CompilerParams(
            collective_id=0, has_side_effects=True, vmem_limit_bytes=60 * 2**20
        ),
    )(tokens, w_qkv, w_out)


def solution(mesh):
    return jax.shard_map(
        functools.partial(on_device, mesh.shape["seq"], mesh.shape["tp"]),
        mesh=mesh,
        in_specs=(P("seq", None), P(None, None, "tp"), P("tp", None)),
        out_specs=P("seq", "tp"),
        check_vma=False,
    )
```

```python
import functools
import math

import jax
import jax.numpy as jnp
from jax import lax
from jax.experimental import pallas as pl
from jax.experimental.pallas import tpu as pltpu
from jax.sharding import PartitionSpec as P

HEAD_DIM = 64
MARKS = 256
NEWTON = 6
UNITS = 4
D = 1024
W = 256
T = 4096
SEG = 512
C = 1024
SHARE = 256
PER_GROUP = 1 + (T - C) // 256
LOG_SCALE = HEAD_DIM**-0.5 * math.log2(math.e)
bf16, f32 = jnp.bfloat16, jnp.float32
NT = (((1,), (1,)), ((), ()))
MESH = pl.DeviceIdType.MESH
ORDER = (3, 1, 2)


RING = 4
OFFSETS = sorted(
    ((dz, dx, dc) for dz in range(RING) for dx in range(RING) for dc in range(2) if dz or dx or dc),
    key=lambda o: -(min(o[0], RING - o[0]) + min(o[1], RING - o[1])),
)


def dot(a, b):
    return jnp.dot(a, b, preferred_element_type=f32)


def dot_nt(a, b):
    return lax.dot_general(a, b, NT, preferred_element_type=f32)


def halves(a):
    hi = a.astype(bf16)
    return hi, (a - hi.astype(f32)).astype(bf16)


def dot3(a, b):
    ah, al = halves(a)
    bh, bl = halves(b)
    return dot(jnp.concatenate([ah, al, ah], 1), jnp.concatenate([bh, bh, bl], 0))


def low_lanes(rows):
    return lax.broadcasted_iota(jnp.int32, (rows, 128), 1) < 64


def one_head(block, head):
    low = low_lanes(block.shape[0])
    return jnp.where(low if head % 2 == 0 else ~low, block, 0.0)


def pair_columns(array, pair):
    return array[:, pair * 128 : (pair + 1) * 128]


def softmax_terms(logits):
    return jnp.exp2(logits - jnp.max(logits, axis=1, keepdims=True))


def three_lines(level, sub):
    first = level.astype(bf16).astype(f32)
    second = (level - first).astype(bf16).astype(f32)
    third = level - first - second
    return jnp.where(
        sub == 0, first, jnp.where(sub == 1, second, jnp.where(sub == 2, third, 0.0))
    )


def kernel(
    n_seq, n_tp,
    x_hbm, w_hbm, wo_hbm, out_hbm,
    x, wk, wv, wq, wo, q, k, v, means, mk_r, qm, km, kmt,
    lv_s, lv_t, lv_m, lv_r, a_ref, z_ref, mid_r, midt, midb, e_own, outv, sent,
    load_sem, x_sem, out_sem,
    mk_sems, lv_sems, mid_sems, mate_sems,
    wq_sems, wo_sems, km_sems, mt_sems, share_sems,
):
    seq, tp = lax.axis_index("seq"), lax.axis_index("tp")
    core, chip, n_chips = lax.rem(seq, 2), lax.div(seq, 2), n_seq // 2
    n_chunks = T // C

    def rows_of(i):
        return pl.ds(pl.multiple_of(i * C, C), C)

    def to_tp(j):
        return lax.rem(tp + j, n_tp)

    def from_tp(j):
        return lax.rem(tp + n_tp - j, n_tp)

    barrier = pltpu.get_barrier_semaphore()

    loads = [
        pltpu.make_async_copy(w_hbm.at[1], wk, load_sem.at[0]),
        pltpu.make_async_copy(w_hbm.at[0], wq.at[tp], load_sem.at[1]),
        pltpu.make_async_copy(w_hbm.at[2], wv, load_sem.at[2]),
        pltpu.make_async_copy(wo_hbm, wo.at[tp], load_sem.at[3]),
    ]

    def x_load(i):
        return pltpu.make_async_copy(x_hbm.at[rows_of(i)], x.at[rows_of(i)], x_sem.at[i])

    loads[0].start()
    loads[1].start()
    for i in range(n_chunks):
        x_load(i).start()
    loads[2].start()
    loads[3].start()

    def peer(j):
        return {"seq": 2 * lax.rem(chip + j, n_chips) + core}

    mate = {"seq": seq + 1 - 2 * core}

    zs = [lax.rem(lax.div(chip, RING) + d, RING) for d in range(RING)]
    xs = [lax.rem(lax.rem(chip, RING) + d, RING) for d in range(RING)]
    cores = [core, 1 - core]

    def ahead(offset):
        dz, dx, dc = offset
        return (zs[dz] * RING + xs[dx]) * 2 + cores[dc]

    def behind(offset):
        dz, dx, dc = offset
        return ahead(((RING - dz) % RING, (RING - dx) % RING, dc))

    for offset in OFFSETS:
        pl.semaphore_signal(
            barrier, inc=1, device_id={"seq": ahead(offset)}, device_id_type=MESH
        )
    for j in range(1, n_tp):
        pl.semaphore_signal(
            barrier, inc=1, device_id={"tp": to_tp(j)}, device_id_type=MESH
        )

    class Gather:
        def __init__(self, source, ref, sems):
            half = ref.shape[1] // 2
            self.source, self.ref, self.sems = source, ref, sems
            self.mine = pl.ds(pl.multiple_of(core * half, half), half)
            self.other = pl.ds(pl.multiple_of((1 - core) * half, half), half)

        def over(self, j, slot):
            return pltpu.make_async_remote_copy(
                src_ref=self.source(j, self.mine), dst_ref=self.ref.at[slot, self.mine],
                send_sem=self.sems.at[0, j], recv_sem=self.sems.at[1, j],
                device_id={"tp": to_tp(j)}, device_id_type=MESH,
            )

        def across(self, j, part):
            t = from_tp(j)
            return pltpu.make_async_remote_copy(
                src_ref=self.ref.at[t, part], dst_ref=self.ref.at[t, part],
                send_sem=self.sems.at[2, j], recv_sem=self.sems.at[3, j],
                device_id=mate, device_id_type=MESH,
            )

        def send(self):
            for j in ORDER:
                self.over(j, tp).start()

        def swap(self, j):
            self.over(j, from_tp(j)).wait_recv()
            self.across(j, self.mine).start()

        def ready(self, j):
            self.across(j, self.other).wait_recv()

        def drain(self):
            for j in ORDER:
                self.over(j, tp).wait_send()
                self.across(j, self.mine).wait_send()

    def columns_of(t):
        return pl.ds(pl.multiple_of(t * W, W), W)

    def share_of(t):
        return pl.ds(pl.multiple_of(t * SHARE, SHARE), SHARE)

    wq_all = Gather(lambda j, part: w_hbm.at[0, part], wq, wq_sems)
    wo_all = Gather(lambda j, part: wo_hbm.at[part], wo, wo_sems)
    km_all = Gather(lambda j, part: kmt.at[tp, part], kmt, km_sems)
    mt_all = Gather(lambda j, part: midt.at[tp, part], midt, mt_sems)

    def own_rows(i):
        x_load(i).wait()
        rows = rows_of(i)
        xc = x[rows, :]
        kp = dot(xc, wk[...])
        qp = dot(xc, wq[tp]) * LOG_SCALE
        k[rows, :] = kp.astype(bf16)
        q[tp, rows, :] = qp.astype(bf16)
        for s in range(C // SEG):
            at = i * (C // SEG) + s
            part = slice(s * SEG, (s + 1) * SEG)
            means[pl.ds(at, 1), :] = jnp.sum(qp[part], axis=0, keepdims=True) * (1.0 / SEG)
            means[pl.ds(8 + at, 1), :] = jnp.sum(kp[part], axis=0, keepdims=True) * (1.0 / SEG)

    def to_chips(src, dst, sems, j):
        return pltpu.make_async_remote_copy(
            src_ref=src, dst_ref=dst, send_sem=sems.at[0, j], recv_sem=sems.at[1, j],
            device_id=peer(j), device_id_type=MESH,
        )

    def to_mate(src, dst):
        return pltpu.make_async_remote_copy(
            src_ref=src, dst_ref=dst, send_sem=mate_sems.at[0], recv_sem=mate_sems.at[1],
            device_id=mate, device_id_type=MESH,
        )

    def chip_before(j):
        return lax.rem(chip + n_chips - j, n_chips)

    class Spread:
        def __init__(self, ref, sems):
            self.ref, self.sems = ref, sems

        def copy(self, offset, place):
            j = (offset[0] * RING + offset[1]) * 2 + offset[2]
            return pltpu.make_async_remote_copy(
                src_ref=self.ref.at[seq], dst_ref=self.ref.at[place],
                send_sem=self.sems.at[0, j], recv_sem=self.sems.at[1, j],
                device_id={"seq": ahead(offset)}, device_id_type=MESH,
            )

        def send(self):
            for offset in OFFSETS:
                self.copy(offset, seq).start()

        def ready(self):
            for offset in OFFSETS:
                self.copy(offset, behind(offset)).wait_recv()

        def drain(self):
            for offset in OFFSETS:
                self.copy(offset, seq).wait_send()

    mk_all = Spread(mk_r, mk_sems)
    mid_all = Spread(mid_r, mid_sems)

    loads[0].wait()
    loads[1].wait()
    pl.loop(0, n_chunks)(own_rows)
    mk_r[seq] = means[...].astype(bf16)
    pl.semaphore_wait(barrier, n_seq - 1 + n_tp - 1)
    mk_all.send()
    wq_all.send()

    loads[2].wait()
    ones = jnp.ones((C, 128), bf16)

    def own_values(i):
        rows = rows_of(i)
        vp = dot(x[rows, :], wv[...]).astype(bf16)
        for p in range(2):
            v[p, rows, 0:128] = pair_columns(vp, p)
            v[p, rows, 128:256] = ones

    pl.loop(0, n_chunks)(own_values)
    mk_all.ready()
    marks = mk_r[...].astype(f32)
    q_marks = marks[:, 0:8, :].reshape(MARKS, W)
    k_marks = marks[:, 8:16, :].reshape(MARKS, W)
    kmt[tp] = k_marks.astype(bf16)
    km_all.send()
    wo_all.send()
    for h in range(4):
        qm[h] = one_head(pair_columns(q_marks, h // 2), h).astype(bf16)
        km[tp * 4 + h] = one_head(pair_columns(k_marks, h // 2), h).astype(bf16)

    sub = lax.broadcasted_iota(jnp.int32, (8, W), 0)
    for p in range(2):
        parts, levels = [], []
        for i in range(2):
            s = dot_nt(qm[2 * p + i], k[:, p * 128 : (p + 1) * 128])
            top = jnp.max(s, axis=1, keepdims=True)
            r = dot(jnp.exp2(s - top).astype(bf16), v[p])
            parts.append(r[:, :128] / r[:, 128:])
            levels.append((top + jnp.log2(r[:, 128:])).T[0:8, :])
        mean_values = jnp.where(low_lanes(MARKS), parts[0], parts[1]).T
        for i, level in enumerate(levels):
            lines = three_lines(level, sub)
            for b in range(8):
                part = mean_values[i * 64 + b * 8 : i * 64 + b * 8 + 8, :]
                at = (2 * p + i) * 8 + b
                lv_s[at // n_chips, at % n_chips] = jnp.concatenate([part, lines], 0).astype(bf16)

    lv_mate = to_mate(lv_s.at[1 - core], lv_t)
    lv_mate.start()
    wq_all.swap(ORDER[0])

    def lv_copy(j, place):
        return to_chips(lv_m.at[lax.rem(chip + j, n_chips)], lv_r.at[place], lv_sems, j)

    def values_and_level(blocks):
        blocks = blocks.astype(f32)
        return blocks[:, 0:8, :], blocks[:, 8:9, :] + blocks[:, 9:10, :] + blocks[:, 10:11, :]

    head = 2 * core + lax.div(chip, 8)
    terms = softmax_terms(dot_nt(qm[head], km[tp * 4 + head]))
    kernel_a = terms / jnp.sum(terms, axis=1, keepdims=True)
    col = jnp.max(jnp.sum(kernel_a, axis=0, keepdims=True), axis=1, keepdims=True)
    row = jnp.max(jnp.sum(kernel_a, axis=1, keepdims=True), axis=0, keepdims=True)
    a_ref[...] = kernel_a
    z_ref[...] = kernel_a.T / (col * row)
    wq_all.ready(ORDER[0])

    def unit(u):
        g, r = lax.div(u, PER_GROUP), lax.rem(u, PER_GROUP)
        t = lax.rem(tp + 1 + 2 * g + lax.div(g, 2), n_tp)
        later = lax.div(r + PER_GROUP - 1, PER_GROUP)
        start = (1 - later) * tp * SHARE + later * (C + (r - 1) * 256)
        rows = pl.ds(pl.multiple_of(start, 256), 256)
        q[t, rows, :] = (dot(x[rows, :], wq[t]) * LOG_SCALE).astype(bf16)

    def newton_turn(turn):
        eye = jnp.where(
            lax.broadcasted_iota(jnp.int32, (MARKS, MARKS), 0)
            == lax.broadcasted_iota(jnp.int32, (MARKS, MARKS), 1),
            1.0,
            0.0,
        )
        first = turn * UNITS
        z = z_ref[...]
        az = dot3(a_ref[...], z)
        unit(first)
        inner = dot3(az, 7.0 * eye - az)
        unit(first + 1)
        outer = dot3(az, 15.0 * eye - inner)
        unit(first + 2)
        z_ref[...] = 0.25 * dot3(z, 13.0 * eye - outer)
        unit(first + 3)

    newton_turn(0)
    lv_mate.wait_recv()
    (va, la), (vb, lb) = values_and_level(lv_s[core]), values_and_level(lv_t[...])
    top = jnp.maximum(la, lb)
    wa, wb = jnp.exp2(la - top), jnp.exp2(lb - top)
    level = jnp.broadcast_to(top + jnp.log2(wa + wb), va.shape)
    lines = three_lines(level, lax.broadcasted_iota(jnp.int32, va.shape, 1))
    lv_m[...] = jnp.concatenate([(va * wa + vb * wb) / (wa + wb), lines], 1).astype(bf16)

    @pl.loop(1, n_chips)
    def _(j):
        lv_copy(j, chip).start()

    lv_r[chip] = lv_m[chip]
    newton_turn(1)
    wq_all.swap(ORDER[1])
    newton_turn(2)
    wq_all.ready(ORDER[1])
    pl.loop(3, NEWTON)(newton_turn)
    wq_all.swap(ORDER[2])

    @pl.loop(1, n_chips)
    def _(j):
        lv_copy(j, chip_before(j)).wait_recv()

    values, level = values_and_level(lv_r[...])
    share = jnp.exp2(level - jnp.max(level, axis=0, keepdims=True))
    columns = jnp.sum(values * share, axis=0) / jnp.sum(share, axis=0)
    ch, cl = halves(columns)
    zh, zl = halves(z_ref[...])
    mid_r[seq] = dot_nt(jnp.concatenate([ch, cl, ch], 1), jnp.concatenate([zh, zh, zl], 1))
    mid_all.send()

    own_share = share_of(tp)

    def own_terms(rows):
        for h in range(4):
            p = h // 2
            logits = dot_nt(q[tp, rows, p * 128 : (p + 1) * 128], km[tp * 4 + h])
            e_own[rows, h * MARKS : (h + 1) * MARKS] = softmax_terms(logits).astype(bf16)

    def chunks(first, last, work):
        @pl.loop(first, last)
        def _(i):
            work(rows_of(i))

    chunks(1, n_chunks, own_terms)
    own_terms(own_share)
    wq_all.ready(ORDER[2])
    pl.loop(24, 36)(unit)
    for j in ORDER:
        km_all.swap(j)
    for j in ORDER:
        wo_all.swap(j)
    mid_all.ready()

    def place_middle(t):
        m = midt[t].astype(f32)
        low = low_lanes(MARKS)
        for p in range(2):
            both = pair_columns(m, p)
            for i in range(2):
                mask = low if i == 0 else ~low
                midb[t * 2 + p, i * MARKS : (i + 1) * MARKS, :] = jnp.concatenate(
                    [jnp.where(mask, both, 0.0), jnp.where(mask, 1.0, 0.0)], 1
                ).astype(bf16)

    pieces = [mid_r[2 * (n % n_chips) + n // n_chips] for n in range(n_seq)]
    midt[tp] = jnp.concatenate(pieces, 0).T.astype(bf16)
    mt_all.send()
    place_middle(tp)

    def normalised(r):
        return (r[:, :128] * (1.0 / r[:, 128:])).astype(bf16)

    def own_attended(rows):
        for p in range(2):
            r = dot(e_own[rows, p * 512 : (p + 1) * 512], midb[tp * 2 + p])
            q[tp, rows, p * 128 : (p + 1) * 128] = normalised(r)

    def attended_of(t, rows):
        parts = []
        for p in range(2):
            qc = q[t, rows, p * 128 : (p + 1) * 128]
            e = [softmax_terms(dot_nt(qc, km[t * 4 + 2 * p + b])).astype(bf16) for b in range(2)]
            parts.append(normalised(dot(jnp.concatenate(e, 1), midb[t * 2 + p])))
        return parts

    def place_group(j):
        t = from_tp(j)
        km_all.ready(j)
        others = kmt[t].astype(f32)
        for h in range(4):
            km[t * 4 + h] = one_head(pair_columns(others, h // 2), h).astype(bf16)
        mt_all.ready(j)
        place_middle(t)

    groups = [from_tp(j) for j in ORDER]

    def first_group(rows):
        q[groups[0], rows, :] = jnp.concatenate(attended_of(groups[0], rows), 1)

    chunks(1, n_chunks - 1, own_attended)
    pl.loop(36, 3 * PER_GROUP)(unit)
    mt_all.swap(ORDER[0])
    chunks(n_chunks - 1, n_chunks, own_attended)
    own_attended(own_share)
    place_group(ORDER[0])
    chunks(1, n_chunks - 1, first_group)
    for j in ORDER[1:]:
        mt_all.swap(j)
    chunks(n_chunks - 1, n_chunks, first_group)
    first_group(own_share)
    for j in ORDER[1:]:
        place_group(j)
    loads[3].wait()
    for j in ORDER:
        wo_all.ready(j)

    def out_copy(i):
        return pltpu.make_async_copy(outv.at[rows_of(i)], out_hbm.at[rows_of(i)], out_sem.at[i])

    def all_attended(rows):
        parts = [q[tp, rows, :], q[groups[0], rows, :]]
        for t in groups[1:]:
            parts += attended_of(t, rows)
        return jnp.concatenate(parts, 1)

    def out_columns(attended, t):
        columns = columns_of(t)
        weights = jnp.concatenate([wo[g, :, columns] for g in [tp] + groups], 0)
        return dot(attended, weights).astype(bf16)

    def share_copy(j, t):
        return pltpu.make_async_remote_copy(
            src_ref=sent.at[j], dst_ref=outv.at[share_of(t)],
            send_sem=share_sems.at[0, j], recv_sem=share_sems.at[1, j],
            device_id={"tp": to_tp(j)}, device_id_type=MESH,
        )

    attended = all_attended(own_share)
    for j in (2, 1, 3):
        sent[j] = out_columns(attended, to_tp(j))
        share_copy(j, tp).start()
    outv[own_share, :] = out_columns(attended, tp)

    @pl.loop(1, n_chunks)
    def _(i):
        rows = rows_of(i)
        outv[rows, :] = out_columns(all_attended(rows), tp)
        out_copy(i).start()

    for j in ORDER:
        share_copy(j, from_tp(j)).wait_recv()
    out_copy(0).start()
    for j in ORDER:
        share_copy(j, tp).wait_send()

    @pl.loop(1, n_chips)
    def _(j):
        lv_copy(j, chip).wait_send()

    lv_mate.wait_send()
    for part in (mk_all, mid_all, wq_all, wo_all, km_all, mt_all):
        part.drain()
    for i in range(n_chunks):
        out_copy(i).wait()


def on_device(n_seq, n_tp, tokens, w_qkv, w_out):
    vmem = pltpu.VMEM
    sems = pltpu.SemaphoreType.DMA
    n_chips = n_seq // 2
    scratch = [
        vmem((T, D), bf16),
        vmem((D, W), bf16),
        vmem((D, W), bf16),
        vmem((n_tp, D, W), bf16),
        vmem((n_tp, W, D), bf16),
        vmem((n_tp, T, W), bf16),
        vmem((T, W), bf16),
        vmem((2, T, 256), bf16),
        vmem((16, W), f32),
        vmem((n_seq, 16, W), bf16),
        vmem((4, MARKS, 128), bf16),
        vmem((4 * n_tp, MARKS, 128), bf16),
        vmem((n_tp, MARKS, W), bf16),
        vmem((2, n_chips, 16, MARKS), bf16),
        vmem((n_chips, 16, MARKS), bf16),
        vmem((n_chips, 16, MARKS), bf16),
        vmem((n_chips, 16, MARKS), bf16),
        vmem((MARKS, MARKS), f32),
        vmem((MARKS, MARKS), f32),
        vmem((n_seq, 8, MARKS), f32),
        vmem((n_tp, MARKS, W), bf16),
        vmem((2 * n_tp, 2 * MARKS, 256), bf16),
        vmem((T, 4 * MARKS), bf16),
        vmem((T, W), bf16),
        vmem((n_tp, SHARE, W), bf16),
        sems((4,)), sems((T // C,)), sems((T // C,)),
        sems((2, n_seq)), sems((2, n_chips)), sems((2, n_seq)),
        sems((2,)),
        *[sems((4, n_tp))] * 4,
        sems((2, n_tp)),
    ]
    hbm = pl.BlockSpec(memory_space=pl.ANY)
    return pl.pallas_call(
        functools.partial(kernel, n_seq, n_tp),
        out_shape=jax.ShapeDtypeStruct((T, W), bf16),
        in_specs=[hbm] * 3,
        out_specs=hbm,
        scratch_shapes=scratch,
        compiler_params=pltpu.CompilerParams(
            collective_id=0, has_side_effects=True, vmem_limit_bytes=60 * 2**20
        ),
    )(tokens, w_qkv, w_out)


def solution(mesh):
    return jax.shard_map(
        functools.partial(on_device, mesh.shape["seq"], mesh.shape["tp"]),
        mesh=mesh,
        in_specs=(P("seq", None), P(None, None, "tp"), P("tp", None)),
        out_specs=P("seq", "tp"),
        check_vma=False,
    )
```

```python
import functools
import math

import jax
import jax.numpy as jnp
from jax import lax
from jax.experimental import pallas as pl
from jax.experimental.pallas import tpu as pltpu
from jax.sharding import PartitionSpec as P

HEAD_DIM = 64
MARKS = 256
NEWTON = 6
UNITS = 4
D = 1024
W = 256
T = 4096
SEG = 512
C = 1024
SHARE = 256
PER_GROUP = 1 + (T - C) // 256
LOG_SCALE = HEAD_DIM**-0.5 * math.log2(math.e)
bf16, f32 = jnp.bfloat16, jnp.float32
NT = (((1,), (1,)), ((), ()))
MESH = pl.DeviceIdType.MESH
ORDER = (3, 1, 2)


def dot(a, b):
    return jnp.dot(a, b, preferred_element_type=f32)


def dot_nt(a, b):
    return lax.dot_general(a, b, NT, preferred_element_type=f32)


def halves(a):
    hi = a.astype(bf16)
    return hi, (a - hi.astype(f32)).astype(bf16)


def dot3(a, b):
    ah, al = halves(a)
    bh, bl = halves(b)
    return dot(jnp.concatenate([ah, al, ah], 1), jnp.concatenate([bh, bh, bl], 0))


def low_lanes(rows):
    return lax.broadcasted_iota(jnp.int32, (rows, 128), 1) < 64


def one_head(block, head):
    low = low_lanes(block.shape[0])
    return jnp.where(low if head % 2 == 0 else ~low, block, 0.0)


def pair_columns(array, pair):
    return array[:, pair * 128 : (pair + 1) * 128]


def softmax_terms(logits):
    return jnp.exp2(logits - jnp.max(logits, axis=1, keepdims=True))


def three_lines(level, sub):
    first = level.astype(bf16).astype(f32)
    second = (level - first).astype(bf16).astype(f32)
    third = level - first - second
    return jnp.where(
        sub == 0, first, jnp.where(sub == 1, second, jnp.where(sub == 2, third, 0.0))
    )


def kernel(
    n_seq, n_tp,
    x_hbm, w_hbm, wo_hbm, out_hbm,
    x, wk, wv, wq, wo, q, k, v, means, mk_r, qm, km, kmt,
    lv_s, lv_t, lv_m, lv_r, a_ref, z_ref, mid_r, midt, midb, e_own, outv, sent,
    load_sem, x_sem, out_sem,
    mk_sems, lv_sems, mid_sems, mate_sems,
    wq_sems, wo_sems, km_sems, mt_sems, share_sems,
):
    seq, tp = lax.axis_index("seq"), lax.axis_index("tp")
    core, chip, n_chips = lax.rem(seq, 2), lax.div(seq, 2), n_seq // 2
    n_chunks = T // C

    def rows_of(i):
        return pl.ds(pl.multiple_of(i * C, C), C)

    def to_tp(j):
        return lax.rem(tp + j, n_tp)

    def from_tp(j):
        return lax.rem(tp + n_tp - j, n_tp)

    barrier = pltpu.get_barrier_semaphore()

    loads = [
        pltpu.make_async_copy(w_hbm.at[1], wk, load_sem.at[0]),
        pltpu.make_async_copy(w_hbm.at[0], wq.at[tp], load_sem.at[1]),
        pltpu.make_async_copy(w_hbm.at[2], wv, load_sem.at[2]),
        pltpu.make_async_copy(wo_hbm, wo.at[tp], load_sem.at[3]),
    ]

    def x_load(i):
        return pltpu.make_async_copy(x_hbm.at[rows_of(i)], x.at[rows_of(i)], x_sem.at[i])

    loads[0].start()
    loads[1].start()
    for i in range(n_chunks):
        x_load(i).start()
    loads[2].start()
    loads[3].start()

    def peer(j):
        return {"seq": 2 * lax.rem(chip + j, n_chips) + core}

    mate = {"seq": seq + 1 - 2 * core}

    def any_peer(j):
        return {"seq": lax.rem(seq + j, n_seq)}

    @pl.loop(1, n_seq)
    def _(j):
        pl.semaphore_signal(barrier, inc=1, device_id=any_peer(j), device_id_type=MESH)

    for j in range(1, n_tp):
        pl.semaphore_signal(
            barrier, inc=1, device_id={"tp": to_tp(j)}, device_id_type=MESH
        )

    class Gather:
        def __init__(self, source, ref, sems):
            half = ref.shape[1] // 2
            self.source, self.ref, self.sems = source, ref, sems
            self.mine = pl.ds(pl.multiple_of(core * half, half), half)
            self.other = pl.ds(pl.multiple_of((1 - core) * half, half), half)

        def over(self, j, slot):
            return pltpu.make_async_remote_copy(
                src_ref=self.source(j, self.mine), dst_ref=self.ref.at[slot, self.mine],
                send_sem=self.sems.at[0, j], recv_sem=self.sems.at[1, j],
                device_id={"tp": to_tp(j)}, device_id_type=MESH,
            )

        def across(self, j, part):
            t = from_tp(j)
            return pltpu.make_async_remote_copy(
                src_ref=self.ref.at[t, part], dst_ref=self.ref.at[t, part],
                send_sem=self.sems.at[2, j], recv_sem=self.sems.at[3, j],
                device_id=mate, device_id_type=MESH,
            )

        def send(self):
            for j in ORDER:
                self.over(j, tp).start()

        def swap(self, j):
            self.over(j, from_tp(j)).wait_recv()
            self.across(j, self.mine).start()

        def ready(self, j):
            self.across(j, self.other).wait_recv()

        def drain(self):
            for j in ORDER:
                self.over(j, tp).wait_send()
                self.across(j, self.mine).wait_send()

    def columns_of(t):
        return pl.ds(pl.multiple_of(t * W, W), W)

    def share_of(t):
        return pl.ds(pl.multiple_of(t * SHARE, SHARE), SHARE)

    wq_all = Gather(lambda j, part: w_hbm.at[0, part], wq, wq_sems)
    wo_all = Gather(lambda j, part: wo_hbm.at[part], wo, wo_sems)
    km_all = Gather(lambda j, part: kmt.at[tp, part], kmt, km_sems)
    mt_all = Gather(lambda j, part: midt.at[tp, part], midt, mt_sems)

    def own_rows(i):
        x_load(i).wait()
        rows = rows_of(i)
        xc = x[rows, :]
        kp = dot(xc, wk[...])
        qp = dot(xc, wq[tp]) * LOG_SCALE
        k[rows, :] = kp.astype(bf16)
        q[tp, rows, :] = qp.astype(bf16)
        for s in range(C // SEG):
            at = i * (C // SEG) + s
            part = slice(s * SEG, (s + 1) * SEG)
            means[pl.ds(at, 1), :] = jnp.sum(qp[part], axis=0, keepdims=True) * (1.0 / SEG)
            means[pl.ds(8 + at, 1), :] = jnp.sum(kp[part], axis=0, keepdims=True) * (1.0 / SEG)

    def to_chips(src, dst, sems, j):
        return pltpu.make_async_remote_copy(
            src_ref=src, dst_ref=dst, send_sem=sems.at[0, j], recv_sem=sems.at[1, j],
            device_id=peer(j), device_id_type=MESH,
        )

    def to_mate(src, dst):
        return pltpu.make_async_remote_copy(
            src_ref=src, dst_ref=dst, send_sem=mate_sems.at[0], recv_sem=mate_sems.at[1],
            device_id=mate, device_id_type=MESH,
        )

    def chip_before(j):
        return lax.rem(chip + n_chips - j, n_chips)

    class Spread:
        def __init__(self, ref, sems):
            self.ref, self.sems = ref, sems

        def copy(self, j, place):
            return pltpu.make_async_remote_copy(
                src_ref=self.ref.at[seq], dst_ref=self.ref.at[place],
                send_sem=self.sems.at[0, j], recv_sem=self.sems.at[1, j],
                device_id=any_peer(j), device_id_type=MESH,
            )

        def send(self):
            @pl.loop(1, n_seq)
            def _(j):
                self.copy(j, seq).start()

        def ready(self):
            @pl.loop(1, n_seq)
            def _(j):
                self.copy(j, lax.rem(seq + n_seq - j, n_seq)).wait_recv()

        def drain(self):
            @pl.loop(1, n_seq)
            def _(j):
                self.copy(j, seq).wait_send()

    mk_all = Spread(mk_r, mk_sems)
    mid_all = Spread(mid_r, mid_sems)

    loads[0].wait()
    loads[1].wait()
    pl.loop(0, n_chunks)(own_rows)
    mk_r[seq] = means[...].astype(bf16)
    pl.semaphore_wait(barrier, n_seq - 1 + n_tp - 1)
    mk_all.send()
    wq_all.send()

    loads[2].wait()
    ones = jnp.ones((C, 128), bf16)

    def own_values(i):
        rows = rows_of(i)
        vp = dot(x[rows, :], wv[...]).astype(bf16)
        for p in range(2):
            v[p, rows, 0:128] = pair_columns(vp, p)
            v[p, rows, 128:256] = ones

    pl.loop(0, n_chunks)(own_values)
    mk_all.ready()
    marks = mk_r[...].astype(f32)
    q_marks = marks[:, 0:8, :].reshape(MARKS, W)
    k_marks = marks[:, 8:16, :].reshape(MARKS, W)
    kmt[tp] = k_marks.astype(bf16)
    km_all.send()
    wo_all.send()
    for h in range(4):
        qm[h] = one_head(pair_columns(q_marks, h // 2), h).astype(bf16)
        km[tp * 4 + h] = one_head(pair_columns(k_marks, h // 2), h).astype(bf16)

    sub = lax.broadcasted_iota(jnp.int32, (8, W), 0)
    for p in range(2):
        parts, levels = [], []
        for i in range(2):
            s = dot_nt(qm[2 * p + i], k[:, p * 128 : (p + 1) * 128])
            top = jnp.max(s, axis=1, keepdims=True)
            r = dot(jnp.exp2(s - top).astype(bf16), v[p])
            parts.append(r[:, :128] / r[:, 128:])
            levels.append((top + jnp.log2(r[:, 128:])).T[0:8, :])
        mean_values = jnp.where(low_lanes(MARKS), parts[0], parts[1]).T
        for i, level in enumerate(levels):
            lines = three_lines(level, sub)
            for b in range(8):
                part = mean_values[i * 64 + b * 8 : i * 64 + b * 8 + 8, :]
                at = (2 * p + i) * 8 + b
                lv_s[at // n_chips, at % n_chips] = jnp.concatenate([part, lines], 0).astype(bf16)

    lv_mate = to_mate(lv_s.at[1 - core], lv_t)
    lv_mate.start()
    wq_all.swap(ORDER[0])

    def lv_copy(j, place):
        return to_chips(lv_m.at[lax.rem(chip + j, n_chips)], lv_r.at[place], lv_sems, j)

    def values_and_level(blocks):
        blocks = blocks.astype(f32)
        return blocks[:, 0:8, :], blocks[:, 8:9, :] + blocks[:, 9:10, :] + blocks[:, 10:11, :]

    head = 2 * core + lax.div(chip, 8)
    terms = softmax_terms(dot_nt(qm[head], km[tp * 4 + head]))
    kernel_a = terms / jnp.sum(terms, axis=1, keepdims=True)
    col = jnp.max(jnp.sum(kernel_a, axis=0, keepdims=True), axis=1, keepdims=True)
    row = jnp.max(jnp.sum(kernel_a, axis=1, keepdims=True), axis=0, keepdims=True)
    a_ref[...] = kernel_a
    z_ref[...] = kernel_a.T / (col * row)
    wq_all.ready(ORDER[0])

    def unit(u):
        g, r = lax.div(u, PER_GROUP), lax.rem(u, PER_GROUP)
        t = lax.rem(tp + 1 + 2 * g + lax.div(g, 2), n_tp)
        later = lax.div(r + PER_GROUP - 1, PER_GROUP)
        start = (1 - later) * tp * SHARE + later * (C + (r - 1) * 256)
        rows = pl.ds(pl.multiple_of(start, 256), 256)
        q[t, rows, :] = (dot(x[rows, :], wq[t]) * LOG_SCALE).astype(bf16)

    def newton_turn(turn):
        eye = jnp.where(
            lax.broadcasted_iota(jnp.int32, (MARKS, MARKS), 0)
            == lax.broadcasted_iota(jnp.int32, (MARKS, MARKS), 1),
            1.0,
            0.0,
        )
        first = turn * UNITS
        z = z_ref[...]
        az = dot3(a_ref[...], z)
        unit(first)
        inner = dot3(az, 7.0 * eye - az)
        unit(first + 1)
        outer = dot3(az, 15.0 * eye - inner)
        unit(first + 2)
        z_ref[...] = 0.25 * dot3(z, 13.0 * eye - outer)
        unit(first + 3)

    newton_turn(0)
    lv_mate.wait_recv()
    (va, la), (vb, lb) = values_and_level(lv_s[core]), values_and_level(lv_t[...])
    top = jnp.maximum(la, lb)
    wa, wb = jnp.exp2(la - top), jnp.exp2(lb - top)
    level = jnp.broadcast_to(top + jnp.log2(wa + wb), va.shape)
    lines = three_lines(level, lax.broadcasted_iota(jnp.int32, va.shape, 1))
    lv_m[...] = jnp.concatenate([(va * wa + vb * wb) / (wa + wb), lines], 1).astype(bf16)

    @pl.loop(1, n_chips)
    def _(j):
        lv_copy(j, chip).start()

    lv_r[chip] = lv_m[chip]
    newton_turn(1)
    wq_all.swap(ORDER[1])
    newton_turn(2)
    wq_all.ready(ORDER[1])
    pl.loop(3, NEWTON)(newton_turn)
    wq_all.swap(ORDER[2])

    @pl.loop(1, n_chips)
    def _(j):
        lv_copy(j, chip_before(j)).wait_recv()

    values, level = values_and_level(lv_r[...])
    share = jnp.exp2(level - jnp.max(level, axis=0, keepdims=True))
    columns = jnp.sum(values * share, axis=0) / jnp.sum(share, axis=0)
    ch, cl = halves(columns)
    zh, zl = halves(z_ref[...])
    middle = dot_nt(jnp.concatenate([ch, cl, ch], 1), jnp.concatenate([zh, zh, zl], 1))
    mid_r[seq] = jnp.concatenate([middle[:, :128], middle[:, 128:]], 0).astype(bf16)
    mid_all.send()

    own_share = share_of(tp)

    def own_terms(rows):
        for h in range(4):
            p = h // 2
            logits = dot_nt(q[tp, rows, p * 128 : (p + 1) * 128], km[tp * 4 + h])
            e_own[rows, h * MARKS : (h + 1) * MARKS] = softmax_terms(logits).astype(bf16)

    def chunks(first, last, work):
        @pl.loop(first, last)
        def _(i):
            work(rows_of(i))

    chunks(1, n_chunks, own_terms)
    own_terms(own_share)
    wq_all.ready(ORDER[2])
    pl.loop(24, 36)(unit)
    for j in ORDER:
        km_all.swap(j)
    for j in ORDER:
        wo_all.swap(j)
    mid_all.ready()

    def place_middle(t):
        m = midt[t].astype(f32)
        low = low_lanes(MARKS)
        for p in range(2):
            both = pair_columns(m, p)
            for i in range(2):
                mask = low if i == 0 else ~low
                midb[t * 2 + p, i * MARKS : (i + 1) * MARKS, :] = jnp.concatenate(
                    [jnp.where(mask, both, 0.0), jnp.where(mask, 1.0, 0.0)], 1
                ).astype(bf16)

    pieces = [mid_r[2 * (n % n_chips) + n // n_chips].astype(f32) for n in range(n_seq)]
    lines = [jnp.concatenate([piece[0:8], piece[8:16]], 1) for piece in pieces]
    midt[tp] = jnp.concatenate(lines, 0).T.astype(bf16)
    mt_all.send()
    place_middle(tp)

    def normalised(r):
        return (r[:, :128] * (1.0 / r[:, 128:])).astype(bf16)

    def own_attended(rows):
        for p in range(2):
            r = dot(e_own[rows, p * 512 : (p + 1) * 512], midb[tp * 2 + p])
            q[tp, rows, p * 128 : (p + 1) * 128] = normalised(r)

    def attended_of(t, rows):
        parts = []
        for p in range(2):
            qc = q[t, rows, p * 128 : (p + 1) * 128]
            e = [softmax_terms(dot_nt(qc, km[t * 4 + 2 * p + b])).astype(bf16) for b in range(2)]
            parts.append(normalised(dot(jnp.concatenate(e, 1), midb[t * 2 + p])))
        return parts

    def place_group(j):
        t = from_tp(j)
        km_all.ready(j)
        others = kmt[t].astype(f32)
        for h in range(4):
            km[t * 4 + h] = one_head(pair_columns(others, h // 2), h).astype(bf16)
        mt_all.ready(j)
        place_middle(t)

    groups = [from_tp(j) for j in ORDER]

    def first_group(rows):
        q[groups[0], rows, :] = jnp.concatenate(attended_of(groups[0], rows), 1)

    chunks(1, n_chunks - 1, own_attended)
    pl.loop(36, 3 * PER_GROUP)(unit)
    mt_all.swap(ORDER[0])
    chunks(n_chunks - 1, n_chunks, own_attended)
    own_attended(own_share)
    place_group(ORDER[0])
    chunks(1, n_chunks - 1, first_group)
    for j in ORDER[1:]:
        mt_all.swap(j)
    chunks(n_chunks - 1, n_chunks, first_group)
    first_group(own_share)
    for j in ORDER[1:]:
        place_group(j)
    loads[3].wait()
    for j in ORDER:
        wo_all.ready(j)

    def out_copy(i):
        return pltpu.make_async_copy(outv.at[rows_of(i)], out_hbm.at[rows_of(i)], out_sem.at[i])

    def all_attended(rows):
        parts = [q[tp, rows, :], q[groups[0], rows, :]]
        for t in groups[1:]:
            parts += attended_of(t, rows)
        return jnp.concatenate(parts, 1)

    def out_columns(attended, t):
        columns = columns_of(t)
        weights = jnp.concatenate([wo[g, :, columns] for g in [tp] + groups], 0)
        return dot(attended, weights).astype(bf16)

    def share_copy(j, t):
        return pltpu.make_async_remote_copy(
            src_ref=sent.at[j], dst_ref=outv.at[share_of(t)],
            send_sem=share_sems.at[0, j], recv_sem=share_sems.at[1, j],
            device_id={"tp": to_tp(j)}, device_id_type=MESH,
        )

    attended = all_attended(own_share)
    for j in (2, 1, 3):
        sent[j] = out_columns(attended, to_tp(j))
        share_copy(j, tp).start()
    outv[own_share, :] = out_columns(attended, tp)

    @pl.loop(1, n_chunks)
    def _(i):
        rows = rows_of(i)
        outv[rows, :] = out_columns(all_attended(rows), tp)
        out_copy(i).start()

    for j in ORDER:
        share_copy(j, from_tp(j)).wait_recv()
    out_copy(0).start()
    for j in ORDER:
        share_copy(j, tp).wait_send()

    @pl.loop(1, n_chips)
    def _(j):
        lv_copy(j, chip).wait_send()

    lv_mate.wait_send()
    for part in (mk_all, mid_all, wq_all, wo_all, km_all, mt_all):
        part.drain()
    for i in range(n_chunks):
        out_copy(i).wait()


def on_device(n_seq, n_tp, tokens, w_qkv, w_out):
    vmem = pltpu.VMEM
    sems = pltpu.SemaphoreType.DMA
    n_chips = n_seq // 2
    scratch = [
        vmem((T, D), bf16),
        vmem((D, W), bf16),
        vmem((D, W), bf16),
        vmem((n_tp, D, W), bf16),
        vmem((n_tp, W, D), bf16),
        vmem((n_tp, T, W), bf16),
        vmem((T, W), bf16),
        vmem((2, T, 256), bf16),
        vmem((16, W), f32),
        vmem((n_seq, 16, W), bf16),
        vmem((4, MARKS, 128), bf16),
        vmem((4 * n_tp, MARKS, 128), bf16),
        vmem((n_tp, MARKS, W), bf16),
        vmem((2, n_chips, 16, MARKS), bf16),
        vmem((n_chips, 16, MARKS), bf16),
        vmem((n_chips, 16, MARKS), bf16),
        vmem((n_chips, 16, MARKS), bf16),
        vmem((MARKS, MARKS), f32),
        vmem((MARKS, MARKS), f32),
        vmem((n_seq, 16, MARKS // 2), bf16),
        vmem((n_tp, MARKS, W), bf16),
        vmem((2 * n_tp, 2 * MARKS, 256), bf16),
        vmem((T, 4 * MARKS), bf16),
        vmem((T, W), bf16),
        vmem((n_tp, SHARE, W), bf16),
        sems((4,)), sems((T // C,)), sems((T // C,)),
        sems((2, n_seq)), sems((2, n_chips)), sems((2, n_seq)),
        sems((2,)),
        *[sems((4, n_tp))] * 4,
        sems((2, n_tp)),
    ]
    hbm = pl.BlockSpec(memory_space=pl.ANY)
    return pl.pallas_call(
        functools.partial(kernel, n_seq, n_tp),
        out_shape=jax.ShapeDtypeStruct((T, W), bf16),
        in_specs=[hbm] * 3,
        out_specs=hbm,
        scratch_shapes=scratch,
        compiler_params=pltpu.CompilerParams(
            collective_id=0, has_side_effects=True, vmem_limit_bytes=60 * 2**20
        ),
    )(tokens, w_qkv, w_out)


def solution(mesh):
    return jax.shard_map(
        functools.partial(on_device, mesh.shape["seq"], mesh.shape["tp"]),
        mesh=mesh,
        in_specs=(P("seq", None), P(None, None, "tp"), P("tp", None)),
        out_specs=P("seq", "tp"),
        check_vma=False,
    )
```

```python
import functools
import math

import jax
import jax.numpy as jnp
from jax import lax
from jax.experimental import pallas as pl
from jax.experimental.pallas import tpu as pltpu
from jax.sharding import PartitionSpec as P

HEAD_DIM = 64
MARKS = 256
NEWTON = 6
UNITS = 4
D = 1024
W = 256
T = 4096
SEG = 512
C = 1024
SHARE = 256
PER_GROUP = 1 + (T - C) // 256
LOG_SCALE = HEAD_DIM**-0.5 * math.log2(math.e)
bf16, f32 = jnp.bfloat16, jnp.float32
NT = (((1,), (1,)), ((), ()))
MESH = pl.DeviceIdType.MESH
ORDER = (3, 1, 2)


def dot(a, b):
    return jnp.dot(a, b, preferred_element_type=f32)


def dot_nt(a, b):
    return lax.dot_general(a, b, NT, preferred_element_type=f32)


def halves(a):
    hi = a.astype(bf16)
    return hi, (a - hi.astype(f32)).astype(bf16)


def dot3(a, b):
    ah, al = halves(a)
    bh, bl = halves(b)
    return dot(jnp.concatenate([ah, al, ah], 1), jnp.concatenate([bh, bh, bl], 0))


def low_lanes(rows):
    return lax.broadcasted_iota(jnp.int32, (rows, 128), 1) < 64


def one_head(block, head):
    low = low_lanes(block.shape[0])
    return jnp.where(low if head % 2 == 0 else ~low, block, 0.0)


def pair_columns(array, pair):
    return array[:, pair * 128 : (pair + 1) * 128]


def softmax_terms(logits):
    return jnp.exp2(logits - jnp.max(logits, axis=1, keepdims=True))


def three_lines(level, sub):
    first = level.astype(bf16).astype(f32)
    second = (level - first).astype(bf16).astype(f32)
    third = level - first - second
    return jnp.where(
        sub == 0, first, jnp.where(sub == 1, second, jnp.where(sub == 2, third, 0.0))
    )


def kernel(
    n_seq, n_tp,
    x_hbm, w_hbm, wo_hbm, out_hbm,
    x, wk, wv, wq, wo, q, k, v, means, mk_r, qm, km, kmt,
    lv_s, lv_t, lv_m, lv_r, a_ref, z_ref, mid_r, midt, midb, e_own, outv, sent,
    load_sem, x_sem, out_sem,
    mk_sems, lv_sems, mid_sems, mate_sems,
    wq_sems, wo_sems, km_sems, mt_sems, share_sems,
):
    seq, tp = lax.axis_index("seq"), lax.axis_index("tp")
    core, chip, n_chips = lax.rem(seq, 2), lax.div(seq, 2), n_seq // 2
    n_chunks = T // C

    def rows_of(i):
        return pl.ds(pl.multiple_of(i * C, C), C)

    def to_tp(j):
        return lax.rem(tp + j, n_tp)

    def from_tp(j):
        return lax.rem(tp + n_tp - j, n_tp)

    barrier = pltpu.get_barrier_semaphore()

    loads = [
        pltpu.make_async_copy(w_hbm.at[1], wk, load_sem.at[0]),
        pltpu.make_async_copy(w_hbm.at[0], wq.at[tp], load_sem.at[1]),
        pltpu.make_async_copy(w_hbm.at[2], wv, load_sem.at[2]),
        pltpu.make_async_copy(wo_hbm, wo.at[tp], load_sem.at[3]),
    ]

    def x_load(i):
        return pltpu.make_async_copy(x_hbm.at[rows_of(i)], x.at[rows_of(i)], x_sem.at[i])

    loads[0].start()
    loads[1].start()
    for i in range(n_chunks):
        x_load(i).start()
    loads[2].start()
    loads[3].start()

    def peer(j):
        return {"seq": 2 * lax.rem(chip + j, n_chips) + core}

    mate = {"seq": seq + 1 - 2 * core}

    def any_peer(j):
        return {"seq": lax.rem(seq + j, n_seq)}

    @pl.loop(1, n_seq)
    def _(j):
        pl.semaphore_signal(barrier, inc=1, device_id=any_peer(j), device_id_type=MESH)

    for j in range(1, n_tp):
        pl.semaphore_signal(
            barrier, inc=1, device_id={"tp": to_tp(j)}, device_id_type=MESH
        )

    class Gather:
        def __init__(self, source, ref, sems):
            half = ref.shape[1] // 2
            self.source, self.ref, self.sems = source, ref, sems
            self.mine = pl.ds(pl.multiple_of(core * half, half), half)
            self.other = pl.ds(pl.multiple_of((1 - core) * half, half), half)

        def over(self, j, slot):
            return pltpu.make_async_remote_copy(
                src_ref=self.source(j, self.mine), dst_ref=self.ref.at[slot, self.mine],
                send_sem=self.sems.at[0, j], recv_sem=self.sems.at[1, j],
                device_id={"tp": to_tp(j)}, device_id_type=MESH,
            )

        def across(self, j, part):
            t = from_tp(j)
            return pltpu.make_async_remote_copy(
                src_ref=self.ref.at[t, part], dst_ref=self.ref.at[t, part],
                send_sem=self.sems.at[2, j], recv_sem=self.sems.at[3, j],
                device_id=mate, device_id_type=MESH,
            )

        def send(self):
            for j in ORDER:
                self.over(j, tp).start()

        def swap(self, j):
            self.over(j, from_tp(j)).wait_recv()
            self.across(j, self.mine).start()

        def ready(self, j):
            self.across(j, self.other).wait_recv()

        def drain(self):
            for j in ORDER:
                self.over(j, tp).wait_send()
                self.across(j, self.mine).wait_send()

    def columns_of(t):
        return pl.ds(pl.multiple_of(t * W, W), W)

    def share_of(t):
        return pl.ds(pl.multiple_of(t * SHARE, SHARE), SHARE)

    wq_all = Gather(lambda j, part: w_hbm.at[0, part], wq, wq_sems)
    wo_all = Gather(lambda j, part: wo_hbm.at[part], wo, wo_sems)
    km_all = Gather(lambda j, part: kmt.at[tp, part], kmt, km_sems)
    mt_all = Gather(lambda j, part: midt.at[tp, part], midt, mt_sems)

    def own_rows(i):
        x_load(i).wait()
        rows = rows_of(i)
        xc = x[rows, :]
        kp = dot(xc, wk[...])
        qp = dot(xc, wq[tp]) * LOG_SCALE
        k[rows, :] = kp.astype(bf16)
        q[tp, rows, :] = qp.astype(bf16)
        for s in range(C // SEG):
            at = i * (C // SEG) + s
            part = slice(s * SEG, (s + 1) * SEG)
            means[pl.ds(at, 1), :] = jnp.sum(qp[part], axis=0, keepdims=True) * (1.0 / SEG)
            means[pl.ds(8 + at, 1), :] = jnp.sum(kp[part], axis=0, keepdims=True) * (1.0 / SEG)

    def to_chips(src, dst, sems, j):
        return pltpu.make_async_remote_copy(
            src_ref=src, dst_ref=dst, send_sem=sems.at[0, j], recv_sem=sems.at[1, j],
            device_id=peer(j), device_id_type=MESH,
        )

    def to_mate(src, dst):
        return pltpu.make_async_remote_copy(
            src_ref=src, dst_ref=dst, send_sem=mate_sems.at[0], recv_sem=mate_sems.at[1],
            device_id=mate, device_id_type=MESH,
        )

    def chip_before(j):
        return lax.rem(chip + n_chips - j, n_chips)

    class Spread:
        def __init__(self, ref, sems):
            self.ref, self.sems = ref, sems

        def copy(self, j, place):
            return pltpu.make_async_remote_copy(
                src_ref=self.ref.at[seq], dst_ref=self.ref.at[place],
                send_sem=self.sems.at[0, j], recv_sem=self.sems.at[1, j],
                device_id=any_peer(j), device_id_type=MESH,
            )

        def send(self):
            @pl.loop(1, n_seq)
            def _(j):
                self.copy(j, seq).start()

        def ready(self):
            @pl.loop(1, n_seq)
            def _(j):
                self.copy(j, lax.rem(seq + n_seq - j, n_seq)).wait_recv()

        def drain(self):
            @pl.loop(1, n_seq)
            def _(j):
                self.copy(j, seq).wait_send()

    mk_all = Spread(mk_r, mk_sems)
    mid_all = Spread(mid_r, mid_sems)

    loads[0].wait()
    loads[1].wait()
    pl.loop(0, n_chunks)(own_rows)
    mk_r[seq] = means[...].astype(bf16)
    pl.semaphore_wait(barrier, n_seq - 1 + n_tp - 1)
    mk_all.send()
    wq_all.send()

    loads[2].wait()
    ones = jnp.ones((C, 128), bf16)

    def own_values(i):
        rows = rows_of(i)
        vp = dot(x[rows, :], wv[...]).astype(bf16)
        for p in range(2):
            v[p, rows, 0:128] = pair_columns(vp, p)
            v[p, rows, 128:256] = ones

    pl.loop(0, n_chunks)(own_values)
    mk_all.ready()
    marks = mk_r[...].astype(f32)
    q_marks = marks[:, 0:8, :].reshape(MARKS, W)
    k_marks = marks[:, 8:16, :].reshape(MARKS, W)
    kmt[tp] = k_marks.astype(bf16)
    km_all.send()
    wo_all.send()
    for h in range(4):
        qm[h] = one_head(pair_columns(q_marks, h // 2), h).astype(bf16)
        km[tp * 4 + h] = one_head(pair_columns(k_marks, h // 2), h).astype(bf16)

    sub = lax.broadcasted_iota(jnp.int32, (8, W), 0)
    for p in range(2):
        parts, levels = [], []
        for i in range(2):
            s = dot_nt(qm[2 * p + i], k[:, p * 128 : (p + 1) * 128])
            top = jnp.max(s, axis=1, keepdims=True)
            r = dot(jnp.exp2(s - top).astype(bf16), v[p])
            parts.append(r[:, :128] / r[:, 128:])
            levels.append((top + jnp.log2(r[:, 128:])).T[0:8, :])
        mean_values = jnp.where(low_lanes(MARKS), parts[0], parts[1]).T
        for i, level in enumerate(levels):
            lines = three_lines(level, sub)
            for b in range(8):
                part = mean_values[i * 64 + b * 8 : i * 64 + b * 8 + 8, :]
                at = (2 * p + i) * 8 + b
                lv_s[at // n_chips, at % n_chips] = jnp.concatenate([part, lines], 0).astype(bf16)

    lv_mate = to_mate(lv_s.at[1 - core], lv_t)
    lv_mate.start()
    wq_all.swap(ORDER[0])

    def lv_copy(j, place):
        return to_chips(lv_m.at[lax.rem(chip + j, n_chips)], lv_r.at[place], lv_sems, j)

    def values_and_level(blocks):
        blocks = blocks.astype(f32)
        return blocks[:, 0:8, :], blocks[:, 8:9, :] + blocks[:, 9:10, :] + blocks[:, 10:11, :]

    head = 2 * core + lax.div(chip, 8)
    terms = softmax_terms(dot_nt(qm[head], km[tp * 4 + head]))
    kernel_a = terms / jnp.sum(terms, axis=1, keepdims=True)
    col = jnp.max(jnp.sum(kernel_a, axis=0, keepdims=True), axis=1, keepdims=True)
    row = jnp.max(jnp.sum(kernel_a, axis=1, keepdims=True), axis=0, keepdims=True)
    a_ref[...] = kernel_a
    z_ref[...] = kernel_a.T / (col * row)
    wq_all.ready(ORDER[0])

    def unit(u):
        g, r = lax.div(u, PER_GROUP), lax.rem(u, PER_GROUP)
        t = lax.rem(tp + 1 + 2 * g + lax.div(g, 2), n_tp)
        later = lax.div(r + PER_GROUP - 1, PER_GROUP)
        start = (1 - later) * tp * SHARE + later * (C + (r - 1) * 256)
        rows = pl.ds(pl.multiple_of(start, 256), 256)
        q[t, rows, :] = (dot(x[rows, :], wq[t]) * LOG_SCALE).astype(bf16)

    def newton_turn(turn):
        eye = jnp.where(
            lax.broadcasted_iota(jnp.int32, (MARKS, MARKS), 0)
            == lax.broadcasted_iota(jnp.int32, (MARKS, MARKS), 1),
            1.0,
            0.0,
        )
        first = turn * UNITS
        z = z_ref[...]
        az = dot3(a_ref[...], z)
        unit(first)
        inner = dot3(az, 7.0 * eye - az)
        unit(first + 1)
        outer = dot3(az, 15.0 * eye - inner)
        unit(first + 2)
        z_ref[...] = 0.25 * dot3(z, 13.0 * eye - outer)
        unit(first + 3)

    newton_turn(0)
    lv_mate.wait_recv()
    (va, la), (vb, lb) = values_and_level(lv_s[core]), values_and_level(lv_t[...])
    top = jnp.maximum(la, lb)
    wa, wb = jnp.exp2(la - top), jnp.exp2(lb - top)
    level = jnp.broadcast_to(top + jnp.log2(wa + wb), va.shape)
    lines = three_lines(level, lax.broadcasted_iota(jnp.int32, va.shape, 1))
    lv_m[...] = jnp.concatenate([(va * wa + vb * wb) / (wa + wb), lines], 1).astype(bf16)

    @pl.loop(1, n_chips)
    def _(j):
        lv_copy(j, chip).start()

    lv_r[chip] = lv_m[chip]
    newton_turn(1)
    wq_all.swap(ORDER[1])
    newton_turn(2)
    wq_all.ready(ORDER[1])
    pl.loop(3, NEWTON)(newton_turn)
    wq_all.swap(ORDER[2])

    @pl.loop(1, n_chips)
    def _(j):
        lv_copy(j, chip_before(j)).wait_recv()

    values, level = values_and_level(lv_r[...])
    share = jnp.exp2(level - jnp.max(level, axis=0, keepdims=True))
    columns = jnp.sum(values * share, axis=0) / jnp.sum(share, axis=0)
    ch, cl = halves(columns)
    zh, zl = halves(z_ref[...])
    mid_r[seq] = dot_nt(jnp.concatenate([ch, cl, ch], 1), jnp.concatenate([zh, zh, zl], 1))
    mid_all.send()

    own_share = share_of(tp)

    def own_terms(rows):
        for h in range(4):
            p = h // 2
            logits = dot_nt(q[tp, rows, p * 128 : (p + 1) * 128], km[tp * 4 + h])
            e_own[rows, h * MARKS : (h + 1) * MARKS] = softmax_terms(logits).astype(bf16)

    def chunks(first, last, work):
        @pl.loop(first, last)
        def _(i):
            work(rows_of(i))

    chunks(1, n_chunks, own_terms)
    own_terms(own_share)
    wq_all.ready(ORDER[2])
    pl.loop(24, 36)(unit)
    for j in ORDER:
        km_all.swap(j)
    for j in ORDER:
        wo_all.swap(j)
    mid_all.ready()

    def place_middle(t):
        m = midt[t].astype(f32)
        low = low_lanes(MARKS)
        for p in range(2):
            both = pair_columns(m, p)
            for i in range(2):
                mask = low if i == 0 else ~low
                midb[t * 2 + p, i * MARKS : (i + 1) * MARKS, :] = jnp.concatenate(
                    [jnp.where(mask, both, 0.0), jnp.where(mask, 1.0, 0.0)], 1
                ).astype(bf16)

    pieces = [mid_r[2 * (n % n_chips) + n // n_chips] for n in range(n_seq)]
    midt[tp] = jnp.concatenate(pieces, 0).T.astype(bf16)
    mt_all.send()
    place_middle(tp)

    def normalised(r):
        return (r[:, :128] * (1.0 / r[:, 128:])).astype(bf16)

    def own_attended(rows):
        for p in range(2):
            r = dot(e_own[rows, p * 512 : (p + 1) * 512], midb[tp * 2 + p])
            q[tp, rows, p * 128 : (p + 1) * 128] = normalised(r)

    def attended_of(t, rows):
        parts = []
        for p in range(2):
            qc = q[t, rows, p * 128 : (p + 1) * 128]
            e = [softmax_terms(dot_nt(qc, km[t * 4 + 2 * p + b])).astype(bf16) for b in range(2)]
            parts.append(normalised(dot(jnp.concatenate(e, 1), midb[t * 2 + p])))
        return parts

    def place_group(j):
        t = from_tp(j)
        km_all.ready(j)
        others = kmt[t].astype(f32)
        for h in range(4):
            km[t * 4 + h] = one_head(pair_columns(others, h // 2), h).astype(bf16)
        mt_all.ready(j)
        place_middle(t)

    groups = [from_tp(j) for j in ORDER]

    def first_group(rows):
        q[groups[0], rows, :] = jnp.concatenate(attended_of(groups[0], rows), 1)

    chunks(1, n_chunks - 1, own_attended)
    pl.loop(36, 3 * PER_GROUP)(unit)
    mt_all.swap(ORDER[0])
    chunks(n_chunks - 1, n_chunks, own_attended)
    own_attended(own_share)
    place_group(ORDER[0])
    first_group(own_share)
    chunks(1, 2, first_group)
    for j in ORDER[1:]:
        mt_all.swap(j)
    chunks(2, n_chunks - 1, first_group)
    for j in ORDER[1:]:
        place_group(j)
    loads[3].wait()
    for j in ORDER:
        wo_all.ready(j)

    def out_copy(i):
        return pltpu.make_async_copy(outv.at[rows_of(i)], out_hbm.at[rows_of(i)], out_sem.at[i])

    def all_attended(rows):
        parts = [q[tp, rows, :], q[groups[0], rows, :]]
        for t in groups[1:]:
            parts += attended_of(t, rows)
        return jnp.concatenate(parts, 1)

    def out_columns(attended, t):
        columns = columns_of(t)
        weights = jnp.concatenate([wo[g, :, columns] for g in [tp] + groups], 0)
        return dot(attended, weights).astype(bf16)

    def share_copy(j, t):
        return pltpu.make_async_remote_copy(
            src_ref=sent.at[j], dst_ref=outv.at[share_of(t)],
            send_sem=share_sems.at[0, j], recv_sem=share_sems.at[1, j],
            device_id={"tp": to_tp(j)}, device_id_type=MESH,
        )

    attended = all_attended(own_share)
    for j in (2, 1, 3):
        sent[j] = out_columns(attended, to_tp(j))
        share_copy(j, tp).start()
    outv[own_share, :] = out_columns(attended, tp)
    chunks(n_chunks - 1, n_chunks, first_group)

    @pl.loop(1, n_chunks)
    def _(i):
        rows = rows_of(i)
        outv[rows, :] = out_columns(all_attended(rows), tp)
        out_copy(i).start()

    for j in ORDER:
        share_copy(j, from_tp(j)).wait_recv()
    out_copy(0).start()
    for j in ORDER:
        share_copy(j, tp).wait_send()

    @pl.loop(1, n_chips)
    def _(j):
        lv_copy(j, chip).wait_send()

    lv_mate.wait_send()
    for part in (mk_all, mid_all, wq_all, wo_all, km_all, mt_all):
        part.drain()
    for i in range(n_chunks):
        out_copy(i).wait()


def on_device(n_seq, n_tp, tokens, w_qkv, w_out):
    vmem = pltpu.VMEM
    sems = pltpu.SemaphoreType.DMA
    n_chips = n_seq // 2
    scratch = [
        vmem((T, D), bf16),
        vmem((D, W), bf16),
        vmem((D, W), bf16),
        vmem((n_tp, D, W), bf16),
        vmem((n_tp, W, D), bf16),
        vmem((n_tp, T, W), bf16),
        vmem((T, W), bf16),
        vmem((2, T, 256), bf16),
        vmem((16, W), f32),
        vmem((n_seq, 16, W), bf16),
        vmem((4, MARKS, 128), bf16),
        vmem((4 * n_tp, MARKS, 128), bf16),
        vmem((n_tp, MARKS, W), bf16),
        vmem((2, n_chips, 16, MARKS), bf16),
        vmem((n_chips, 16, MARKS), bf16),
        vmem((n_chips, 16, MARKS), bf16),
        vmem((n_chips, 16, MARKS), bf16),
        vmem((MARKS, MARKS), f32),
        vmem((MARKS, MARKS), f32),
        vmem((n_seq, 8, MARKS), f32),
        vmem((n_tp, MARKS, W), bf16),
        vmem((2 * n_tp, 2 * MARKS, 256), bf16),
        vmem((T, 4 * MARKS), bf16),
        vmem((T, W), bf16),
        vmem((n_tp, SHARE, W), bf16),
        sems((4,)), sems((T // C,)), sems((T // C,)),
        sems((2, n_seq)), sems((2, n_chips)), sems((2, n_seq)),
        sems((2,)),
        *[sems((4, n_tp))] * 4,
        sems((2, n_tp)),
    ]
    hbm = pl.BlockSpec(memory_space=pl.ANY)
    return pl.pallas_call(
        functools.partial(kernel, n_seq, n_tp),
        out_shape=jax.ShapeDtypeStruct((T, W), bf16),
        in_specs=[hbm] * 3,
        out_specs=hbm,
        scratch_shapes=scratch,
        compiler_params=pltpu.CompilerParams(
            collective_id=0, has_side_effects=True, vmem_limit_bytes=60 * 2**20
        ),
    )(tokens, w_qkv, w_out)


def solution(mesh):
    return jax.shard_map(
        functools.partial(on_device, mesh.shape["seq"], mesh.shape["tp"]),
        mesh=mesh,
        in_specs=(P("seq", None), P(None, None, "tp"), P("tp", None)),
        out_specs=P("seq", "tp"),
        check_vma=False,
    )
```
